32 devices in a mesh: section: 2 (over y), expert: 16 (over z, x, core).
Axes of the slice: x: 2, y: 2, z: 4, core: 2. Of those that a mesh axis runs over, the one named last changes fastest.
Arguments:
- fresh: bfloat16 [2048, 2048], P('expert'), may hold values from -6 to 6
- previous: bfloat16 [2, 2048, 2048], P('section', 'expert'), may hold values from -6 to 6
- norm_gain: float32 [2, 2048], P('section'), may hold values from 0.1 to 1.9
- routes: int32 [2, 2048, 8], P('section', 'expert'), may hold values from 0 to 15, all different within a row; in each aligned block of 128 rows (0 to 127, 128 to 255, ..., all dimensions but the last counted through in order) at most 68 rows name the same one
- gate_weights: float32 [2, 2048, 8], P('section', 'expert'), may hold values from 0.03 to 0.3
- w_gate_up: bfloat16 [2, 16, 2048, 1536], P('section', 'expert'), may hold values from -0.125 to 0.125
- w_down: bfloat16 [2, 16, 768, 2048], P('section', 'expert'), may hold values from -0.21875 to 0.21875
Outputs:
- section_output: bfloat16 [2, 2048, 2048], P('section', 'expert')
The draws below stay inside these ranges and needn't reach their ends.
Inputs may be any that keep to these rules, and one draw needn't show every extreme that they name: `routes`: within one section, among the 128 tokens of one device (aligned blocks of tokens) no expert is chosen by more than 68 tokens, and some expert is chosen by exactly 68 of them; the 8 experts of a token differ.
All inputs are finite; a program needn't handle non-finite values.
Results may differ from the reference program's by a relative error of at most 0.0033.
Values may be sent and summed in bfloat16 or wider, within the bound.
No kernel may reach another device: no remote copies, remote signals or barrier semaphores. Data moves between devices by JAX's collectives and lax.ppermute only.
A program may use at most 64 MiB of HBM per device.

```python
import math
import jax
import jax.numpy as jnp
import numpy as np
from jax import lax

D = 2048
F = 768
TOPK = 8
TOK_DEV = 128
SECTIONS = 2
EXPERTS = 16
TOKENS = 2048
CAP = 68
ROWS_MAX = 1088


def levels(stream_key, extent, pieces, smallest, top_value):
    level, own = 1.0, jax.random.fold_in(stream_key, 6)
    for dim, parts in pieces:
        steps = jnp.exp(jax.random.uniform(jax.random.fold_in(own, dim), (parts,), jnp.float32, smallest / len(pieces), top_value / len(pieces)))
        level = level * jnp.repeat(steps, extent[dim] // parts).reshape([-1 if axis == dim else 1 for axis in range(len(extent))])
    return level


def routed_block(own_key, own, number, rows, amount, top, limit, lean):
    sequence = jax.random.permutation(own_key, amount)
    heavy_load, usual = load_shares(amount, rows * top, limit, lean, True), load_shares(amount, rows * top, limit, lean, False)
    places = jnp.arange(amount)

    def named(lengths, rotation):
        used = int((lengths > 0).sum())
        fixed = max(1, used // 4)
        moved = fixed + (places - fixed + rotation * (used - fixed)) % max(1, amount - fixed)
        return jnp.zeros((amount,), jnp.int32).at[sequence[jnp.where(places < fixed, places, moved)]].set(jnp.asarray(lengths, jnp.int32))

    lengths = jnp.where(number % 4 == 0, named(heavy_load, number // 4), named(usual, number - number // 4 - 1))
    mixed = jax.random.permutation(jax.random.fold_in(own, 3), amount)
    source_of, taker = mixed[0:amount // 2 * 2:2], mixed[1:amount // 2 * 2:2]
    slack = jnp.minimum(lengths[source_of] - 1, limit - lengths[taker]) // 2
    slack = jnp.where((source_of == sequence[0]) | (taker == sequence[0]) | (lengths[taker] == 0), 0, jnp.maximum(slack, 0))
    moved = jax.random.randint(jax.random.fold_in(own, 4), (amount // 2,), 0, 1 << 20) % (slack + 1)
    lengths = lengths.at[source_of].add(-moved).at[taker].add(moved)
    labels = jnp.searchsorted(jnp.cumsum(lengths), jnp.arange(rows * top), side="right").astype(jnp.int32)
    table = labels.reshape(top, rows).T
    table = table[jax.random.permutation(jax.random.fold_in(own, 1), rows)]
    rotation = jax.random.randint(jax.random.fold_in(own, 2), (rows, 1), 0, top)
    return jnp.take_along_axis(table, (jnp.arange(top)[None, :] + rotation) % top, axis=1)


def load_shares(number_of, total, most, slope, full):
    portions = [(1 << 20) // math.isqrt(grade ** slope) + 1 for grade in range(1, number_of + 1)]
    largest = most if full else min(most, max(-(-total // number_of), total * portions[0] // sum(portions)))
    least = 1 if total - largest >= number_of - 1 else 0
    counts, surplus = [largest] + [least] * (number_of - 1), total - largest - least * (number_of - 1)
    while surplus > 0:
        candidates = [i for i in range(1, number_of) if counts[i] < largest] or [i for i in range(1, number_of) if counts[i] < most]
        mass, remaining = sum([portions[i] for i in candidates]), surplus
        for i in candidates:
            more = min(most - counts[i], max(1, remaining * portions[i] // mass), surplus)
            counts[i] = counts[i] + more
            surplus = surplus - more
    return np.array(counts)


def scatter_about(stream_key, dims, scale, limit, shards=(), kind=jnp.bfloat16):
    loudness = levels(stream_key, dims, shards, -0.22, 0.18) if shards else 1.0
    entries = jax.random.normal(stream_key, dims, jnp.float32) * scale * loudness
    return jnp.minimum(jnp.maximum(entries, -limit), limit).astype(kind)


def setup_inputs(seed: int = 0) -> dict:
    key_of = jax.random.split(jax.random.key(seed), 8)
    fresh = scatter_about(key_of[0], (TOKENS, D), 1.0, 6.0, ((0, 16),))
    previous = scatter_about(key_of[1], (SECTIONS, TOKENS, D), 1.0, 6.0, ((0, 2), (1, 16)))
    norm_gain = jnp.clip(1.0 + 0.18 * jax.random.normal(key_of[2], (SECTIONS, D), jnp.float32), 0.1, 1.9)
    routes_keys = jax.random.split(jax.random.fold_in(key_of[3], 1), SECTIONS * TOKENS // TOK_DEV)
    routes_turns = jax.random.permutation(jax.random.fold_in(key_of[3], 3), SECTIONS * TOKENS // TOK_DEV)
    routes = jax.vmap(lambda own, number: routed_block(jax.random.fold_in(key_of[3], 2), own, number, TOK_DEV, EXPERTS, TOPK, CAP, 2))(routes_keys, routes_turns).reshape((SECTIONS, TOKENS, TOPK))
    gate_weights = jnp.clip(jnp.exp(math.log(0.3) - 2.3025852 * jax.random.uniform(key_of[4], (SECTIONS, TOKENS, TOPK), jnp.float32) ** levels(key_of[4], (SECTIONS, TOKENS, TOPK), ((0, 2), (1, 16)), -0.2, 0.2)), 0.03, 0.3)
    w_gate_up = scatter_about(key_of[5], (SECTIONS, EXPERTS, D, 2 * F), D ** -0.5, 0.125, ((0, 2), (1, 16)))
    w_down = scatter_about(key_of[6], (SECTIONS, EXPERTS, F, D), F ** -0.5, 0.21875, ((0, 2), (1, 16)))
    return dict(fresh=fresh, previous=previous, norm_gain=norm_gain, routes=routes, gate_weights=gate_weights, w_gate_up=w_gate_up, w_down=w_down)


epsilon = 1e-06

def one_layer(arrival, gain, route_ids, gates, gate_up, down):
    wide_input = arrival.astype(jnp.float32)
    scale = lax.rsqrt(lax.optimization_barrier(jnp.mean(wide_input * wide_input, axis=-1, keepdims=True)) + epsilon)
    normed = (wide_input * scale * gain[None, :]).astype(jnp.bfloat16)
    flat_ids = route_ids.reshape(-1).astype(jnp.int32)
    total_rows = flat_ids.shape[0]
    padded = jnp.concatenate([normed, jnp.zeros((1, D), jnp.bfloat16)], axis=0)

    def run_expert(expert_num):
        row_index = jnp.nonzero(flat_ids == expert_num, size=ROWS_MAX, fill_value=total_rows)[0].astype(jnp.int32)
        rows = padded[row_index // TOPK]
        projected = jnp.dot(rows, gate_up[expert_num], preferred_element_type=jnp.float32)
        hidden = (jax.nn.silu(projected[:, :F]) * projected[:, F:]).astype(jnp.bfloat16)
        result = jnp.dot(hidden, down[expert_num], preferred_element_type=jnp.float32).astype(jnp.bfloat16)
        return (row_index, result)
    indices, results = lax.map(run_expert, jnp.arange(EXPERTS, dtype=jnp.int32))
    table = jnp.zeros((total_rows + 1, D), jnp.bfloat16).at[indices.reshape(-1)].set(results.reshape(-1, D))
    picked = table[:total_rows].reshape(TOKENS, TOPK, D).astype(jnp.float32)
    mixed = lax.optimization_barrier(jnp.sum(picked * gates[:, :, None], axis=1))
    return (wide_input + mixed).astype(jnp.bfloat16)

def reference(fresh, previous, norm_gain, routes, gate_weights, w_gate_up, w_down):
    layers_out = []
    for section_num in range(SECTIONS):
        arrival = fresh if section_num == 0 else previous[section_num - 1]
        layers_out.append(one_layer(arrival, norm_gain[section_num], routes[section_num], gate_weights[section_num], w_gate_up[section_num], w_down[section_num]))
    return jnp.stack(layers_out, axis=0)
```

```python
import functools

import jax
import jax.numpy as jnp
from jax import lax
from jax.experimental import pallas as pl
from jax.experimental.pallas import tpu as pltpu
from jax.sharding import PartitionSpec as P

epsilon = 1e-06
LANES = 128
CORES = 2


def from_behind(value, axis, by):
    peers = lax.axis_size(axis)
    pairs = [(i, i + by) for i in range(peers) if 0 <= i + by < peers]
    return lax.ppermute(value, axis, pairs)


def routed_body(fresh, previous, norm_gain, routes, gate_weights, w_gate_up, w_down):
    devices_exp = lax.axis_size("expert")
    section_id = lax.axis_index("section")
    tok_dev = fresh.shape[0]
    width = fresh.shape[1]
    topk_count = routes.shape[2]
    local_experts = w_gate_up.shape[1]
    hidden_units = w_down.shape[2]
    experts_total = devices_exp * local_experts
    capacity = min(tok_dev, 17 * tok_dev * topk_count // (16 * experts_total))
    total_rows = tok_dev * topk_count
    arrived = from_behind(previous[0], "section", 1)
    arrival = jnp.where(section_id == 0, fresh, arrived)
    wide_input = arrival.astype(jnp.float32)
    scale = lax.rsqrt(jnp.mean(wide_input * wide_input, axis=-1, keepdims=True) + epsilon)
    normed = (wide_input * scale * norm_gain[0][None, :]).astype(jnp.bfloat16)
    flat_ids = routes[0].reshape(-1)
    one_hot = (flat_ids[:, None] == jnp.arange(experts_total, dtype=jnp.int32)[None, :]).astype(
        jnp.int32
    )
    slot_rank = jnp.sum(jnp.cumsum(one_hot, axis=0) * one_hot, axis=1) - 1
    position = flat_ids * capacity + slot_rank
    source_row = (
        jnp.full((experts_total * capacity,), total_rows, jnp.int32)
        .at[position]
        .set(jnp.arange(total_rows, dtype=jnp.int32))
    )
    padded = jnp.concatenate([normed, jnp.zeros((1, width), jnp.bfloat16)], axis=0)
    send_buffer = padded[source_row // topk_count].reshape(
        devices_exp, local_experts, capacity, width
    )
    received = lax.all_to_all(send_buffer, "expert", split_axis=0, concat_axis=0, tiled=True)
    projected = jnp.einsum(
        "secd,edf->secf", received, w_gate_up[0], preferred_element_type=jnp.float32
    )
    hidden = (jax.nn.silu(projected[..., :hidden_units]) * projected[..., hidden_units:]).astype(
        jnp.bfloat16
    )
    returned = lax.all_to_all(
        jnp.einsum("secf,efd->secd", hidden, w_down[0], preferred_element_type=jnp.float32).astype(
            jnp.bfloat16
        ),
        "expert",
        split_axis=0,
        concat_axis=0,
        tiled=True,
    )
    flat_back = returned.reshape(experts_total * capacity, width)
    picked = flat_back[position].reshape(tok_dev, topk_count, width).astype(jnp.float32)
    mixed = jnp.sum(picked * gate_weights[0][:, :, None], axis=1)
    return (wide_input + mixed).astype(jnp.bfloat16)[None]


def norm_kernel(section_ref, fresh_ref, arrived_ref, gain_ref, routes_ref, gates_ref, rows_ref, *, experts):
    width = fresh_ref.shape[1]
    rows = fresh_ref.shape[0]
    first = section_ref[0] == 0
    wide = jnp.where(first, fresh_ref[...], arrived_ref[...]).astype(jnp.float32)
    scale = lax.rsqrt(jnp.mean(wide * wide, axis=-1, keepdims=True) + epsilon)
    rows_ref[:, :width] = (wide * scale * gain_ref[...]).astype(jnp.bfloat16)
    lane = lax.broadcasted_iota(jnp.int32, (rows, LANES), 1)
    expert = lane % experts
    term = lane // experts
    weight = jnp.zeros((rows, LANES), jnp.float32)
    for k in range(routes_ref.shape[1]):
        weight += jnp.where(routes_ref[:, k : k + 1] == expert, gates_ref[:, k : k + 1], 0.0)
    high = weight.astype(jnp.bfloat16).astype(jnp.float32)
    middle = (weight - high).astype(jnp.bfloat16).astype(jnp.float32)
    low = weight - high - middle
    terms = jnp.where(term == 0, high, jnp.where(term == 1, middle, jnp.where(term == 2, low, 0.0)))
    rows_ref[:, width:] = terms.astype(jnp.bfloat16)


def norm_rows(section_id, fresh, arrived, gain, routes, gates, experts):
    rows, width = fresh.shape
    vmem = pl.BlockSpec(memory_space=pltpu.VMEM)
    return pl.pallas_call(
        functools.partial(norm_kernel, experts=experts),
        out_shape=jax.ShapeDtypeStruct((rows, width + LANES), jnp.bfloat16),
        in_specs=[pl.BlockSpec(memory_space=pltpu.SMEM)] + [vmem] * 5,
        out_specs=vmem,
        compiler_params=pltpu.CompilerParams(vmem_limit_bytes=32 << 20),
        cost_estimate=pl.CostEstimate(flops=rows * width * 6, bytes_accessed=rows * width * 6, transcendentals=rows),
        name="norm_rows",
    )(section_id.reshape(1), fresh, arrived, gain, routes, gates)


def mlp_kernel(ids_ref, *refs, parts, tiles, experts):
    payloads = refs[:parts]
    weights = refs[parts : parts + 6]
    out_ref, x_ref, coef_ref = refs[parts + 6 :]
    step = pl.program_id(0)
    width = out_ref.shape[1]

    @pl.when(step == 0)
    def _():
        start = 0
        for payload in payloads:
            count = payload.shape[0]
            x_ref[start : start + count, :] = payload[:, :width]
            tail = payload[:, width:].astype(jnp.float32)
            lane = lax.broadcasted_iota(jnp.int32, tail.shape, 1) % experts
            for which in range(2):
                value = jnp.sum(jnp.where(lane == ids_ref[which], tail, 0.0), axis=1, keepdims=True)
                coef_ref[which, start : start + count, :] = jnp.broadcast_to(value, (count, LANES))
            start += count

    def expert(which, gate_ref, up_ref, down_ref):
        gate = jnp.dot(x_ref[...], gate_ref[...], preferred_element_type=jnp.float32)
        up = jnp.dot(x_ref[...], up_ref[...], preferred_element_type=jnp.float32)
        hidden = jax.nn.silu(gate) * up * coef_ref[which][:, :1]
        return jnp.dot(hidden.astype(jnp.bfloat16), down_ref[...], preferred_element_type=jnp.float32)

    @pl.when(step == 0)
    def _():
        out_ref[...] = expert(0, *weights[:3])

    @pl.when((step > 0) & (step < tiles))
    def _():
        out_ref[...] += expert(0, *weights[:3])

    @pl.when(step >= tiles)
    def _():
        out_ref[...] += expert(1, *weights[3:])


def expert_rows(ids, payloads, weights, experts):
    (own_gate_up, own_down), (other_gate_up, other_down) = weights
    width = own_gate_up.shape[0]
    hidden = own_down.shape[0]
    tile = 256
    tiles = hidden // tile
    rows = sum(p.shape[0] for p in payloads)

    def first(step):
        return jnp.minimum(step, tiles - 1)

    def second(step):
        return jnp.maximum(step - tiles, 0)

    def specs(index):
        return [
            pl.BlockSpec((width, tile), lambda i: (0, index(i))),
            pl.BlockSpec((width, tile), lambda i: (0, tiles + index(i))),
            pl.BlockSpec((tile, width), lambda i: (index(i), 0)),
        ]

    return pl.pallas_call(
        functools.partial(mlp_kernel, parts=len(payloads), tiles=tiles, experts=experts),
        grid=(2 * tiles,),
        out_shape=jax.ShapeDtypeStruct((rows, width), jnp.float32),
        in_specs=[pl.BlockSpec(memory_space=pltpu.SMEM)]
        + [pl.BlockSpec(p.shape, lambda i: (0, 0)) for p in payloads]
        + specs(first)
        + specs(second),
        out_specs=pl.BlockSpec((rows, width), lambda i: (0, 0)),
        scratch_shapes=[
            pltpu.VMEM((rows, width), jnp.bfloat16),
            pltpu.VMEM((2, rows, LANES), jnp.float32),
        ],
        compiler_params=pltpu.CompilerParams(vmem_limit_bytes=40 << 20),
        cost_estimate=pl.CostEstimate(
            flops=2 * rows * width * hidden * 6,
            bytes_accessed=width * hidden * 12 + rows * width * 6,
            transcendentals=rows * hidden * 2,
        ),
        name="expert_rows",
    )(ids, *payloads, own_gate_up, own_gate_up, own_down, other_gate_up, other_gate_up, other_down)


def chip_ring(depth, across):
    walk = []
    for z in range(depth):
        xs = list(range(1, across))
        walk += [(z, x) for x in (xs if z % 2 == 0 else xs[::-1])]
    return [z * across + x for z, x in walk + [(z, 0) for z in reversed(range(depth))]]


def relay_body(fresh, previous, norm_gain, routes, gate_weights, w_gate_up, w_down, *, across):
    devices_exp = lax.axis_size("expert")
    section_id = lax.axis_index("section")
    expert_id = lax.axis_index("expert")
    rows = fresh.shape[0]
    half = rows // 2
    chips = devices_exp // CORES
    ring = chip_ring(chips // across, across)
    links = list(zip(ring, ring[1:] + ring[:1]))
    up = [(a * CORES + c, b * CORES + c) for a, b in links for c in range(CORES)]
    down = [(b, a) for a, b in up]
    swap = [(i, i ^ 1) for i in range(devices_exp)]

    def move(value, pairs):
        return lax.ppermute(value, "expert", pairs)

    arrived = from_behind(previous[0], "section", 1)
    own = (w_gate_up[0, 0], w_down[0, 0])
    other = tuple(move(w, swap) for w in own)
    ids = jnp.stack([expert_id, expert_id ^ 1]).astype(jnp.int32)
    packed = norm_rows(section_id, fresh, arrived, norm_gain, routes[0], gate_weights[0], devices_exp)

    def mlp(payloads):
        return expert_rows(ids, payloads, (own, other), devices_exp)

    hops = chips // 2
    ups, downs = [packed], [packed]
    for _ in range(hops - 1):
        ups.append(move(ups[-1], up))
        downs.append(move(downs[-1], down))
    far = [move(ups[-1][:half], up), move(downs[-1][half:], down)]

    sums = [mlp([ups[s], downs[s]]) for s in range(1, hops)]
    far_sum = mlp(far)
    own_sum = mlp([packed])

    going_up = move(far_sum[:half].astype(jnp.bfloat16), up)
    going_down = move(far_sum[half:].astype(jnp.bfloat16), down)
    for s in reversed(range(1, hops)):
        to_up = sums[s - 1][rows:]
        to_down = sums[s - 1][:rows]
        if s == hops - 1:
            going_up = jnp.concatenate([to_up[:half] + going_up, to_up[half:]], axis=0)
            going_down = jnp.concatenate([to_down[:half], to_down[half:] + going_down], axis=0)
        else:
            going_up = to_up + going_up
            going_down = to_down + going_down
        going_up = move(going_up.astype(jnp.bfloat16), up)
        going_down = move(going_down.astype(jnp.bfloat16), down)

    arrival = jnp.where(section_id == 0, fresh, arrived).astype(jnp.float32)
    return (arrival + (own_sum + going_up + going_down)).astype(jnp.bfloat16)[None]


def solution(mesh):
    across = mesh.shape["section"]
    devices_exp = mesh.shape["expert"]

    def body(*args):
        topk_count, local_experts = args[3].shape[2], args[5].shape[1]
        if local_experts == 1 and devices_exp <= 2 * topk_count and devices_exp % (2 * CORES * across) == 0:
            return relay_body(*args, across=across)
        return routed_body(*args)

    return jax.shard_map(
        body,
        mesh=mesh,
        in_specs=(
            P("expert", None),
            P("section", "expert", None),
            P("section", None),
            P("section", "expert", None),
            P("section", "expert", None),
            P("section", "expert", None, None),
            P("section", "expert", None, None),
        ),
        out_specs=P("section", "expert", None),
        check_vma=False,
    )
```

```python
import functools

import jax
import jax.numpy as jnp
from jax import lax
from jax.experimental import pallas as pl
from jax.experimental.pallas import tpu as pltpu
from jax.sharding import PartitionSpec as P

epsilon = 1e-06
LANES = 128
CORES = 2


def from_behind(value, axis, by):
    peers = lax.axis_size(axis)
    pairs = [(i, i + by) for i in range(peers) if 0 <= i + by < peers]
    return lax.ppermute(value, axis, pairs)


def routed_body(fresh, previous, norm_gain, routes, gate_weights, w_gate_up, w_down):
    devices_exp = lax.axis_size("expert")
    section_id = lax.axis_index("section")
    tok_dev = fresh.shape[0]
    width = fresh.shape[1]
    topk_count = routes.shape[2]
    local_experts = w_gate_up.shape[1]
    hidden_units = w_down.shape[2]
    experts_total = devices_exp * local_experts
    capacity = min(tok_dev, 17 * tok_dev * topk_count // (16 * experts_total))
    total_rows = tok_dev * topk_count
    arrived = from_behind(previous[0], "section", 1)
    arrival = jnp.where(section_id == 0, fresh, arrived)
    wide_input = arrival.astype(jnp.float32)
    scale = lax.rsqrt(jnp.mean(wide_input * wide_input, axis=-1, keepdims=True) + epsilon)
    normed = (wide_input * scale * norm_gain[0][None, :]).astype(jnp.bfloat16)
    flat_ids = routes[0].reshape(-1)
    one_hot = (flat_ids[:, None] == jnp.arange(experts_total, dtype=jnp.int32)[None, :]).astype(
        jnp.int32
    )
    slot_rank = jnp.sum(jnp.cumsum(one_hot, axis=0) * one_hot, axis=1) - 1
    position = flat_ids * capacity + slot_rank
    source_row = (
        jnp.full((experts_total * capacity,), total_rows, jnp.int32)
        .at[position]
        .set(jnp.arange(total_rows, dtype=jnp.int32))
    )
    padded = jnp.concatenate([normed, jnp.zeros((1, width), jnp.bfloat16)], axis=0)
    send_buffer = padded[source_row // topk_count].reshape(
        devices_exp, local_experts, capacity, width
    )
    received = lax.all_to_all(send_buffer, "expert", split_axis=0, concat_axis=0, tiled=True)
    projected = jnp.einsum(
        "secd,edf->secf", received, w_gate_up[0], preferred_element_type=jnp.float32
    )
    hidden = (jax.nn.silu(projected[..., :hidden_units]) * projected[..., hidden_units:]).astype(
        jnp.bfloat16
    )
    returned = lax.all_to_all(
        jnp.einsum("secf,efd->secd", hidden, w_down[0], preferred_element_type=jnp.float32).astype(
            jnp.bfloat16
        ),
        "expert",
        split_axis=0,
        concat_axis=0,
        tiled=True,
    )
    flat_back = returned.reshape(experts_total * capacity, width)
    picked = flat_back[position].reshape(tok_dev, topk_count, width).astype(jnp.float32)
    mixed = jnp.sum(picked * gate_weights[0][:, :, None], axis=1)
    return (wide_input + mixed).astype(jnp.bfloat16)[None]


def base_kernel(fresh_ref, gain_ref, routes_ref, gates_ref, rows_ref, gain_out_ref, *, experts):
    width = fresh_ref.shape[1]
    rows = fresh_ref.shape[0]
    rows_ref[:, :width] = normed_rows(fresh_ref[...], gain_ref[...])
    lane = lax.broadcasted_iota(jnp.int32, (rows, LANES), 1)
    expert = lane % experts
    term = lane // experts
    weight = jnp.zeros((rows, LANES), jnp.float32)
    for k in range(routes_ref.shape[1]):
        weight += jnp.where(routes_ref[:, k : k + 1] == expert, gates_ref[:, k : k + 1], 0.0)
    high = weight.astype(jnp.bfloat16).astype(jnp.float32)
    middle = (weight - high).astype(jnp.bfloat16).astype(jnp.float32)
    low = weight - high - middle
    terms = jnp.where(term == 0, high, jnp.where(term == 1, middle, jnp.where(term == 2, low, 0.0)))
    rows_ref[:, width:] = terms.astype(jnp.bfloat16)
    gain_out_ref[...] = gain_ref[...]


def normed_rows(rows, gain):
    wide = rows.astype(jnp.float32)
    scale = lax.rsqrt(jnp.mean(wide * wide, axis=-1, keepdims=True) + epsilon)
    return (wide * scale * gain).astype(jnp.bfloat16)


def base_rows(fresh, gain, routes, gates, experts):
    rows, width = fresh.shape
    vmem = pl.BlockSpec(memory_space=pltpu.VMEM)
    return pl.pallas_call(
        functools.partial(base_kernel, experts=experts),
        out_shape=(
            jax.ShapeDtypeStruct((rows, width + LANES), jnp.bfloat16),
            jax.ShapeDtypeStruct(gain.shape, jnp.float32),
        ),
        in_specs=[vmem] * 4,
        out_specs=(vmem, vmem),
        compiler_params=pltpu.CompilerParams(vmem_limit_bytes=12 << 20),
        cost_estimate=pl.CostEstimate(flops=rows * width * 6, bytes_accessed=rows * width * 4, transcendentals=rows),
        name="base_rows",
    )(fresh, gain, routes, gates)


def norm_kernel(section_ref, base_ref, arrived_ref, gain_ref, rows_ref, *, start):
    rows, width = arrived_ref.shape
    here = slice(start, start + rows)

    @pl.when(section_ref[0] == 0)
    def _():
        rows_ref[:, :width] = base_ref[here, :width]

    @pl.when(section_ref[0] != 0)
    def _():
        rows_ref[:, :width] = normed_rows(arrived_ref[...], gain_ref[...])

    rows_ref[:, width:] = base_ref[here, width:]


def norm_rows(section_id, base, arrived, gain, start):
    rows, width = arrived.shape
    vmem = pl.BlockSpec(memory_space=pltpu.VMEM)
    return pl.pallas_call(
        functools.partial(norm_kernel, start=start),
        out_shape=jax.ShapeDtypeStruct((rows, base.shape[1]), jnp.bfloat16),
        in_specs=[pl.BlockSpec(memory_space=pltpu.SMEM)] + [vmem] * 3,
        out_specs=vmem,
        compiler_params=pltpu.CompilerParams(vmem_limit_bytes=12 << 20),
        cost_estimate=pl.CostEstimate(flops=rows * width * 6, bytes_accessed=rows * width * 6, transcendentals=rows),
        name="norm_rows",
    )(section_id.reshape(1), base, arrived, gain)


def mlp_kernel(ids_ref, *refs, parts, chained, experts):
    payloads = refs[:parts]
    weights = (refs[parts : parts + 2], refs[parts + 2 : parts + 4])
    refs = refs[parts + 4 + chained :]
    outs = refs[:parts]
    x_ref, coef_ref, hidden_ref = refs[parts:]
    width = x_ref.shape[1]
    hidden = weights[0][1].shape[0]
    bounds = []
    start = 0
    for payload in payloads:
        here = slice(start, start + payload.shape[0])
        bounds.append(here)
        start += payload.shape[0]
        x_ref[here, :] = payload[:, :width]
        tail = payload[:, width:].astype(jnp.float32)
        lane = lax.broadcasted_iota(jnp.int32, tail.shape, 1) % experts
        for which in range(2):
            value = jnp.sum(jnp.where(lane == ids_ref[which], tail, 0.0), axis=1, keepdims=True)
            coef_ref[which, here, :] = jnp.broadcast_to(value, tail.shape)
    tile = 256
    for which, (gate_up, _) in enumerate(weights):
        for t in range(0, hidden, tile):
            gate = jnp.dot(x_ref[...], gate_up[:, t : t + tile], preferred_element_type=jnp.float32)
            up = jnp.dot(x_ref[...], gate_up[:, hidden + t : hidden + t + tile], preferred_element_type=jnp.float32)
            value = jax.nn.silu(gate) * up * coef_ref[which][:, :1]
            hidden_ref[:, which * hidden + t : which * hidden + t + tile] = value.astype(jnp.bfloat16)
    tile = 512
    for t in range(0, width, tile):
        total = jnp.zeros((x_ref.shape[0], tile), jnp.float32)
        for which, (_, down) in enumerate(weights):
            rows = hidden_ref[:, which * hidden : (which + 1) * hidden]
            total += jnp.dot(rows, down[:, t : t + tile], preferred_element_type=jnp.float32)
        for here, out in zip(bounds, outs):
            out[:, t : t + tile] = total[here, :]


def expert_rows(ids, payloads, weights, after, experts):
    (own_gate_up, own_down), (other_gate_up, other_down) = weights
    width = own_gate_up.shape[0]
    hidden = own_down.shape[0]
    rows = sum(p.shape[0] for p in payloads)
    vmem = pl.BlockSpec(memory_space=pltpu.VMEM)
    chain = [] if after is None else [after]
    return pl.pallas_call(
        functools.partial(mlp_kernel, parts=len(payloads), chained=len(chain), experts=experts),
        out_shape=[jax.ShapeDtypeStruct((p.shape[0], width), jnp.float32) for p in payloads],
        in_specs=[pl.BlockSpec(memory_space=pltpu.SMEM)]
        + [vmem] * (len(payloads) + 4)
        + [pl.BlockSpec(memory_space=pl.ANY)] * len(chain),
        out_specs=[vmem] * len(payloads),
        scratch_shapes=[
            pltpu.VMEM((rows, width), jnp.bfloat16),
            pltpu.VMEM((2, rows, LANES), jnp.float32),
            pltpu.VMEM((rows, 2 * hidden), jnp.bfloat16),
        ],
        compiler_params=pltpu.CompilerParams(vmem_limit_bytes=12 << 20),
        cost_estimate=pl.CostEstimate(
            flops=2 * rows * width * hidden * 6,
            bytes_accessed=rows * width * 6,
            transcendentals=rows * hidden * 2,
        ),
        name="expert_rows",
    )(ids, *payloads, own_gate_up, own_down, other_gate_up, other_down, *chain)


def chip_ring(depth, across):
    walk = []
    for z in range(depth):
        xs = list(range(1, across))
        walk += [(z, x) for x in (xs if z % 2 == 0 else xs[::-1])]
    return [z * across + x for z, x in walk + [(z, 0) for z in reversed(range(depth))]]


def relay_body(fresh, previous, norm_gain, routes, gate_weights, w_gate_up, w_down, *, across):
    devices_exp = lax.axis_size("expert")
    section_id = lax.axis_index("section")
    expert_id = lax.axis_index("expert")
    rows = fresh.shape[0]
    half = rows // 2
    chips = devices_exp // CORES
    ring = chip_ring(chips // across, across)
    links = list(zip(ring, ring[1:] + ring[:1]))
    up = [(a * CORES + c, b * CORES + c) for a, b in links for c in range(CORES)]
    down = [(b, a) for a, b in up]
    swap = [(i, i ^ 1) for i in range(devices_exp)]

    def move(value, pairs):
        return lax.ppermute(value, "expert", pairs)

    cuts = [slice(0, half), slice(half, rows)]
    arrived = [from_behind(previous[0, cut], "section", 1) for cut in cuts]
    own = (w_gate_up[0, 0], w_down[0, 0])
    other = tuple(move(w, swap) for w in own)
    ids = jnp.stack([expert_id, expert_id ^ 1]).astype(jnp.int32)
    base, gain = base_rows(fresh, norm_gain, routes[0], gate_weights[0], devices_exp)
    packed = [norm_rows(section_id, base, arrived[c], gain, cuts[c].start) for c in range(2)]

    last = None

    def mlp(payloads):
        nonlocal last
        sums = expert_rows(ids, payloads, (own, other), last, devices_exp)
        last = sums[0]
        return sums

    hops = chips // 2
    ups = [packed] + [[None, None] for _ in range(hops)]
    downs = [packed] + [[None, None] for _ in range(hops)]
    to_down, to_up, own_sums = {}, {}, None
    for s in range(hops):
        for c in range(2):
            rising, falling = lax.optimization_barrier((ups[s][c], downs[s][c], last))[:2]
            if s < hops - 1 or c == 0:
                ups[s + 1][c] = move(rising, up)
            if s < hops - 1 or c == 1:
                downs[s + 1][c] = move(falling, down)
            if s > 0:
                to_down[s, c], to_up[s, c] = mlp([ups[s][c], downs[s][c]])
            elif c == 1:
                own_sums = mlp(packed)
    to_up[hops, 0], to_down[hops, 1] = mlp([ups[hops][0], downs[hops][1]])

    flows = [(to_down, 0, down), (to_up, 1, up), (to_up, 0, up), (to_down, 1, down)]
    totals = [None] * len(flows)
    for s in reversed(range(1, hops + 1)):
        for i, (terms, c, pairs) in enumerate(flows):
            place = s if (hops, c) in terms else s - 1
            if place == 0:
                continue
            if totals[i] is None:
                total = terms[place, c]
            else:
                carried = lax.optimization_barrier((totals[i], last))[0]
                total = terms[place, c] + carried.astype(jnp.float32)
            totals[i] = move(total.astype(jnp.bfloat16), pairs)

    outs = []
    for c in range(2):
        arrival = jnp.where(section_id == 0, fresh[cuts[c]], arrived[c]).astype(jnp.float32)
        mixed = own_sums[c]
        for total, flow in zip(totals, flows):
            if flow[1] == c:
                mixed += total.astype(jnp.float32)
        outs.append((arrival + mixed).astype(jnp.bfloat16))
    return jnp.concatenate(outs, axis=0)[None]


def solution(mesh):
    across = mesh.shape["section"]
    devices_exp = mesh.shape["expert"]

    def body(*args):
        topk_count, local_experts = args[3].shape[2], args[5].shape[1]
        if local_experts == 1 and devices_exp <= 2 * topk_count and devices_exp % (2 * CORES * across) == 0:
            return relay_body(*args, across=across)
        return routed_body(*args)

    return jax.shard_map(
        body,
        mesh=mesh,
        in_specs=(
            P("expert", None),
            P("section", "expert", None),
            P("section", None),
            P("section", "expert", None),
            P("section", "expert", None),
            P("section", "expert", None, None),
            P("section", "expert", None, None),
        ),
        out_specs=P("section", "expert", None),
        check_vma=False,
    )
```

```python
import functools

import jax
import jax.numpy as jnp
from jax import lax
from jax.experimental import pallas as pl
from jax.experimental.pallas import tpu as pltpu
from jax.sharding import PartitionSpec as P

epsilon = 1e-06
LANES = 128
CORES = 2
MIB = 1 << 20


def from_behind(value, axis, by):
    peers = lax.axis_size(axis)
    pairs = [(i, i + by) for i in range(peers) if 0 <= i + by < peers]
    return lax.ppermute(value, axis, pairs)


def routed_body(fresh, previous, norm_gain, routes, gate_weights, w_gate_up, w_down):
    devices_exp = lax.axis_size("expert")
    section_id = lax.axis_index("section")
    tok_dev = fresh.shape[0]
    width = fresh.shape[1]
    topk_count = routes.shape[2]
    local_experts = w_gate_up.shape[1]
    hidden_units = w_down.shape[2]
    experts_total = devices_exp * local_experts
    capacity = min(tok_dev, 17 * tok_dev * topk_count // (16 * experts_total))
    total_rows = tok_dev * topk_count
    arrived = from_behind(previous[0], "section", 1)
    arrival = jnp.where(section_id == 0, fresh, arrived)
    wide_input = arrival.astype(jnp.float32)
    scale = lax.rsqrt(jnp.mean(wide_input * wide_input, axis=-1, keepdims=True) + epsilon)
    normed = (wide_input * scale * norm_gain[0][None, :]).astype(jnp.bfloat16)
    flat_ids = routes[0].reshape(-1)
    one_hot = (flat_ids[:, None] == jnp.arange(experts_total, dtype=jnp.int32)[None, :]).astype(
        jnp.int32
    )
    slot_rank = jnp.sum(jnp.cumsum(one_hot, axis=0) * one_hot, axis=1) - 1
    position = flat_ids * capacity + slot_rank
    source_row = (
        jnp.full((experts_total * capacity,), total_rows, jnp.int32)
        .at[position]
        .set(jnp.arange(total_rows, dtype=jnp.int32))
    )
    padded = jnp.concatenate([normed, jnp.zeros((1, width), jnp.bfloat16)], axis=0)
    send_buffer = padded[source_row // topk_count].reshape(
        devices_exp, local_experts, capacity, width
    )
    received = lax.all_to_all(send_buffer, "expert", split_axis=0, concat_axis=0, tiled=True)
    projected = jnp.einsum(
        "secd,edf->secf", received, w_gate_up[0], preferred_element_type=jnp.float32
    )
    hidden = (jax.nn.silu(projected[..., :hidden_units]) * projected[..., hidden_units:]).astype(
        jnp.bfloat16
    )
    returned = lax.all_to_all(
        jnp.einsum("secf,efd->secd", hidden, w_down[0], preferred_element_type=jnp.float32).astype(
            jnp.bfloat16
        ),
        "expert",
        split_axis=0,
        concat_axis=0,
        tiled=True,
    )
    flat_back = returned.reshape(experts_total * capacity, width)
    picked = flat_back[position].reshape(tok_dev, topk_count, width).astype(jnp.float32)
    mixed = jnp.sum(picked * gate_weights[0][:, :, None], axis=1)
    return (wide_input + mixed).astype(jnp.bfloat16)[None]


def base_kernel(fresh_ref, gain_ref, routes_ref, gates_ref, gate_up_ref, down_ref, rows_ref, gain_out_ref, *, experts):
    del gate_up_ref, down_ref
    width = fresh_ref.shape[1]
    rows = fresh_ref.shape[0]
    rows_ref[:, :width] = normed_rows(fresh_ref[...], gain_ref[...])
    lane = lax.broadcasted_iota(jnp.int32, (rows, LANES), 1)
    expert = lane % experts
    term = lane // experts
    weight = jnp.zeros((rows, LANES), jnp.float32)
    for k in range(routes_ref.shape[1]):
        weight += jnp.where(routes_ref[:, k : k + 1] == expert, gates_ref[:, k : k + 1], 0.0)
    high = weight.astype(jnp.bfloat16).astype(jnp.float32)
    middle = (weight - high).astype(jnp.bfloat16).astype(jnp.float32)
    low = weight - high - middle
    terms = jnp.where(term == 0, high, jnp.where(term == 1, middle, jnp.where(term == 2, low, 0.0)))
    rows_ref[:, width:] = terms.astype(jnp.bfloat16)
    gain_out_ref[...] = gain_ref[...]


def normed_rows(rows, gain):
    wide = rows.astype(jnp.float32)
    scale = lax.rsqrt(jnp.mean(wide * wide, axis=-1, keepdims=True) + epsilon)
    return (wide * scale * gain).astype(jnp.bfloat16)


def base_rows(fresh, gain, routes, gates, weights, experts):
    rows, width = fresh.shape
    vmem = pl.BlockSpec(memory_space=pltpu.VMEM)
    return pl.pallas_call(
        functools.partial(base_kernel, experts=experts),
        out_shape=(
            jax.ShapeDtypeStruct((rows, width + LANES), jnp.bfloat16),
            jax.ShapeDtypeStruct(gain.shape, jnp.float32),
        ),
        in_specs=[vmem] * 6,
        out_specs=(vmem, vmem),
        compiler_params=pltpu.CompilerParams(vmem_limit_bytes=16 * MIB),
        cost_estimate=pl.CostEstimate(
            flops=rows * width * 6, bytes_accessed=weights[0].size * 6, transcendentals=rows
        ),
        name="base_rows",
    )(fresh, gain, routes, gates, *weights)


def norm_kernel(section_ref, base_ref, arrived_ref, gain_ref, rows_ref, *, start):
    rows, width = arrived_ref.shape
    here = slice(start, start + rows)

    @pl.when(section_ref[0] == 0)
    def _():
        rows_ref[:, :width] = base_ref[here, :width]

    @pl.when(section_ref[0] != 0)
    def _():
        rows_ref[:, :width] = normed_rows(arrived_ref[...], gain_ref[...])

    rows_ref[:, width:] = base_ref[here, width:]


def norm_rows(section_id, base, arrived, gain, start):
    rows, width = arrived.shape
    vmem = pl.BlockSpec(memory_space=pltpu.VMEM)
    return pl.pallas_call(
        functools.partial(norm_kernel, start=start),
        out_shape=jax.ShapeDtypeStruct((rows, base.shape[1]), jnp.bfloat16),
        in_specs=[pl.BlockSpec(memory_space=pltpu.SMEM)] + [vmem] * 3,
        out_specs=vmem,
        compiler_params=pltpu.CompilerParams(vmem_limit_bytes=12 * MIB),
        cost_estimate=pl.CostEstimate(flops=rows * width * 6, bytes_accessed=rows * width * 6, transcendentals=rows),
        name="norm_rows",
    )(section_id.reshape(1), base, arrived, gain)


def mlp_kernel(ids_ref, *refs, parts, chained, held, experts):
    payloads = refs[:parts]
    own, other = refs[parts : parts + 2], refs[parts + 2 : parts + 4]
    refs = refs[parts + 4 + chained :]
    outs = refs[:parts]
    refs = refs[parts:]
    if held:
        copy = pltpu.make_async_copy(other[0], refs[0], refs[-1])
        copy.start()
        refs = refs[1:-1]
    weights = (own, other)
    x_ref, coef_ref, hidden_ref = refs
    width = x_ref.shape[1]
    hidden = own[1].shape[0]
    bounds = []
    start = 0
    for payload in payloads:
        here = slice(start, start + payload.shape[0])
        bounds.append(here)
        start += payload.shape[0]
        x_ref[here, :] = payload[:, :width]
        tail = payload[:, width:].astype(jnp.float32)
        lane = lax.broadcasted_iota(jnp.int32, tail.shape, 1) % experts
        for which in range(2):
            value = jnp.sum(jnp.where(lane == ids_ref[which], tail, 0.0), axis=1, keepdims=True)
            coef_ref[which, here, :] = jnp.broadcast_to(value, tail.shape)
    tile = 256
    for which, (gate_up, _) in enumerate(weights):
        for t in range(0, hidden, tile):
            gate = jnp.dot(x_ref[...], gate_up[:, t : t + tile], preferred_element_type=jnp.float32)
            up = jnp.dot(x_ref[...], gate_up[:, hidden + t : hidden + t + tile], preferred_element_type=jnp.float32)
            value = jax.nn.silu(gate) * up * coef_ref[which][:, :1]
            hidden_ref[:, which * hidden + t : which * hidden + t + tile] = value.astype(jnp.bfloat16)
    tile = 512
    for t in range(0, width, tile):
        total = jnp.zeros((x_ref.shape[0], tile), jnp.float32)
        for which, (_, down) in enumerate(weights):
            rows = hidden_ref[:, which * hidden : (which + 1) * hidden]
            total += jnp.dot(rows, down[:, t : t + tile], preferred_element_type=jnp.float32)
        for here, out in zip(bounds, outs):
            out[:, t : t + tile] = total[here, :]
    if held:
        copy.wait()


def expert_rows(ids, payloads, own, other, after, experts, hold=False):
    width = own[0].shape[0]
    hidden = own[1].shape[0]
    rows = sum(p.shape[0] for p in payloads)
    vmem = pl.BlockSpec(memory_space=pltpu.VMEM)
    chain = [] if after is None else [after]
    held = [jax.ShapeDtypeStruct(other[0].shape, other[0].dtype)] if hold else []
    results = pl.pallas_call(
        functools.partial(mlp_kernel, parts=len(payloads), chained=len(chain), held=hold, experts=experts),
        out_shape=[jax.ShapeDtypeStruct((p.shape[0], width), jnp.float32) for p in payloads] + held,
        in_specs=[pl.BlockSpec(memory_space=pltpu.SMEM)]
        + [vmem] * (len(payloads) + 4)
        + [pl.BlockSpec(memory_space=pl.ANY)] * len(chain),
        out_specs=[vmem] * (len(payloads) + len(held)),
        scratch_shapes=[
            pltpu.VMEM((rows, width), jnp.bfloat16),
            pltpu.VMEM((2, rows, LANES), jnp.float32),
            pltpu.VMEM((rows, 2 * hidden), jnp.bfloat16),
        ]
        + ([pltpu.SemaphoreType.DMA] if hold else []),
        compiler_params=pltpu.CompilerParams(vmem_limit_bytes=16 * MIB),
        cost_estimate=pl.CostEstimate(
            flops=2 * rows * width * hidden * 6,
            bytes_accessed=rows * width * 6,
            transcendentals=rows * hidden * 2,
        ),
        name="expert_rows",
    )(ids, *payloads, *own, *other, *chain)
    return (results[:-1], results[-1]) if hold else results


def last_kernel(base_ref, first_ref, second_ref, out_ref):
    half = first_ref.shape[0]
    for start, total_ref in ((0, first_ref), (half, second_ref)):
        here = slice(start, start + half)
        out_ref[here, :] = (base_ref[here, :] + total_ref[...].astype(jnp.float32)).astype(jnp.bfloat16)


def last_rows(base, first, second):
    rows, width = base.shape
    vmem = pl.BlockSpec(memory_space=pltpu.VMEM)
    return pl.pallas_call(
        last_kernel,
        out_shape=jax.ShapeDtypeStruct((rows, width), jnp.bfloat16),
        in_specs=[vmem] * 3,
        out_specs=vmem,
        compiler_params=pltpu.CompilerParams(vmem_limit_bytes=8 * MIB),
        cost_estimate=pl.CostEstimate(flops=rows * width, bytes_accessed=rows * width * 8, transcendentals=0),
        name="last_rows",
    )(base, first, second)


def chip_ring(depth, across):
    walk = []
    for z in range(depth):
        xs = list(range(1, across))
        walk += [(z, x) for x in (xs if z % 2 == 0 else xs[::-1])]
    return [z * across + x for z, x in walk + [(z, 0) for z in reversed(range(depth))]]


def relay_body(fresh, previous, norm_gain, routes, gate_weights, w_gate_up, w_down, *, across):
    devices_exp = lax.axis_size("expert")
    section_id = lax.axis_index("section")
    expert_id = lax.axis_index("expert")
    rows = fresh.shape[0]
    half = rows // 2
    chips = devices_exp // CORES
    ring = chip_ring(chips // across, across)
    links = list(zip(ring, ring[1:] + ring[:1]))
    up = [(a * CORES + c, b * CORES + c) for a, b in links for c in range(CORES)]
    down = [(b, a) for a, b in up]
    swap = [(i, i ^ 1) for i in range(devices_exp)]

    def move(value, pairs):
        return lax.ppermute(value, "expert", pairs)

    own = (w_gate_up[0, 0], w_down[0, 0])
    far_other = tuple(move(w, swap) for w in own)
    cuts = [slice(0, half), slice(half, rows)]
    first_cut = previous[0, cuts[0]]
    second_cut = lax.optimization_barrier((previous, first_cut))[0][0, cuts[1]]
    arrived = [from_behind(cut, "section", 1) for cut in (first_cut, second_cut)]
    ids = jnp.stack([expert_id, expert_id ^ 1]).astype(jnp.int32)
    base, gain = base_rows(fresh, norm_gain, routes[0], gate_weights[0], own, devices_exp)
    packed = [norm_rows(section_id, base, arrived[c], gain, cuts[c].start) for c in range(2)]

    hops = chips // 2
    ups = [packed] + [[None, None] for _ in range(hops)]
    downs = [packed] + [[None, None] for _ in range(hops)]

    def pass_on(s, c, after):
        rising, falling = lax.optimization_barrier((ups[s][c], downs[s][c], after))[:2]
        if s < hops - 1 or c == 0:
            ups[s + 1][c] = move(rising, up)
        if s < hops - 1 or c == 1:
            downs[s + 1][c] = move(falling, down)

    pass_on(0, 0, None)
    pass_on(0, 1, None)
    own_sums, other_gate_up = expert_rows(ids, packed, own, far_other, None, devices_exp, hold=True)
    other = (other_gate_up, far_other[1])
    last = own_sums[0]

    def mlp(payloads):
        nonlocal last
        sums = expert_rows(ids, payloads, own, other, last, devices_exp)
        last = sums[0]
        return sums

    to_down, to_up = {}, {}
    for s in range(1, hops - 1):
        pass_on(s, 0, last)
        pass_on(s, 1, (last, ups[s][0], downs[s][0]))
        to_down[s, 0], to_down[s, 1], to_up[s, 0], to_up[s, 1] = mlp(ups[s] + downs[s])
    for c in range(2):
        pass_on(hops - 1, c, (last, ups[hops - 1][0], downs[hops - 1][0]))
        to_down[hops - 1, c], to_up[hops - 1, c] = mlp([ups[hops - 1][c], downs[hops - 1][c]])
    to_up[hops, 0], to_down[hops, 1] = mlp([ups[hops][0], downs[hops][1]])

    flows = [(to_down, 0, down), (to_up, 1, up), (to_up, 0, up), (to_down, 1, down)]
    totals = [None] * len(flows)
    for s in reversed(range(1, hops + 1)):
        for i, (terms, c, pairs) in enumerate(flows):
            place = s if (hops, c) in terms else s - 1
            if place == 0:
                continue
            if totals[i] is None:
                total = terms[place, c]
            else:
                carried = lax.optimization_barrier((totals[i], last))[0]
                total = terms[place, c] + carried.astype(jnp.float32)
            totals[i] = move(total.astype(jnp.bfloat16), pairs)

    arrival = jnp.where(section_id == 0, fresh, jnp.concatenate(arrived, axis=0)).astype(jnp.float32)
    near = [own_sums[c] + totals[c].astype(jnp.float32) for c in range(2)]
    near = lax.optimization_barrier(arrival + jnp.concatenate(near, axis=0))
    return last_rows(near, totals[2], totals[3])[None]


def solution(mesh):
    across = mesh.shape["section"]
    devices_exp = mesh.shape["expert"]

    def body(*args):
        topk_count, local_experts = args[3].shape[2], args[5].shape[1]
        if local_experts == 1 and devices_exp <= 2 * topk_count and devices_exp % (2 * CORES * across) == 0:
            return relay_body(*args, across=across)
        return routed_body(*args)

    return jax.shard_map(
        body,
        mesh=mesh,
        in_specs=(
            P("expert", None),
            P("section", "expert", None),
            P("section", None),
            P("section", "expert", None),
            P("section", "expert", None),
            P("section", "expert", None, None),
            P("section", "expert", None, None),
        ),
        out_specs=P("section", "expert", None),
        check_vma=False,
    )
```

```python
import functools

import jax
import jax.numpy as jnp
from jax import lax
from jax.experimental import pallas as pl
from jax.experimental.pallas import tpu as pltpu
from jax.sharding import PartitionSpec as P

epsilon = 1e-06
LANES = 128
CORES = 2
MIB = 1 << 20
HOLD = False


def from_behind(value, axis, by):
    peers = lax.axis_size(axis)
    pairs = [(i, i + by) for i in range(peers) if 0 <= i + by < peers]
    return lax.ppermute(value, axis, pairs)


def routed_body(fresh, previous, norm_gain, routes, gate_weights, w_gate_up, w_down):
    devices_exp = lax.axis_size("expert")
    section_id = lax.axis_index("section")
    tok_dev = fresh.shape[0]
    width = fresh.shape[1]
    topk_count = routes.shape[2]
    local_experts = w_gate_up.shape[1]
    hidden_units = w_down.shape[2]
    experts_total = devices_exp * local_experts
    capacity = min(tok_dev, 17 * tok_dev * topk_count // (16 * experts_total))
    total_rows = tok_dev * topk_count
    arrived = from_behind(previous[0], "section", 1)
    arrival = jnp.where(section_id == 0, fresh, arrived)
    wide_input = arrival.astype(jnp.float32)
    scale = lax.rsqrt(jnp.mean(wide_input * wide_input, axis=-1, keepdims=True) + epsilon)
    normed = (wide_input * scale * norm_gain[0][None, :]).astype(jnp.bfloat16)
    flat_ids = routes[0].reshape(-1)
    one_hot = (flat_ids[:, None] == jnp.arange(experts_total, dtype=jnp.int32)[None, :]).astype(
        jnp.int32
    )
    slot_rank = jnp.sum(jnp.cumsum(one_hot, axis=0) * one_hot, axis=1) - 1
    position = flat_ids * capacity + slot_rank
    source_row = (
        jnp.full((experts_total * capacity,), total_rows, jnp.int32)
        .at[position]
        .set(jnp.arange(total_rows, dtype=jnp.int32))
    )
    padded = jnp.concatenate([normed, jnp.zeros((1, width), jnp.bfloat16)], axis=0)
    send_buffer = padded[source_row // topk_count].reshape(
        devices_exp, local_experts, capacity, width
    )
    received = lax.all_to_all(send_buffer, "expert", split_axis=0, concat_axis=0, tiled=True)
    projected = jnp.einsum(
        "secd,edf->secf", received, w_gate_up[0], preferred_element_type=jnp.float32
    )
    hidden = (jax.nn.silu(projected[..., :hidden_units]) * projected[..., hidden_units:]).astype(
        jnp.bfloat16
    )
    returned = lax.all_to_all(
        jnp.einsum("secf,efd->secd", hidden, w_down[0], preferred_element_type=jnp.float32).astype(
            jnp.bfloat16
        ),
        "expert",
        split_axis=0,
        concat_axis=0,
        tiled=True,
    )
    flat_back = returned.reshape(experts_total * capacity, width)
    picked = flat_back[position].reshape(tok_dev, topk_count, width).astype(jnp.float32)
    mixed = jnp.sum(picked * gate_weights[0][:, :, None], axis=1)
    return (wide_input + mixed).astype(jnp.bfloat16)[None]


def normed_rows(rows, gain):
    wide = rows.astype(jnp.float32)
    scale = lax.rsqrt(jnp.mean(wide * wide, axis=-1, keepdims=True) + epsilon)
    return (wide * scale * gain).astype(jnp.bfloat16)


def base_kernel(fresh_ref, gain_ref, routes_ref, gates_ref, rows_ref, fresh_out_ref, gain_out_ref, *, experts):
    width = fresh_ref.shape[1]
    rows = fresh_ref.shape[0]
    rows_ref[:, :width] = normed_rows(fresh_ref[...], gain_ref[...])
    line = lax.broadcasted_iota(jnp.int32, (LANES, rows), 0)
    expert = line % experts
    term = line // experts
    weight = jnp.zeros((LANES, rows), jnp.float32)
    for k in range(routes_ref.shape[0]):
        weight += jnp.where(routes_ref[k : k + 1, :] == expert, gates_ref[k : k + 1, :], 0.0)
    high = weight.astype(jnp.bfloat16).astype(jnp.float32)
    middle = (weight - high).astype(jnp.bfloat16).astype(jnp.float32)
    low = weight - high - middle
    terms = jnp.where(term == 0, high, jnp.where(term == 1, middle, jnp.where(term == 2, low, 0.0)))
    rows_ref[:, width:] = terms.T.astype(jnp.bfloat16)
    fresh_out_ref[...] = fresh_ref[...]
    gain_out_ref[...] = gain_ref[...]


def base_rows(fresh, gain, routes, gates, experts):
    rows, width = fresh.shape
    vmem = pl.BlockSpec(memory_space=pltpu.VMEM)
    return pl.pallas_call(
        functools.partial(base_kernel, experts=experts),
        out_shape=(
            jax.ShapeDtypeStruct((rows, width + LANES), jnp.bfloat16),
            jax.ShapeDtypeStruct(fresh.shape, fresh.dtype),
            jax.ShapeDtypeStruct(gain.shape, jnp.float32),
        ),
        in_specs=[vmem] * 4,
        out_specs=(vmem,) * 3,
        compiler_params=pltpu.CompilerParams(vmem_limit_bytes=12 * MIB),
        cost_estimate=pl.CostEstimate(flops=rows * width * 6, bytes_accessed=rows * width * 8, transcendentals=rows),
        name="base_rows",
    )(fresh, gain, routes, gates)


def norm_kernel(section_ref, base_ref, fresh_ref, arrived_ref, gain_ref, rows_ref, arrival_ref, *, start):
    rows, width = arrived_ref.shape
    here = slice(start, start + rows)

    @pl.when(section_ref[0] == 0)
    def _():
        rows_ref[:, :width] = base_ref[here, :width]
        arrival_ref[...] = fresh_ref[here, :]

    @pl.when(section_ref[0] != 0)
    def _():
        rows_ref[:, :width] = normed_rows(arrived_ref[...], gain_ref[...])
        arrival_ref[...] = arrived_ref[...]

    rows_ref[:, width:] = base_ref[here, width:]


def norm_rows(section_id, base, fresh, arrived, gain, start):
    rows, width = arrived.shape
    vmem = pl.BlockSpec(memory_space=pltpu.VMEM)
    return pl.pallas_call(
        functools.partial(norm_kernel, start=start),
        out_shape=(
            jax.ShapeDtypeStruct((rows, base.shape[1]), jnp.bfloat16),
            jax.ShapeDtypeStruct((rows, width), jnp.bfloat16),
        ),
        in_specs=[pl.BlockSpec(memory_space=pltpu.SMEM)] + [vmem] * 4,
        out_specs=(vmem, vmem),
        compiler_params=pltpu.CompilerParams(vmem_limit_bytes=12 * MIB),
        cost_estimate=pl.CostEstimate(flops=rows * width * 6, bytes_accessed=rows * width * 8, transcendentals=rows),
        name="norm_rows",
    )(section_id, base, fresh, arrived, gain)


def mlp_kernel(expert_ref, *refs, parts, chained, held, experts):
    payloads = refs[:parts]
    own, other = refs[parts : parts + 2], refs[parts + 2 : parts + 4]
    refs = refs[parts + 4 + chained :]
    outs = refs[:parts]
    refs = refs[parts:]
    if held:
        copy = pltpu.make_async_copy(other[0], refs[0], refs[-1])
        copy.start()
        refs = refs[1:-1]
    weights = (own, other)
    x_ref, coef_ref, hidden_ref = refs
    width = x_ref.shape[1]
    hidden = own[1].shape[0]
    bounds = []
    start = 0
    for payload in payloads:
        here = slice(start, start + payload.shape[0])
        bounds.append(here)
        start += payload.shape[0]
        x_ref[here, :] = payload[:, :width]
        tail = payload[:, width:].astype(jnp.float32)
        lane = lax.broadcasted_iota(jnp.int32, tail.shape, 1) % experts
        for which in range(2):
            value = jnp.sum(jnp.where(lane == expert_ref[0] ^ which, tail, 0.0), axis=1, keepdims=True)
            coef_ref[which, here, :] = jnp.broadcast_to(value, tail.shape)
    tile = 256
    for which, (gate_up, _) in enumerate(weights):
        for t in range(0, hidden, tile):
            gate = jnp.dot(x_ref[...], gate_up[:, t : t + tile], preferred_element_type=jnp.float32)
            up = jnp.dot(x_ref[...], gate_up[:, hidden + t : hidden + t + tile], preferred_element_type=jnp.float32)
            value = jax.nn.silu(gate) * up * coef_ref[which][:, :1]
            hidden_ref[:, which * hidden + t : which * hidden + t + tile] = value.astype(jnp.bfloat16)
    tile = 512
    for t in range(0, width, tile):
        total = jnp.zeros((x_ref.shape[0], tile), jnp.float32)
        for which, (_, down) in enumerate(weights):
            rows = hidden_ref[:, which * hidden : (which + 1) * hidden]
            total += jnp.dot(rows, down[:, t : t + tile], preferred_element_type=jnp.float32)
        for here, out in zip(bounds, outs):
            out[:, t : t + tile] = total[here, :]
    if held:
        copy.wait()


def expert_rows(expert_id, payloads, own, other, after, experts, hold=False):
    width = own[0].shape[0]
    hidden = own[1].shape[0]
    rows = sum(p.shape[0] for p in payloads)
    vmem = pl.BlockSpec(memory_space=pltpu.VMEM)
    chain = [] if after is None else [after]
    held = [jax.ShapeDtypeStruct(other[0].shape, other[0].dtype)] if hold else []
    results = pl.pallas_call(
        functools.partial(mlp_kernel, parts=len(payloads), chained=len(chain), held=hold, experts=experts),
        out_shape=[jax.ShapeDtypeStruct((p.shape[0], width), jnp.float32) for p in payloads] + held,
        in_specs=[pl.BlockSpec(memory_space=pltpu.SMEM)]
        + [vmem] * (len(payloads) + 4)
        + [pl.BlockSpec(memory_space=pl.ANY)] * len(chain),
        out_specs=[vmem] * (len(payloads) + len(held)),
        scratch_shapes=[
            pltpu.VMEM((rows, width), jnp.bfloat16),
            pltpu.VMEM((2, rows, LANES), jnp.float32),
            pltpu.VMEM((rows, 2 * hidden), jnp.bfloat16),
        ]
        + ([pltpu.SemaphoreType.DMA] if hold else []),
        compiler_params=pltpu.CompilerParams(vmem_limit_bytes=16 * MIB),
        cost_estimate=pl.CostEstimate(
            flops=2 * rows * width * hidden * 6,
            bytes_accessed=rows * width * 6,
            transcendentals=rows * hidden * 2,
        ),
        name="expert_rows",
    )(expert_id, *payloads, *own, *other, *chain)
    return (results[:-1], results[-1]) if hold else results


def last_kernel(near0_ref, near1_ref, total0_ref, total1_ref, out_ref):
    half = near0_ref.shape[0]
    for start, near_ref, total_ref in ((0, near0_ref, total0_ref), (half, near1_ref, total1_ref)):
        total = near_ref[...] + total_ref[...].astype(jnp.float32)
        out_ref[start : start + half, :] = total.astype(jnp.bfloat16)


def last_rows(nears, totals):
    rows, width = nears[0].shape
    vmem = pl.BlockSpec(memory_space=pltpu.VMEM)
    return pl.pallas_call(
        last_kernel,
        out_shape=jax.ShapeDtypeStruct((2 * rows, width), jnp.bfloat16),
        in_specs=[vmem] * 4,
        out_specs=vmem,
        compiler_params=pltpu.CompilerParams(vmem_limit_bytes=8 * MIB),
        cost_estimate=pl.CostEstimate(flops=2 * rows * width, bytes_accessed=rows * width * 16, transcendentals=0),
        name="last_rows",
    )(*nears, *totals)


def chip_ring(depth, across):
    walk = []
    for z in range(depth):
        xs = list(range(1, across))
        walk += [(z, x) for x in (xs if z % 2 == 0 else xs[::-1])]
    return [z * across + x for z, x in walk + [(z, 0) for z in reversed(range(depth))]]


def relay_body(fresh, previous, norm_gain, routes, gate_weights, w_gate_up, w_down, *, across):
    devices_exp = lax.axis_size("expert")
    section_id = lax.axis_index("section").astype(jnp.int32).reshape(1)
    expert_id = lax.axis_index("expert").astype(jnp.int32).reshape(1)
    rows = fresh.shape[0]
    half = rows // 2
    chips = devices_exp // CORES
    ring = chip_ring(chips // across, across)
    links = list(zip(ring, ring[1:] + ring[:1]))
    up = [(a * CORES + c, b * CORES + c) for a, b in links for c in range(CORES)]
    down = [(b, a) for a, b in up]
    swap = [(i, i ^ 1) for i in range(devices_exp)]

    def move(value, pairs):
        return lax.ppermute(value, "expert", pairs)

    cuts = [slice(0, half), slice(half, rows)]
    arrived = [from_behind(previous[0, cut], "section", 1) for cut in cuts]
    own = (w_gate_up[0, 0], w_down[0, 0])
    swapped = lax.optimization_barrier((*own, section_id, expert_id))[:2]
    other = tuple(move(w, swap) for w in swapped)
    base, fresh, gain = base_rows(fresh, norm_gain, routes[0].T, gate_weights[0].T, devices_exp)
    packed, arrival = zip(*(norm_rows(section_id, base, fresh, arrived[c], gain, cuts[c].start) for c in range(2)))
    packed = list(packed)

    hops = chips // 2
    ups = [packed] + [[None, None] for _ in range(hops)]
    downs = [packed] + [[None, None] for _ in range(hops)]

    def pass_on(s, c, after):
        rising, falling = lax.optimization_barrier((ups[s][c], downs[s][c], after))[:2]
        if s < hops - 1 or c == 0:
            ups[s + 1][c] = move(rising, up)
        if s < hops - 1 or c == 1:
            downs[s + 1][c] = move(falling, down)

    last = None

    def mlp(payloads, hold=False):
        nonlocal last, other
        sums = expert_rows(expert_id, payloads, own, other, last, devices_exp, hold)
        if hold:
            sums, other_gate_up = sums
            other = (other_gate_up, other[1])
        last = sums[0]
        return sums

    to_down, to_up = {}, {}
    pass_on(0, 0, None)
    pass_on(0, 1, None)
    own_sums = mlp(packed, HOLD)
    for s in range(1, hops):
        for c in range(2):
            pass_on(s, c, last)
            to_down[s, c], to_up[s, c] = mlp([ups[s][c], downs[s][c]])
    to_up[hops, 0], to_down[hops, 1] = mlp([ups[hops][0], downs[hops][1]])

    flows = [(to_down, 0, down), (to_up, 1, up), (to_up, 0, up), (to_down, 1, down)]
    totals = [None] * len(flows)
    for s in reversed(range(1, hops + 1)):
        for i, (terms, c, pairs) in enumerate(flows):
            place = s if (hops, c) in terms else s - 1
            if place == 0:
                continue
            if totals[i] is None:
                total = terms[place, c]
            else:
                carried = lax.optimization_barrier((totals[i], last))[0]
                total = terms[place, c] + carried.astype(jnp.float32)
            totals[i] = move(total.astype(jnp.bfloat16), pairs)

    nears = [
        arrival[c].astype(jnp.float32) + (own_sums[c] + totals[c].astype(jnp.float32)) for c in range(2)
    ]
    nears = lax.optimization_barrier(nears)
    return last_rows(nears, totals[2:])[None]


def solution(mesh):
    across = mesh.shape["section"]
    devices_exp = mesh.shape["expert"]

    def body(*args):
        topk_count, local_experts = args[3].shape[2], args[5].shape[1]
        if local_experts == 1 and devices_exp <= 2 * topk_count and devices_exp % (2 * CORES * across) == 0:
            return relay_body(*args, across=across)
        return routed_body(*args)

    return jax.shard_map(
        body,
        mesh=mesh,
        in_specs=(
            P("expert", None),
            P("section", "expert", None),
            P("section", None),
            P("section", "expert", None),
            P("section", "expert", None),
            P("section", "expert", None, None),
            P("section", "expert", None, None),
        ),
        out_specs=P("section", "expert", None),
        check_vma=False,
    )
```

```python
import functools

import jax
import jax.numpy as jnp
from jax import lax
from jax.experimental import pallas as pl
from jax.experimental.pallas import tpu as pltpu
from jax.sharding import PartitionSpec as P

epsilon = 1e-06
LANES = 128
CORES = 2
MIB = 1 << 20


def from_behind(value, axis, by):
    peers = lax.axis_size(axis)
    pairs = [(i, i + by) for i in range(peers) if 0 <= i + by < peers]
    return lax.ppermute(value, axis, pairs)


def routed_body(fresh, previous, norm_gain, routes, gate_weights, w_gate_up, w_down):
    devices_exp = lax.axis_size("expert")
    section_id = lax.axis_index("section")
    tok_dev = fresh.shape[0]
    width = fresh.shape[1]
    topk_count = routes.shape[2]
    local_experts = w_gate_up.shape[1]
    hidden_units = w_down.shape[2]
    experts_total = devices_exp * local_experts
    capacity = min(tok_dev, 17 * tok_dev * topk_count // (16 * experts_total))
    total_rows = tok_dev * topk_count
    arrived = from_behind(previous[0], "section", 1)
    arrival = jnp.where(section_id == 0, fresh, arrived)
    wide_input = arrival.astype(jnp.float32)
    scale = lax.rsqrt(jnp.mean(wide_input * wide_input, axis=-1, keepdims=True) + epsilon)
    normed = (wide_input * scale * norm_gain[0][None, :]).astype(jnp.bfloat16)
    flat_ids = routes[0].reshape(-1)
    one_hot = (flat_ids[:, None] == jnp.arange(experts_total, dtype=jnp.int32)[None, :]).astype(
        jnp.int32
    )
    slot_rank = jnp.sum(jnp.cumsum(one_hot, axis=0) * one_hot, axis=1) - 1
    position = flat_ids * capacity + slot_rank
    source_row = (
        jnp.full((experts_total * capacity,), total_rows, jnp.int32)
        .at[position]
        .set(jnp.arange(total_rows, dtype=jnp.int32))
    )
    padded = jnp.concatenate([normed, jnp.zeros((1, width), jnp.bfloat16)], axis=0)
    send_buffer = padded[source_row // topk_count].reshape(
        devices_exp, local_experts, capacity, width
    )
    received = lax.all_to_all(send_buffer, "expert", split_axis=0, concat_axis=0, tiled=True)
    projected = jnp.einsum(
        "secd,edf->secf", received, w_gate_up[0], preferred_element_type=jnp.float32
    )
    hidden = (jax.nn.silu(projected[..., :hidden_units]) * projected[..., hidden_units:]).astype(
        jnp.bfloat16
    )
    returned = lax.all_to_all(
        jnp.einsum("secf,efd->secd", hidden, w_down[0], preferred_element_type=jnp.float32).astype(
            jnp.bfloat16
        ),
        "expert",
        split_axis=0,
        concat_axis=0,
        tiled=True,
    )
    flat_back = returned.reshape(experts_total * capacity, width)
    picked = flat_back[position].reshape(tok_dev, topk_count, width).astype(jnp.float32)
    mixed = jnp.sum(picked * gate_weights[0][:, :, None], axis=1)
    return (wide_input + mixed).astype(jnp.bfloat16)[None]


def normed_rows(rows, gain):
    wide = rows.astype(jnp.float32)
    scale = lax.rsqrt(jnp.mean(wide * wide, axis=-1, keepdims=True) + epsilon)
    return (wide * scale * gain).astype(jnp.bfloat16)


def base_kernel(fresh_ref, gain_ref, routes_ref, gates_ref, rows_ref, fresh_out_ref, gain_out_ref, *, experts):
    width = fresh_ref.shape[1]
    rows = fresh_ref.shape[0]
    rows_ref[:, :width] = normed_rows(fresh_ref[...], gain_ref[...])
    line = lax.broadcasted_iota(jnp.int32, (LANES, rows), 0)
    expert = line % experts
    term = line // experts
    weight = jnp.zeros((LANES, rows), jnp.float32)
    for k in range(routes_ref.shape[0]):
        weight += jnp.where(routes_ref[k : k + 1, :] == expert, gates_ref[k : k + 1, :], 0.0)
    high = weight.astype(jnp.bfloat16).astype(jnp.float32)
    middle = (weight - high).astype(jnp.bfloat16).astype(jnp.float32)
    low = weight - high - middle
    terms = jnp.where(term == 0, high, jnp.where(term == 1, middle, jnp.where(term == 2, low, 0.0)))
    rows_ref[:, width:] = terms.T.astype(jnp.bfloat16)
    fresh_out_ref[...] = fresh_ref[...]
    gain_out_ref[...] = gain_ref[...]


def base_rows(fresh, gain, routes, gates, experts):
    rows, width = fresh.shape
    vmem = pl.BlockSpec(memory_space=pltpu.VMEM)
    return pl.pallas_call(
        functools.partial(base_kernel, experts=experts),
        out_shape=(
            jax.ShapeDtypeStruct((rows, width + LANES), jnp.bfloat16),
            jax.ShapeDtypeStruct(fresh.shape, fresh.dtype),
            jax.ShapeDtypeStruct(gain.shape, jnp.float32),
        ),
        in_specs=[vmem] * 4,
        out_specs=(vmem,) * 3,
        compiler_params=pltpu.CompilerParams(vmem_limit_bytes=12 * MIB),
        cost_estimate=pl.CostEstimate(flops=rows * width * 6, bytes_accessed=rows * width * 8, transcendentals=rows),
        name="base_rows",
    )(fresh, gain, routes, gates)


def norm_kernel(section_ref, base_ref, fresh_ref, arrived_ref, gain_ref, rows_ref, arrival_ref, *, start):
    rows, width = arrived_ref.shape
    here = slice(start, start + rows)

    @pl.when(section_ref[0] == 0)
    def _():
        rows_ref[:, :width] = base_ref[here, :width]
        arrival_ref[...] = fresh_ref[here, :]

    @pl.when(section_ref[0] != 0)
    def _():
        rows_ref[:, :width] = normed_rows(arrived_ref[...], gain_ref[...])
        arrival_ref[...] = arrived_ref[...]

    rows_ref[:, width:] = base_ref[here, width:]


def norm_rows(section_id, base, fresh, arrived, gain, start):
    rows, width = arrived.shape
    vmem = pl.BlockSpec(memory_space=pltpu.VMEM)
    return pl.pallas_call(
        functools.partial(norm_kernel, start=start),
        out_shape=(
            jax.ShapeDtypeStruct((rows, base.shape[1]), jnp.bfloat16),
            jax.ShapeDtypeStruct((rows, width), jnp.bfloat16),
        ),
        in_specs=[pl.BlockSpec(memory_space=pltpu.SMEM)] + [vmem] * 4,
        out_specs=(vmem, vmem),
        compiler_params=pltpu.CompilerParams(vmem_limit_bytes=12 * MIB),
        cost_estimate=pl.CostEstimate(flops=rows * width * 6, bytes_accessed=rows * width * 8, transcendentals=rows),
        name="norm_rows",
    )(section_id, base, fresh, arrived, gain)


def mlp_kernel(expert_ref, *refs, parts, chained, experts):
    payloads = refs[:parts]
    own, other = refs[parts : parts + 2], refs[parts + 2 : parts + 4]
    refs = refs[parts + 4 + chained :]
    outs = refs[:parts]
    refs = refs[parts:]
    weights = (own, other)
    x_ref, coef_ref, hidden_ref = refs
    width = x_ref.shape[1]
    hidden = own[1].shape[0]
    bounds = []
    start = 0
    for payload in payloads:
        here = slice(start, start + payload.shape[0])
        bounds.append(here)
        start += payload.shape[0]
        x_ref[here, :] = payload[:, :width]
        tail = payload[:, width:].astype(jnp.float32)
        lane = lax.broadcasted_iota(jnp.int32, tail.shape, 1) % experts
        for which in range(2):
            value = jnp.sum(jnp.where(lane == expert_ref[0] ^ which, tail, 0.0), axis=1, keepdims=True)
            coef_ref[which, here, :] = jnp.broadcast_to(value, tail.shape)
    tile = 256
    for which, (gate_up, _) in enumerate(weights):
        for t in range(0, hidden, tile):
            gate = jnp.dot(x_ref[...], gate_up[:, t : t + tile], preferred_element_type=jnp.float32)
            up = jnp.dot(x_ref[...], gate_up[:, hidden + t : hidden + t + tile], preferred_element_type=jnp.float32)
            value = jax.nn.silu(gate) * up * coef_ref[which][:, :1]
            hidden_ref[:, which * hidden + t : which * hidden + t + tile] = value.astype(jnp.bfloat16)
    tile = 512
    for t in range(0, width, tile):
        total = jnp.zeros((x_ref.shape[0], tile), jnp.float32)
        for which, (_, down) in enumerate(weights):
            rows = hidden_ref[:, which * hidden : (which + 1) * hidden]
            total += jnp.dot(rows, down[:, t : t + tile], preferred_element_type=jnp.float32)
        for here, out in zip(bounds, outs):
            out[:, t : t + tile] = total[here, :]


def expert_rows(expert_id, payloads, own, other, after, experts):
    width = own[0].shape[0]
    hidden = own[1].shape[0]
    rows = sum(p.shape[0] for p in payloads)
    vmem = pl.BlockSpec(memory_space=pltpu.VMEM)
    chain = [] if after is None else [after]
    return pl.pallas_call(
        functools.partial(mlp_kernel, parts=len(payloads), chained=len(chain), experts=experts),
        out_shape=[jax.ShapeDtypeStruct((p.shape[0], width), jnp.float32) for p in payloads],
        in_specs=[pl.BlockSpec(memory_space=pltpu.SMEM)]
        + [vmem] * (len(payloads) + 4)
        + [pl.BlockSpec(memory_space=pl.ANY)] * len(chain),
        out_specs=[vmem] * len(payloads),
        scratch_shapes=[
            pltpu.VMEM((rows, width), jnp.bfloat16),
            pltpu.VMEM((2, rows, LANES), jnp.float32),
            pltpu.VMEM((rows, 2 * hidden), jnp.bfloat16),
        ],
        compiler_params=pltpu.CompilerParams(vmem_limit_bytes=16 * MIB),
        cost_estimate=pl.CostEstimate(
            flops=2 * rows * width * hidden * 6,
            bytes_accessed=rows * width * 6,
            transcendentals=rows * hidden * 2,
        ),
        name="expert_rows",
    )(expert_id, *payloads, *own, *other, *chain)


def last_kernel(near0_ref, near1_ref, total0_ref, total1_ref, out_ref):
    half = near0_ref.shape[0]
    for start, near_ref, total_ref in ((0, near0_ref, total0_ref), (half, near1_ref, total1_ref)):
        total = near_ref[...] + total_ref[...].astype(jnp.float32)
        out_ref[start : start + half, :] = total.astype(jnp.bfloat16)


def last_rows(nears, totals):
    rows, width = nears[0].shape
    vmem = pl.BlockSpec(memory_space=pltpu.VMEM)
    return pl.pallas_call(
        last_kernel,
        out_shape=jax.ShapeDtypeStruct((2 * rows, width), jnp.bfloat16),
        in_specs=[vmem] * 4,
        out_specs=vmem,
        compiler_params=pltpu.CompilerParams(vmem_limit_bytes=8 * MIB),
        cost_estimate=pl.CostEstimate(flops=2 * rows * width, bytes_accessed=rows * width * 16, transcendentals=0),
        name="last_rows",
    )(*nears, *totals)


def chip_ring(depth, across):
    walk = []
    for z in range(depth):
        xs = list(range(1, across))
        walk += [(z, x) for x in (xs if z % 2 == 0 else xs[::-1])]
    return [z * across + x for z, x in walk + [(z, 0) for z in reversed(range(depth))]]


def relay_body(fresh, previous, norm_gain, routes, gate_weights, w_gate_up, w_down, *, across):
    devices_exp = lax.axis_size("expert")
    section_id = lax.axis_index("section").astype(jnp.int32).reshape(1)
    expert_id = lax.axis_index("expert").astype(jnp.int32).reshape(1)
    rows = fresh.shape[0]
    half = rows // 2
    chips = devices_exp // CORES
    ring = chip_ring(chips // across, across)
    links = list(zip(ring, ring[1:] + ring[:1]))
    up = [(a * CORES + c, b * CORES + c) for a, b in links for c in range(CORES)]
    down = [(b, a) for a, b in up]
    swap = [(i, i ^ 1) for i in range(devices_exp)]

    def move(value, pairs):
        return lax.ppermute(value, "expert", pairs)

    cuts = [slice(0, half), slice(half, rows)]
    own = (w_gate_up[0, 0], w_down[0, 0])
    swapped = lax.optimization_barrier((*own, section_id, expert_id))[:2]
    other = tuple(move(w, swap) for w in swapped)
    base, fresh, gain = base_rows(fresh, norm_gain, routes[0].T, gate_weights[0].T, devices_exp)
    arrived = [from_behind(previous[0, cut], "section", 1) for cut in cuts]
    packed, arrival = zip(*(norm_rows(section_id, base, fresh, arrived[c], gain, cuts[c].start) for c in range(2)))
    packed = list(packed)

    hops = chips // 2
    ups = [packed] + [[None, None] for _ in range(hops)]
    downs = [packed] + [[None, None] for _ in range(hops)]

    def pass_on(s, c, after):
        rising, falling = lax.optimization_barrier((ups[s][c], downs[s][c], after))[:2]
        if s < hops - 1 or c == 0:
            ups[s + 1][c] = move(rising, up)
        if s < hops - 1 or c == 1:
            downs[s + 1][c] = move(falling, down)

    last = None

    def mlp(payloads):
        nonlocal last
        sums = expert_rows(expert_id, payloads, own, other, last, devices_exp)
        last = sums[0]
        return sums

    to_down, to_up = {}, {}
    pass_on(0, 0, None)
    pass_on(0, 1, None)
    for s in range(1, hops):
        for c in range(2):
            pass_on(s, c, last)
            to_down[s, c], to_up[s, c] = mlp([ups[s][c], downs[s][c]])
    to_up[hops, 0], to_down[hops, 1] = mlp([ups[hops][0], downs[hops][1]])
    own_sums = mlp(packed)

    def send_on(flow, place, total, after):
        terms, c, pairs = flow
        if total is None:
            total = terms[place, c]
        else:
            carried = lax.optimization_barrier((total, after))[0]
            total = terms[place, c] + carried.astype(jnp.float32)
        total = total.astype(jnp.bfloat16)
        return total, move(total, pairs)

    short = [(to_down, 0, down), (to_up, 1, up)]
    long = [(to_up, 0, up), (to_down, 1, down)]
    short_totals = [send_on(flow, hops - 1, None, None)[1] for flow in short]
    long_totals = [send_on(flow, hops, None, None)[1] for flow in long]
    after = to_up[hops, 0]
    for s in reversed(range(1, hops)):
        if s > 1:
            sent, short_totals = zip(*(send_on(f, s - 1, t, after) for f, t in zip(short, short_totals)))
        sent, long_totals = zip(*(send_on(f, s, t, sent) for f, t in zip(long, long_totals)))
        after = sent

    nears = [
        arrival[c].astype(jnp.float32) + (own_sums[c] + short_totals[c].astype(jnp.float32)) for c in range(2)
    ]
    nears = lax.optimization_barrier(nears)
    return last_rows(nears, long_totals)[None]


def solution(mesh):
    across = mesh.shape["section"]
    devices_exp = mesh.shape["expert"]

    def body(*args):
        topk_count, local_experts = args[3].shape[2], args[5].shape[1]
        if local_experts == 1 and devices_exp <= 2 * topk_count and devices_exp % (2 * CORES * across) == 0:
            return relay_body(*args, across=across)
        return routed_body(*args)

    return jax.shard_map(
        body,
        mesh=mesh,
        in_specs=(
            P("expert", None),
            P("section", "expert", None),
            P("section", None),
            P("section", "expert", None),
            P("section", "expert", None),
            P("section", "expert", None, None),
            P("section", "expert", None, None),
        ),
        out_specs=P("section", "expert", None),
        check_vma=False,
    )
```

```python
import functools

import jax
import jax.numpy as jnp
from jax import lax
from jax.experimental import pallas as pl
from jax.experimental.pallas import tpu as pltpu
from jax.sharding import PartitionSpec as P

epsilon = 1e-06
LANES = 128
CORES = 2
MIB = 1 << 20


def from_behind(value, axis, by):
    peers = lax.axis_size(axis)
    pairs = [(i, i + by) for i in range(peers) if 0 <= i + by < peers]
    return lax.ppermute(value, axis, pairs)


def routed_body(fresh, previous, norm_gain, routes, gate_weights, w_gate_up, w_down):
    devices_exp = lax.axis_size("expert")
    section_id = lax.axis_index("section")
    tok_dev = fresh.shape[0]
    width = fresh.shape[1]
    topk_count = routes.shape[2]
    local_experts = w_gate_up.shape[1]
    hidden_units = w_down.shape[2]
    experts_total = devices_exp * local_experts
    capacity = min(tok_dev, 17 * tok_dev * topk_count // (16 * experts_total))
    total_rows = tok_dev * topk_count
    arrived = from_behind(previous[0], "section", 1)
    arrival = jnp.where(section_id == 0, fresh, arrived)
    wide_input = arrival.astype(jnp.float32)
    scale = lax.rsqrt(jnp.mean(wide_input * wide_input, axis=-1, keepdims=True) + epsilon)
    normed = (wide_input * scale * norm_gain[0][None, :]).astype(jnp.bfloat16)
    flat_ids = routes[0].reshape(-1)
    one_hot = (flat_ids[:, None] == jnp.arange(experts_total, dtype=jnp.int32)[None, :]).astype(
        jnp.int32
    )
    slot_rank = jnp.sum(jnp.cumsum(one_hot, axis=0) * one_hot, axis=1) - 1
    position = flat_ids * capacity + slot_rank
    source_row = (
        jnp.full((experts_total * capacity,), total_rows, jnp.int32)
        .at[position]
        .set(jnp.arange(total_rows, dtype=jnp.int32))
    )
    padded = jnp.concatenate([normed, jnp.zeros((1, width), jnp.bfloat16)], axis=0)
    send_buffer = padded[source_row // topk_count].reshape(
        devices_exp, local_experts, capacity, width
    )
    received = lax.all_to_all(send_buffer, "expert", split_axis=0, concat_axis=0, tiled=True)
    projected = jnp.einsum(
        "secd,edf->secf", received, w_gate_up[0], preferred_element_type=jnp.float32
    )
    hidden = (jax.nn.silu(projected[..., :hidden_units]) * projected[..., hidden_units:]).astype(
        jnp.bfloat16
    )
    returned = lax.all_to_all(
        jnp.einsum("secf,efd->secd", hidden, w_down[0], preferred_element_type=jnp.float32).astype(
            jnp.bfloat16
        ),
        "expert",
        split_axis=0,
        concat_axis=0,
        tiled=True,
    )
    flat_back = returned.reshape(experts_total * capacity, width)
    picked = flat_back[position].reshape(tok_dev, topk_count, width).astype(jnp.float32)
    mixed = jnp.sum(picked * gate_weights[0][:, :, None], axis=1)
    return (wide_input + mixed).astype(jnp.bfloat16)[None]


def normed_rows(rows, gain):
    wide = rows.astype(jnp.float32)
    scale = lax.rsqrt(jnp.mean(wide * wide, axis=-1, keepdims=True) + epsilon)
    return (wide * scale * gain).astype(jnp.bfloat16)


def base_kernel(fresh_ref, gain_ref, routes_ref, gates_ref, rows_ref, fresh_out_ref, gain_out_ref, *, experts):
    width = fresh_ref.shape[1]
    rows = fresh_ref.shape[0]
    rows_ref[:, :width] = normed_rows(fresh_ref[...], gain_ref[...])
    line = lax.broadcasted_iota(jnp.int32, (LANES, rows), 0)
    expert = line % experts
    term = line // experts
    weight = jnp.zeros((LANES, rows), jnp.float32)
    for k in range(routes_ref.shape[0]):
        weight += jnp.where(routes_ref[k : k + 1, :] == expert, gates_ref[k : k + 1, :], 0.0)
    high = weight.astype(jnp.bfloat16).astype(jnp.float32)
    middle = (weight - high).astype(jnp.bfloat16).astype(jnp.float32)
    low = weight - high - middle
    terms = jnp.where(term == 0, high, jnp.where(term == 1, middle, jnp.where(term == 2, low, 0.0)))
    rows_ref[:, width:] = terms.T.astype(jnp.bfloat16)
    fresh_out_ref[...] = fresh_ref[...]
    gain_out_ref[...] = gain_ref[...]


def base_rows(fresh, gain, routes, gates, experts):
    rows, width = fresh.shape
    vmem = pl.BlockSpec(memory_space=pltpu.VMEM)
    return pl.pallas_call(
        functools.partial(base_kernel, experts=experts),
        out_shape=(
            jax.ShapeDtypeStruct((rows, width + LANES), jnp.bfloat16),
            jax.ShapeDtypeStruct(fresh.shape, fresh.dtype),
            jax.ShapeDtypeStruct(gain.shape, jnp.float32),
        ),
        in_specs=[vmem] * 4,
        out_specs=(vmem,) * 3,
        compiler_params=pltpu.CompilerParams(vmem_limit_bytes=12 * MIB),
        cost_estimate=pl.CostEstimate(flops=rows * width * 6, bytes_accessed=rows * width * 8, transcendentals=rows),
        name="base_rows",
    )(fresh, gain, routes, gates)


def norm_kernel(section_ref, base_ref, fresh_ref, arrived_ref, gain_ref, rows_ref, arrival_ref, *, start):
    rows, width = arrived_ref.shape
    here = slice(start, start + rows)

    @pl.when(section_ref[0] == 0)
    def _():
        rows_ref[:, :width] = base_ref[here, :width]
        arrival_ref[...] = fresh_ref[here, :]

    @pl.when(section_ref[0] != 0)
    def _():
        rows_ref[:, :width] = normed_rows(arrived_ref[...], gain_ref[...])
        arrival_ref[...] = arrived_ref[...]

    rows_ref[:, width:] = base_ref[here, width:]


def norm_rows(section_id, base, fresh, arrived, gain, start):
    rows, width = arrived.shape
    vmem = pl.BlockSpec(memory_space=pltpu.VMEM)
    return pl.pallas_call(
        functools.partial(norm_kernel, start=start),
        out_shape=(
            jax.ShapeDtypeStruct((rows, base.shape[1]), jnp.bfloat16),
            jax.ShapeDtypeStruct((rows, width), jnp.bfloat16),
        ),
        in_specs=[pl.BlockSpec(memory_space=pltpu.SMEM)] + [vmem] * 4,
        out_specs=(vmem, vmem),
        compiler_params=pltpu.CompilerParams(vmem_limit_bytes=12 * MIB),
        cost_estimate=pl.CostEstimate(flops=rows * width * 6, bytes_accessed=rows * width * 8, transcendentals=rows),
        name="norm_rows",
    )(section_id, base, fresh, arrived, gain)


def mlp_kernel(expert_ref, *refs, parts, chained, experts):
    payloads = refs[:parts]
    own, other = refs[parts : parts + 2], refs[parts + 2 : parts + 4]
    refs = refs[parts + 4 + chained :]
    outs = refs[:parts]
    refs = refs[parts:]
    weights = (own, other)
    x_ref, coef_ref, hidden_ref = refs
    width = x_ref.shape[1]
    hidden = own[1].shape[0]
    bounds = []
    start = 0
    for payload in payloads:
        here = slice(start, start + payload.shape[0])
        bounds.append(here)
        start += payload.shape[0]
        x_ref[here, :] = payload[:, :width]
        tail = payload[:, width:].astype(jnp.float32)
        lane = lax.broadcasted_iota(jnp.int32, tail.shape, 1) % experts
        for which in range(2):
            value = jnp.sum(jnp.where(lane == expert_ref[0] ^ which, tail, 0.0), axis=1, keepdims=True)
            coef_ref[which, here, :] = jnp.broadcast_to(value, tail.shape)
    tile = 256
    for which, (gate_up, _) in enumerate(weights):
        for t in range(0, hidden, tile):
            gate = jnp.dot(x_ref[...], gate_up[:, t : t + tile], preferred_element_type=jnp.float32)
            up = jnp.dot(x_ref[...], gate_up[:, hidden + t : hidden + t + tile], preferred_element_type=jnp.float32)
            value = jax.nn.silu(gate) * up * coef_ref[which][:, :1]
            hidden_ref[:, which * hidden + t : which * hidden + t + tile] = value.astype(jnp.bfloat16)
    tile = 512
    for t in range(0, width, tile):
        total = jnp.zeros((x_ref.shape[0], tile), jnp.float32)
        for which, (_, down) in enumerate(weights):
            rows = hidden_ref[:, which * hidden : (which + 1) * hidden]
            total += jnp.dot(rows, down[:, t : t + tile], preferred_element_type=jnp.float32)
        for here, out in zip(bounds, outs):
            out[:, t : t + tile] = total[here, :]


def expert_rows(expert_id, payloads, own, other, after, experts):
    width = own[0].shape[0]
    hidden = own[1].shape[0]
    rows = sum(p.shape[0] for p in payloads)
    vmem = pl.BlockSpec(memory_space=pltpu.VMEM)
    chain = [] if after is None else [after]
    return pl.pallas_call(
        functools.partial(mlp_kernel, parts=len(payloads), chained=len(chain), experts=experts),
        out_shape=[jax.ShapeDtypeStruct((p.shape[0], width), jnp.float32) for p in payloads],
        in_specs=[pl.BlockSpec(memory_space=pltpu.SMEM)]
        + [vmem] * (len(payloads) + 4)
        + [pl.BlockSpec(memory_space=pl.ANY)] * len(chain),
        out_specs=[vmem] * len(payloads),
        scratch_shapes=[
            pltpu.VMEM((rows, width), jnp.bfloat16),
            pltpu.VMEM((2, rows, LANES), jnp.float32),
            pltpu.VMEM((rows, 2 * hidden), jnp.bfloat16),
        ],
        compiler_params=pltpu.CompilerParams(vmem_limit_bytes=16 * MIB),
        cost_estimate=pl.CostEstimate(
            flops=2 * rows * width * hidden * 6,
            bytes_accessed=rows * width * 6,
            transcendentals=rows * hidden * 2,
        ),
        name="expert_rows",
    )(expert_id, *payloads, *own, *other, *chain)


def last_kernel(near0_ref, near1_ref, total0_ref, total1_ref, out_ref):
    half = near0_ref.shape[0]
    for start, near_ref, total_ref in ((0, near0_ref, total0_ref), (half, near1_ref, total1_ref)):
        total = near_ref[...] + total_ref[...].astype(jnp.float32)
        out_ref[start : start + half, :] = total.astype(jnp.bfloat16)


def last_rows(nears, totals):
    rows, width = nears[0].shape
    vmem = pl.BlockSpec(memory_space=pltpu.VMEM)
    return pl.pallas_call(
        last_kernel,
        out_shape=jax.ShapeDtypeStruct((2 * rows, width), jnp.bfloat16),
        in_specs=[vmem] * 4,
        out_specs=vmem,
        compiler_params=pltpu.CompilerParams(vmem_limit_bytes=8 * MIB),
        cost_estimate=pl.CostEstimate(flops=2 * rows * width, bytes_accessed=rows * width * 16, transcendentals=0),
        name="last_rows",
    )(*nears, *totals)


def chip_ring(depth, across):
    walk = []
    for z in range(depth):
        xs = list(range(1, across))
        walk += [(z, x) for x in (xs if z % 2 == 0 else xs[::-1])]
    return [z * across + x for z, x in walk + [(z, 0) for z in reversed(range(depth))]]


def relay_body(fresh, previous, norm_gain, routes, gate_weights, w_gate_up, w_down, *, across):
    devices_exp = lax.axis_size("expert")
    section_id = lax.axis_index("section").astype(jnp.int32).reshape(1)
    expert_id = lax.axis_index("expert").astype(jnp.int32).reshape(1)
    rows = fresh.shape[0]
    half = rows // 2
    chips = devices_exp // CORES
    ring = chip_ring(chips // across, across)
    links = list(zip(ring, ring[1:] + ring[:1]))
    up = [(a * CORES + c, b * CORES + c) for a, b in links for c in range(CORES)]
    down = [(b, a) for a, b in up]
    swap = [(i, i ^ 1) for i in range(devices_exp)]

    def move(value, pairs):
        return lax.ppermute(value, "expert", pairs)

    cuts = [slice(0, half), slice(half, rows)]
    own = (w_gate_up[0, 0], w_down[0, 0])
    swapped = lax.optimization_barrier((*own, section_id, expert_id))[:2]
    other = tuple(move(w, swap) for w in swapped)
    base, fresh, gain = base_rows(fresh, norm_gain, routes[0].T, gate_weights[0].T, devices_exp)
    arrived = [from_behind(previous[0, cut], "section", 1) for cut in cuts]
    packed, arrival = zip(*(norm_rows(section_id, base, fresh, arrived[c], gain, cuts[c].start) for c in range(2)))
    packed = list(packed)

    hops = chips // 2
    ups = [packed] + [[None, None] for _ in range(hops)]
    downs = [packed] + [[None, None] for _ in range(hops)]

    def pass_on(s, c, after):
        rising, falling = lax.optimization_barrier((ups[s][c], downs[s][c], after))[:2]
        if s < hops - 1 or c == 0:
            ups[s + 1][c] = move(rising, up)
        if s < hops - 1 or c == 1:
            downs[s + 1][c] = move(falling, down)

    last = None

    def mlp(payloads):
        nonlocal last
        sums = expert_rows(expert_id, payloads, own, other, last, devices_exp)
        last = sums[0]
        return sums

    to_down, to_up = {}, {}
    pass_on(0, 0, None)
    pass_on(0, 1, None)
    own_sums = mlp(packed)
    for s in range(1, hops):
        for c in range(2):
            pass_on(s, c, last)
            to_down[s, c], to_up[s, c] = mlp([ups[s][c], downs[s][c]])
    to_up[hops, 0] = mlp([ups[hops][0]])[0]
    to_down[hops, 1] = mlp([downs[hops][1]])[0]

    def send_on(flow, place, total, after):
        terms, c, pairs = flow
        if total is None:
            total = terms[place, c]
        else:
            carried = lax.optimization_barrier((total, after))[0]
            total = terms[place, c] + carried.astype(jnp.float32)
        total = total.astype(jnp.bfloat16)
        return total, move(total, pairs)

    short = [(to_down, 0, down), (to_up, 1, up)]
    long = [(to_up, 0, up), (to_down, 1, down)]
    short_totals = [send_on(flow, hops - 1, None, None)[1] for flow in short]
    long_totals = [send_on(flow, hops, None, None)[1] for flow in long]
    after = last
    for s in reversed(range(1, hops)):
        if s > 1:
            sent, short_totals = zip(*(send_on(f, s - 1, t, after) for f, t in zip(short, short_totals)))
        sent, long_totals = zip(*(send_on(f, s, t, sent) for f, t in zip(long, long_totals)))
        after = sent

    nears = [
        arrival[c].astype(jnp.float32) + (own_sums[c] + short_totals[c].astype(jnp.float32)) for c in range(2)
    ]
    nears = lax.optimization_barrier(nears)
    return last_rows(nears, long_totals)[None]


def solution(mesh):
    across = mesh.shape["section"]
    devices_exp = mesh.shape["expert"]

    def body(*args):
        topk_count, local_experts = args[3].shape[2], args[5].shape[1]
        if local_experts == 1 and devices_exp <= 2 * topk_count and devices_exp % (2 * CORES * across) == 0:
            return relay_body(*args, across=across)
        return routed_body(*args)

    return jax.shard_map(
        body,
        mesh=mesh,
        in_specs=(
            P("expert", None),
            P("section", "expert", None),
            P("section", None),
            P("section", "expert", None),
            P("section", "expert", None),
            P("section", "expert", None, None),
            P("section", "expert", None, None),
        ),
        out_specs=P("section", "expert", None),
        check_vma=False,
    )
```

```python
import functools

import jax
import jax.numpy as jnp
from jax import lax
from jax.experimental import pallas as pl
from jax.experimental.pallas import tpu as pltpu
from jax.sharding import PartitionSpec as P

epsilon = 1e-06
LANES = 128
HALF = LANES // 2
CORES = 2
MIB = 1 << 20


def from_behind(value, axis, by):
    peers = lax.axis_size(axis)
    pairs = [(i, i + by) for i in range(peers) if 0 <= i + by < peers]
    return lax.ppermute(value, axis, pairs)


def routed_body(fresh, previous, norm_gain, routes, gate_weights, w_gate_up, w_down):
    devices_exp = lax.axis_size("expert")
    section_id = lax.axis_index("section")
    tok_dev = fresh.shape[0]
    width = fresh.shape[1]
    topk_count = routes.shape[2]
    local_experts = w_gate_up.shape[1]
    hidden_units = w_down.shape[2]
    experts_total = devices_exp * local_experts
    capacity = min(tok_dev, 17 * tok_dev * topk_count // (16 * experts_total))
    total_rows = tok_dev * topk_count
    arrived = from_behind(previous[0], "section", 1)
    arrival = jnp.where(section_id == 0, fresh, arrived)
    wide_input = arrival.astype(jnp.float32)
    scale = lax.rsqrt(jnp.mean(wide_input * wide_input, axis=-1, keepdims=True) + epsilon)
    normed = (wide_input * scale * norm_gain[0][None, :]).astype(jnp.bfloat16)
    flat_ids = routes[0].reshape(-1)
    one_hot = (flat_ids[:, None] == jnp.arange(experts_total, dtype=jnp.int32)[None, :]).astype(
        jnp.int32
    )
    slot_rank = jnp.sum(jnp.cumsum(one_hot, axis=0) * one_hot, axis=1) - 1
    position = flat_ids * capacity + slot_rank
    source_row = (
        jnp.full((experts_total * capacity,), total_rows, jnp.int32)
        .at[position]
        .set(jnp.arange(total_rows, dtype=jnp.int32))
    )
    padded = jnp.concatenate([normed, jnp.zeros((1, width), jnp.bfloat16)], axis=0)
    send_buffer = padded[source_row // topk_count].reshape(
        devices_exp, local_experts, capacity, width
    )
    received = lax.all_to_all(send_buffer, "expert", split_axis=0, concat_axis=0, tiled=True)
    projected = jnp.einsum(
        "secd,edf->secf", received, w_gate_up[0], preferred_element_type=jnp.float32
    )
    hidden = (jax.nn.silu(projected[..., :hidden_units]) * projected[..., hidden_units:]).astype(
        jnp.bfloat16
    )
    returned = lax.all_to_all(
        jnp.einsum("secf,efd->secd", hidden, w_down[0], preferred_element_type=jnp.float32).astype(
            jnp.bfloat16
        ),
        "expert",
        split_axis=0,
        concat_axis=0,
        tiled=True,
    )
    flat_back = returned.reshape(experts_total * capacity, width)
    picked = flat_back[position].reshape(tok_dev, topk_count, width).astype(jnp.float32)
    mixed = jnp.sum(picked * gate_weights[0][:, :, None], axis=1)
    return (wide_input + mixed).astype(jnp.bfloat16)[None]


def normed_rows(rows, gain):
    wide = rows.astype(jnp.float32)
    scale = lax.rsqrt(jnp.mean(wide * wide, axis=-1, keepdims=True) + epsilon)
    return (wide * scale * gain).astype(jnp.bfloat16)


def base_kernel(fresh_ref, gain_ref, routes_ref, gates_ref, rows_ref, coefs_ref, fresh_out_ref, gain_out_ref):
    rows_ref[...] = normed_rows(fresh_ref[...], gain_ref[...])
    shape = coefs_ref.shape[1:]
    expert = lax.broadcasted_iota(jnp.int32, shape, 0)
    weight = jnp.zeros(shape, jnp.float32)
    for k in range(routes_ref.shape[0]):
        weight += jnp.where(routes_ref[k : k + 1, :] == expert, gates_ref[k : k + 1, :], 0.0)
    high = weight.astype(jnp.bfloat16).astype(jnp.float32)
    low = weight - high
    left = lax.broadcasted_iota(jnp.int32, shape, 1) < HALF
    coefs_ref[0] = jnp.where(left, high, pltpu.roll(low, HALF, 1)).astype(jnp.bfloat16)
    coefs_ref[1] = jnp.where(left, pltpu.roll(high, HALF, 1), low).astype(jnp.bfloat16)
    fresh_out_ref[...] = fresh_ref[...]
    gain_out_ref[...] = gain_ref[...]


def base_rows(fresh, gain, routes, gates, experts):
    rows, width = fresh.shape
    vmem = pl.BlockSpec(memory_space=pltpu.VMEM)
    return pl.pallas_call(
        base_kernel,
        out_shape=(
            jax.ShapeDtypeStruct((rows, width), jnp.bfloat16),
            jax.ShapeDtypeStruct((2, experts, rows), jnp.bfloat16),
            jax.ShapeDtypeStruct(fresh.shape, fresh.dtype),
            jax.ShapeDtypeStruct(gain.shape, jnp.float32),
        ),
        in_specs=[vmem] * 4,
        out_specs=(vmem,) * 4,
        compiler_params=pltpu.CompilerParams(vmem_limit_bytes=12 * MIB),
        cost_estimate=pl.CostEstimate(flops=rows * width * 6, bytes_accessed=rows * width * 8, transcendentals=rows),
        name="base_rows",
    )(fresh, gain, routes, gates)


def norm_kernel(section_ref, base_ref, coefs_ref, fresh_ref, arrived_ref, gain_ref, rows_ref, arrival_ref, *, chunk):
    rows, width = arrived_ref.shape
    here = slice(chunk * rows, (chunk + 1) * rows)

    def pack(normed):
        for i in range(width // LANES):
            rows_ref[i * rows : (i + 1) * rows, :] = normed[:, i * LANES : (i + 1) * LANES]

    @pl.when(section_ref[0] == 0)
    def _():
        pack(base_ref[here, :])
        arrival_ref[...] = fresh_ref[here, :]

    @pl.when(section_ref[0] != 0)
    def _():
        pack(normed_rows(arrived_ref[...], gain_ref[...]))
        arrival_ref[...] = arrived_ref[...]

    rows_ref[rows * (width // LANES) :, :] = coefs_ref[chunk]


def norm_rows(section_id, base, coefs, fresh, arrived, gain, chunk):
    rows, width = arrived.shape
    vmem = pl.BlockSpec(memory_space=pltpu.VMEM)
    return pl.pallas_call(
        functools.partial(norm_kernel, chunk=chunk),
        out_shape=(
            jax.ShapeDtypeStruct((rows * (width // LANES) + coefs.shape[1], LANES), jnp.bfloat16),
            jax.ShapeDtypeStruct((rows, width), jnp.bfloat16),
        ),
        in_specs=[pl.BlockSpec(memory_space=pltpu.SMEM)] + [vmem] * 5,
        out_specs=(vmem, vmem),
        compiler_params=pltpu.CompilerParams(vmem_limit_bytes=12 * MIB),
        cost_estimate=pl.CostEstimate(flops=rows * width * 6, bytes_accessed=rows * width * 8, transcendentals=rows),
        name="norm_rows",
    )(section_id, base, coefs, fresh, arrived, gain)


def mlp_kernel(expert_ref, *refs, parts, chained):
    payloads = refs[:parts]
    weights = (refs[parts : parts + 2], refs[parts + 2 : parts + 4])
    refs = refs[parts + 4 + chained :]
    outs = refs[:parts]
    x_ref, coef_ref, hidden_ref = refs[parts:]
    width = x_ref.shape[1]
    hidden = weights[0][1].shape[0]
    line = lax.broadcasted_iota(jnp.int32, (HALF, LANES), 0)
    token = line == lax.broadcasted_iota(jnp.int32, (HALF, LANES), 1) % HALF
    bounds = []
    for part, payload in enumerate(payloads):
        here = slice(part * HALF, (part + 1) * HALF)
        bounds.append(here)
        for i in range(width // LANES):
            x_ref[here, i * LANES : (i + 1) * LANES] = payload[i * HALF : (i + 1) * HALF, :]
        block = payload[HALF * (width // LANES) :, :].astype(jnp.float32)
        expert = lax.broadcasted_iota(jnp.int32, block.shape, 0)
        for which in range(2):
            terms = jnp.sum(jnp.where(expert == expert_ref[0] ^ which, block, 0.0), axis=0, keepdims=True)
            value = jnp.sum(jnp.where(token, terms, 0.0), axis=1, keepdims=True)
            coef_ref[which, here, :] = jnp.broadcast_to(value, (HALF, LANES))
    tile = 256
    for which, (gate_up, _) in enumerate(weights):
        for t in range(0, hidden, tile):
            gate = jnp.dot(x_ref[...], gate_up[:, t : t + tile], preferred_element_type=jnp.float32)
            up = jnp.dot(x_ref[...], gate_up[:, hidden + t : hidden + t + tile], preferred_element_type=jnp.float32)
            value = jax.nn.silu(gate) * up * coef_ref[which][:, :1]
            hidden_ref[:, which * hidden + t : which * hidden + t + tile] = value.astype(jnp.bfloat16)
    tile = 512
    for t in range(0, width, tile):
        total = jnp.zeros((x_ref.shape[0], tile), jnp.float32)
        for which, (_, down) in enumerate(weights):
            rows = hidden_ref[:, which * hidden : (which + 1) * hidden]
            total += jnp.dot(rows, down[:, t : t + tile], preferred_element_type=jnp.float32)
        for here, out in zip(bounds, outs):
            out[:, t : t + tile] = total[here, :]


def expert_rows(expert_id, payloads, own, other, after):
    width = own[0].shape[0]
    hidden = own[1].shape[0]
    rows = HALF * len(payloads)
    vmem = pl.BlockSpec(memory_space=pltpu.VMEM)
    chain = [] if after is None else [after]
    return pl.pallas_call(
        functools.partial(mlp_kernel, parts=len(payloads), chained=len(chain)),
        out_shape=[jax.ShapeDtypeStruct((HALF, width), jnp.float32)] * len(payloads),
        in_specs=[pl.BlockSpec(memory_space=pltpu.SMEM)]
        + [vmem] * (len(payloads) + 4)
        + [pl.BlockSpec(memory_space=pl.ANY)] * len(chain),
        out_specs=[vmem] * len(payloads),
        scratch_shapes=[
            pltpu.VMEM((rows, width), jnp.bfloat16),
            pltpu.VMEM((2, rows, LANES), jnp.float32),
            pltpu.VMEM((rows, 2 * hidden), jnp.bfloat16),
        ],
        compiler_params=pltpu.CompilerParams(vmem_limit_bytes=16 * MIB),
        cost_estimate=pl.CostEstimate(
            flops=2 * rows * width * hidden * 6,
            bytes_accessed=rows * width * 6,
            transcendentals=rows * hidden * 2,
        ),
        name="expert_rows",
    )(expert_id, *payloads, *own, *other, *chain)


def last_kernel(near0_ref, near1_ref, total0_ref, total1_ref, out_ref):
    half = near0_ref.shape[0]
    for start, near_ref, total_ref in ((0, near0_ref, total0_ref), (half, near1_ref, total1_ref)):
        total = near_ref[...] + total_ref[...].astype(jnp.float32)
        out_ref[start : start + half, :] = total.astype(jnp.bfloat16)


def last_rows(nears, totals):
    rows, width = nears[0].shape
    vmem = pl.BlockSpec(memory_space=pltpu.VMEM)
    return pl.pallas_call(
        last_kernel,
        out_shape=jax.ShapeDtypeStruct((2 * rows, width), jnp.bfloat16),
        in_specs=[vmem] * 4,
        out_specs=vmem,
        compiler_params=pltpu.CompilerParams(vmem_limit_bytes=8 * MIB),
        cost_estimate=pl.CostEstimate(flops=2 * rows * width, bytes_accessed=rows * width * 16, transcendentals=0),
        name="last_rows",
    )(*nears, *totals)


def chip_ring(depth, across):
    walk = []
    for z in range(depth):
        xs = list(range(1, across))
        walk += [(z, x) for x in (xs if z % 2 == 0 else xs[::-1])]
    return [z * across + x for z, x in walk + [(z, 0) for z in reversed(range(depth))]]


def relay_body(fresh, previous, norm_gain, routes, gate_weights, w_gate_up, w_down, *, across):
    devices_exp = lax.axis_size("expert")
    section_id = lax.axis_index("section").astype(jnp.int32).reshape(1)
    expert_id = lax.axis_index("expert").astype(jnp.int32).reshape(1)
    rows = fresh.shape[0]
    half = HALF
    chips = devices_exp // CORES
    ring = chip_ring(chips // across, across)
    links = list(zip(ring, ring[1:] + ring[:1]))
    up = [(a * CORES + c, b * CORES + c) for a, b in links for c in range(CORES)]
    down = [(b, a) for a, b in up]
    swap = [(i, i ^ 1) for i in range(devices_exp)]

    def move(value, pairs):
        return lax.ppermute(value, "expert", pairs)

    cuts = [slice(0, half), slice(half, rows)]
    own = (w_gate_up[0, 0], w_down[0, 0])
    swapped = lax.optimization_barrier((*own, section_id, expert_id))[:2]
    other = tuple(move(w, swap) for w in swapped)
    base, coefs, fresh, gain = base_rows(fresh, norm_gain, routes[0].T, gate_weights[0].T, devices_exp)
    arrived = [from_behind(previous[0, cut], "section", 1) for cut in cuts]
    packed, arrival = zip(*(norm_rows(section_id, base, coefs, fresh, arrived[c], gain, c) for c in range(2)))
    packed = list(packed)

    hops = chips // 2
    ups = [packed] + [[None, None] for _ in range(hops)]
    downs = [packed] + [[None, None] for _ in range(hops)]

    def pass_on(s, c, after):
        rising, falling = lax.optimization_barrier((ups[s][c], downs[s][c], after))[:2]
        if s < hops - 1 or c == 0:
            ups[s + 1][c] = move(rising, up)
        if s < hops - 1 or c == 1:
            downs[s + 1][c] = move(falling, down)

    last = None

    def mlp(payloads):
        nonlocal last
        sums = expert_rows(expert_id, payloads, own, other, last)
        last = sums[0]
        return sums

    to_down, to_up = {}, {}
    pass_on(0, 0, None)
    pass_on(0, 1, None)
    own_sums = mlp(packed)
    for s in range(1, hops):
        for c in range(2):
            pass_on(s, c, last)
            to_down[s, c], to_up[s, c] = mlp([ups[s][c], downs[s][c]])
    to_up[hops, 0], to_down[hops, 1] = mlp([ups[hops][0], downs[hops][1]])

    def send_on(flow, place, total, after):
        terms, c, pairs = flow
        if total is None:
            total = terms[place, c]
        else:
            carried = lax.optimization_barrier((total, after))[0]
            total = terms[place, c] + carried.astype(jnp.float32)
        total = total.astype(jnp.bfloat16)
        return total, move(total, pairs)

    short = [(to_down, 0, down), (to_up, 1, up)]
    long = [(to_up, 0, up), (to_down, 1, down)]
    short_totals = [send_on(flow, hops - 1, None, None)[1] for flow in short]
    long_totals = [send_on(flow, hops, None, None)[1] for flow in long]
    after = to_up[hops, 0]
    for s in reversed(range(1, hops)):
        if s > 1:
            sent, short_totals = zip(*(send_on(f, s - 1, t, after) for f, t in zip(short, short_totals)))
        sent, long_totals = zip(*(send_on(f, s, t, sent) for f, t in zip(long, long_totals)))
        after = sent

    nears = [
        arrival[c].astype(jnp.float32) + (own_sums[c] + short_totals[c].astype(jnp.float32)) for c in range(2)
    ]
    nears = lax.optimization_barrier(nears)
    return last_rows(nears, long_totals)[None]


def solution(mesh):
    across = mesh.shape["section"]
    devices_exp = mesh.shape["expert"]

    def body(*args):
        topk_count, local_experts = args[3].shape[2], args[5].shape[1]
        regular = devices_exp % (2 * CORES * across) == 0 and devices_exp % 16 == 0 and args[0].shape[0] == LANES
        if local_experts == 1 and devices_exp <= 2 * topk_count and regular:
            return relay_body(*args, across=across)
        return routed_body(*args)

    return jax.shard_map(
        body,
        mesh=mesh,
        in_specs=(
            P("expert", None),
            P("section", "expert", None),
            P("section", None),
            P("section", "expert", None),
            P("section", "expert", None),
            P("section", "expert", None, None),
            P("section", "expert", None, None),
        ),
        out_specs=P("section", "expert", None),
        check_vma=False,
    )
```

```python
import functools

import jax
import jax.numpy as jnp
from jax import lax
from jax.experimental import pallas as pl
from jax.experimental.pallas import tpu as pltpu
from jax.sharding import PartitionSpec as P

epsilon = 1e-06
LANES = 128
HALF = LANES // 2
CORES = 2
MIB = 1 << 20


def from_behind(value, axis, by):
    peers = lax.axis_size(axis)
    pairs = [(i, i + by) for i in range(peers) if 0 <= i + by < peers]
    return lax.ppermute(value, axis, pairs)


def routed_body(fresh, previous, norm_gain, routes, gate_weights, w_gate_up, w_down):
    devices_exp = lax.axis_size("expert")
    section_id = lax.axis_index("section")
    tok_dev = fresh.shape[0]
    width = fresh.shape[1]
    topk_count = routes.shape[2]
    local_experts = w_gate_up.shape[1]
    hidden_units = w_down.shape[2]
    experts_total = devices_exp * local_experts
    capacity = min(tok_dev, 17 * tok_dev * topk_count // (16 * experts_total))
    total_rows = tok_dev * topk_count
    arrived = from_behind(previous[0], "section", 1)
    arrival = jnp.where(section_id == 0, fresh, arrived)
    wide_input = arrival.astype(jnp.float32)
    scale = lax.rsqrt(jnp.mean(wide_input * wide_input, axis=-1, keepdims=True) + epsilon)
    normed = (wide_input * scale * norm_gain[0][None, :]).astype(jnp.bfloat16)
    flat_ids = routes[0].reshape(-1)
    one_hot = (flat_ids[:, None] == jnp.arange(experts_total, dtype=jnp.int32)[None, :]).astype(
        jnp.int32
    )
    slot_rank = jnp.sum(jnp.cumsum(one_hot, axis=0) * one_hot, axis=1) - 1
    position = flat_ids * capacity + slot_rank
    source_row = (
        jnp.full((experts_total * capacity,), total_rows, jnp.int32)
        .at[position]
        .set(jnp.arange(total_rows, dtype=jnp.int32))
    )
    padded = jnp.concatenate([normed, jnp.zeros((1, width), jnp.bfloat16)], axis=0)
    send_buffer = padded[source_row // topk_count].reshape(
        devices_exp, local_experts, capacity, width
    )
    received = lax.all_to_all(send_buffer, "expert", split_axis=0, concat_axis=0, tiled=True)
    projected = jnp.einsum(
        "secd,edf->secf", received, w_gate_up[0], preferred_element_type=jnp.float32
    )
    hidden = (jax.nn.silu(projected[..., :hidden_units]) * projected[..., hidden_units:]).astype(
        jnp.bfloat16
    )
    returned = lax.all_to_all(
        jnp.einsum("secf,efd->secd", hidden, w_down[0], preferred_element_type=jnp.float32).astype(
            jnp.bfloat16
        ),
        "expert",
        split_axis=0,
        concat_axis=0,
        tiled=True,
    )
    flat_back = returned.reshape(experts_total * capacity, width)
    picked = flat_back[position].reshape(tok_dev, topk_count, width).astype(jnp.float32)
    mixed = jnp.sum(picked * gate_weights[0][:, :, None], axis=1)
    return (wide_input + mixed).astype(jnp.bfloat16)[None]


def normed_rows(rows, gain):
    wide = rows.astype(jnp.float32)
    scale = lax.rsqrt(jnp.mean(wide * wide, axis=-1, keepdims=True) + epsilon)
    return (wide * scale * gain).astype(jnp.bfloat16)


def base_kernel(fresh_ref, gain_ref, routes_ref, gates_ref, rows_ref, coefs_ref, fresh_out_ref, gain_out_ref):
    rows_ref[...] = normed_rows(fresh_ref[...], gain_ref[...])
    shape = coefs_ref.shape[1:]
    expert = lax.broadcasted_iota(jnp.int32, shape, 0)
    weight = jnp.zeros(shape, jnp.float32)
    for k in range(routes_ref.shape[0]):
        weight += jnp.where(routes_ref[k : k + 1, :] == expert, gates_ref[k : k + 1, :], 0.0)
    high = weight.astype(jnp.bfloat16).astype(jnp.float32)
    low = weight - high
    left = lax.broadcasted_iota(jnp.int32, shape, 1) < HALF
    coefs_ref[0] = jnp.where(left, high, pltpu.roll(low, HALF, 1)).astype(jnp.bfloat16)
    coefs_ref[1] = jnp.where(left, pltpu.roll(high, HALF, 1), low).astype(jnp.bfloat16)
    fresh_out_ref[...] = fresh_ref[...]
    gain_out_ref[...] = gain_ref[...]


def base_rows(fresh, gain, routes, gates, experts):
    rows, width = fresh.shape
    vmem = pl.BlockSpec(memory_space=pltpu.VMEM)
    return pl.pallas_call(
        base_kernel,
        out_shape=(
            jax.ShapeDtypeStruct((rows, width), jnp.bfloat16),
            jax.ShapeDtypeStruct((2, experts, rows), jnp.bfloat16),
            jax.ShapeDtypeStruct(fresh.shape, fresh.dtype),
            jax.ShapeDtypeStruct(gain.shape, jnp.float32),
        ),
        in_specs=[vmem] * 4,
        out_specs=(vmem,) * 4,
        compiler_params=pltpu.CompilerParams(vmem_limit_bytes=12 * MIB),
        cost_estimate=pl.CostEstimate(flops=rows * width * 6, bytes_accessed=rows * width * 8, transcendentals=rows),
        name="base_rows",
    )(fresh, gain, routes, gates)


def norm_kernel(section_ref, base_ref, coefs_ref, fresh_ref, arrived_ref, gain_ref, rows_ref, arrival_ref, *, chunk):
    rows, width = arrived_ref.shape
    here = slice(chunk * rows, (chunk + 1) * rows)

    def pack(normed):
        for i in range(width // LANES):
            rows_ref[i * rows : (i + 1) * rows, :] = normed[:, i * LANES : (i + 1) * LANES]

    @pl.when(section_ref[0] == 0)
    def _():
        pack(base_ref[here, :])
        arrival_ref[...] = fresh_ref[here, :]

    @pl.when(section_ref[0] != 0)
    def _():
        pack(normed_rows(arrived_ref[...], gain_ref[...]))
        arrival_ref[...] = arrived_ref[...]

    rows_ref[rows * (width // LANES) :, :] = coefs_ref[chunk]


def norm_rows(section_id, base, coefs, fresh, arrived, gain, chunk):
    rows, width = arrived.shape
    vmem = pl.BlockSpec(memory_space=pltpu.VMEM)
    return pl.pallas_call(
        functools.partial(norm_kernel, chunk=chunk),
        out_shape=(
            jax.ShapeDtypeStruct((rows * (width // LANES) + coefs.shape[1], LANES), jnp.bfloat16),
            jax.ShapeDtypeStruct((rows, width), jnp.bfloat16),
        ),
        in_specs=[pl.BlockSpec(memory_space=pltpu.SMEM)] + [vmem] * 5,
        out_specs=(vmem, vmem),
        compiler_params=pltpu.CompilerParams(vmem_limit_bytes=12 * MIB),
        cost_estimate=pl.CostEstimate(flops=rows * width * 6, bytes_accessed=rows * width * 8, transcendentals=rows),
        name="norm_rows",
    )(section_id, base, coefs, fresh, arrived, gain)


def mlp_kernel(expert_ref, *refs, parts, chained):
    payloads = refs[:parts]
    weights = (refs[parts : parts + 2], refs[parts + 2 : parts + 4])
    refs = refs[parts + 4 + chained :]
    outs = refs[:parts]
    x_ref, coef_ref, hidden_ref = refs[parts:]
    width = x_ref.shape[1]
    hidden = weights[0][1].shape[0]
    line = lax.broadcasted_iota(jnp.int32, (HALF, LANES), 0)
    token = line == lax.broadcasted_iota(jnp.int32, (HALF, LANES), 1) % HALF
    bounds = []
    for part, payload in enumerate(payloads):
        here = slice(part * HALF, (part + 1) * HALF)
        bounds.append(here)
        for i in range(width // LANES):
            x_ref[here, i * LANES : (i + 1) * LANES] = payload[i * HALF : (i + 1) * HALF, :]
        block = payload[HALF * (width // LANES) :, :].astype(jnp.float32)
        expert = lax.broadcasted_iota(jnp.int32, block.shape, 0)
        for which in range(2):
            terms = jnp.sum(jnp.where(expert == expert_ref[0] ^ which, block, 0.0), axis=0, keepdims=True)
            value = jnp.sum(jnp.where(token, terms, 0.0), axis=1, keepdims=True)
            coef_ref[which, here, :] = jnp.broadcast_to(value, (HALF, LANES))
    tile = 256
    for which, (gate_up, _) in enumerate(weights):
        for t in range(0, hidden, tile):
            gate = jnp.dot(x_ref[...], gate_up[:, t : t + tile], preferred_element_type=jnp.float32)
            up = jnp.dot(x_ref[...], gate_up[:, hidden + t : hidden + t + tile], preferred_element_type=jnp.float32)
            value = jax.nn.silu(gate) * up * coef_ref[which][:, :1]
            hidden_ref[:, which * hidden + t : which * hidden + t + tile] = value.astype(jnp.bfloat16)
    tile = 512
    for t in range(0, width, tile):
        total = jnp.zeros((x_ref.shape[0], tile), jnp.float32)
        for which, (_, down) in enumerate(weights):
            rows = hidden_ref[:, which * hidden : (which + 1) * hidden]
            total += jnp.dot(rows, down[:, t : t + tile], preferred_element_type=jnp.float32)
        for here, out in zip(bounds, outs):
            out[:, t : t + tile] = total[here, :]


def expert_rows(expert_id, payloads, own, other, after):
    width = own[0].shape[0]
    hidden = own[1].shape[0]
    rows = HALF * len(payloads)
    vmem = pl.BlockSpec(memory_space=pltpu.VMEM)
    chain = [] if after is None else [after]
    return pl.pallas_call(
        functools.partial(mlp_kernel, parts=len(payloads), chained=len(chain)),
        out_shape=[jax.ShapeDtypeStruct((HALF, width), jnp.float32)] * len(payloads),
        in_specs=[pl.BlockSpec(memory_space=pltpu.SMEM)]
        + [vmem] * (len(payloads) + 4)
        + [pl.BlockSpec(memory_space=pl.ANY)] * len(chain),
        out_specs=[vmem] * len(payloads),
        scratch_shapes=[
            pltpu.VMEM((rows, width), jnp.bfloat16),
            pltpu.VMEM((2, rows, LANES), jnp.float32),
            pltpu.VMEM((rows, 2 * hidden), jnp.bfloat16),
        ],
        compiler_params=pltpu.CompilerParams(vmem_limit_bytes=16 * MIB),
        cost_estimate=pl.CostEstimate(
            flops=2 * rows * width * hidden * 6,
            bytes_accessed=rows * width * 6,
            transcendentals=rows * hidden * 2,
        ),
        name="expert_rows",
    )(expert_id, *payloads, *own, *other, *chain)


def last_kernel(near0_ref, near1_ref, total0_ref, total1_ref, out_ref):
    half = near0_ref.shape[0]
    for start, near_ref, total_ref in ((0, near0_ref, total0_ref), (half, near1_ref, total1_ref)):
        total = near_ref[...] + total_ref[...].astype(jnp.float32)
        out_ref[start : start + half, :] = total.astype(jnp.bfloat16)


def last_rows(nears, totals):
    rows, width = nears[0].shape
    vmem = pl.BlockSpec(memory_space=pltpu.VMEM)
    return pl.pallas_call(
        last_kernel,
        out_shape=jax.ShapeDtypeStruct((2 * rows, width), jnp.bfloat16),
        in_specs=[vmem] * 4,
        out_specs=vmem,
        compiler_params=pltpu.CompilerParams(vmem_limit_bytes=8 * MIB),
        cost_estimate=pl.CostEstimate(flops=2 * rows * width, bytes_accessed=rows * width * 16, transcendentals=0),
        name="last_rows",
    )(*nears, *totals)


def chip_ring(depth, across):
    walk = []
    for z in range(depth):
        xs = list(range(1, across))
        walk += [(z, x) for x in (xs if z % 2 == 0 else xs[::-1])]
    return [z * across + x for z, x in walk + [(z, 0) for z in reversed(range(depth))]]


def relay_body(fresh, previous, norm_gain, routes, gate_weights, w_gate_up, w_down, *, across):
    devices_exp = lax.axis_size("expert")
    section_id = lax.axis_index("section").astype(jnp.int32).reshape(1)
    expert_id = lax.axis_index("expert").astype(jnp.int32).reshape(1)
    rows = fresh.shape[0]
    half = HALF
    chips = devices_exp // CORES
    ring = chip_ring(chips // across, across)
    links = list(zip(ring, ring[1:] + ring[:1]))
    up = [(a * CORES + c, b * CORES + c) for a, b in links for c in range(CORES)]
    down = [(b, a) for a, b in up]
    swap = [(i, i ^ 1) for i in range(devices_exp)]

    def move(value, pairs):
        return lax.ppermute(value, "expert", pairs)

    cuts = [slice(0, half), slice(half, rows)]
    own = (w_gate_up[0, 0], w_down[0, 0])
    swapped = lax.optimization_barrier((*own, section_id, expert_id))[:2]
    other = tuple(move(w, swap) for w in swapped)
    base, coefs, fresh, gain = base_rows(fresh, norm_gain, routes[0].T, gate_weights[0].T, devices_exp)
    arrived = [from_behind(previous[0, cut], "section", 1) for cut in cuts]
    packed, arrival = zip(*(norm_rows(section_id, base, coefs, fresh, arrived[c], gain, c) for c in range(2)))
    packed = list(packed)

    hops = chips // 2
    ups = [packed] + [[None, None] for _ in range(hops)]
    downs = [packed] + [[None, None] for _ in range(hops)]

    def pass_on(s, c, after):
        rising, falling = lax.optimization_barrier((ups[s][c], downs[s][c], after))[:2]
        if s < hops - 1 or c == 0:
            ups[s + 1][c] = move(rising, up)
        if s < hops - 1 or c == 1:
            downs[s + 1][c] = move(falling, down)

    last = None

    def mlp(payloads):
        nonlocal last
        sums = expert_rows(expert_id, payloads, own, other, last)
        last = sums[0]
        return sums

    to_down, to_up = {}, {}
    pass_on(0, 0, None)
    pass_on(0, 1, other)
    for s in range(1, hops):
        for c in range(2):
            pass_on(s, c, last)
            to_down[s, c], to_up[s, c] = mlp([ups[s][c], downs[s][c]])
    to_up[hops, 0], to_down[hops, 1] = mlp([ups[hops][0], downs[hops][1]])
    own_sums = mlp(packed)

    def send_on(flow, place, total, after):
        terms, c, pairs = flow
        if total is None:
            total = terms[place, c]
        else:
            carried = lax.optimization_barrier((total, after))[0]
            total = terms[place, c] + carried.astype(jnp.float32)
        total = total.astype(jnp.bfloat16)
        return total, move(total, pairs)

    short = [(to_down, 0, down), (to_up, 1, up)]
    long = [(to_up, 0, up), (to_down, 1, down)]
    short_totals = [send_on(flow, hops - 1, None, None)[1] for flow in short]
    long_totals = [send_on(flow, hops, None, None)[1] for flow in long]
    after = to_up[hops, 0]
    for s in reversed(range(1, hops)):
        if s > 1:
            sent, short_totals = zip(*(send_on(f, s - 1, t, after) for f, t in zip(short, short_totals)))
        sent, long_totals = zip(*(send_on(f, s, t, sent) for f, t in zip(long, long_totals)))
        after = sent

    nears = [
        arrival[c].astype(jnp.float32) + (own_sums[c] + short_totals[c].astype(jnp.float32)) for c in range(2)
    ]
    nears = lax.optimization_barrier(nears)
    return last_rows(nears, long_totals)[None]


def solution(mesh):
    across = mesh.shape["section"]
    devices_exp = mesh.shape["expert"]

    def body(*args):
        topk_count, local_experts = args[3].shape[2], args[5].shape[1]
        regular = devices_exp % (2 * CORES * across) == 0 and devices_exp % 16 == 0 and args[0].shape[0] == LANES
        if local_experts == 1 and devices_exp <= 2 * topk_count and regular:
            return relay_body(*args, across=across)
        return routed_body(*args)

    return jax.shard_map(
        body,
        mesh=mesh,
        in_specs=(
            P("expert", None),
            P("section", "expert", None),
            P("section", None),
            P("section", "expert", None),
            P("section", "expert", None),
            P("section", "expert", None, None),
            P("section", "expert", None, None),
        ),
        out_specs=P("section", "expert", None),
        check_vma=False,
    )
```

```python
import functools

import jax
import jax.numpy as jnp
from jax import lax
from jax.experimental import pallas as pl
from jax.experimental.pallas import tpu as pltpu
from jax.sharding import PartitionSpec as P

epsilon = 1e-06
LANES = 128
HALF = LANES // 2
CORES = 2
MIB = 1 << 20


def from_behind(value, axis, by):
    peers = lax.axis_size(axis)
    pairs = [(i, i + by) for i in range(peers) if 0 <= i + by < peers]
    return lax.ppermute(value, axis, pairs)


def routed_body(fresh, previous, norm_gain, routes, gate_weights, w_gate_up, w_down):
    devices_exp = lax.axis_size("expert")
    section_id = lax.axis_index("section")
    tok_dev = fresh.shape[0]
    width = fresh.shape[1]
    topk_count = routes.shape[2]
    local_experts = w_gate_up.shape[1]
    hidden_units = w_down.shape[2]
    experts_total = devices_exp * local_experts
    capacity = min(tok_dev, 17 * tok_dev * topk_count // (16 * experts_total))
    total_rows = tok_dev * topk_count
    arrived = from_behind(previous[0], "section", 1)
    arrival = jnp.where(section_id == 0, fresh, arrived)
    wide_input = arrival.astype(jnp.float32)
    scale = lax.rsqrt(jnp.mean(wide_input * wide_input, axis=-1, keepdims=True) + epsilon)
    normed = (wide_input * scale * norm_gain[0][None, :]).astype(jnp.bfloat16)
    flat_ids = routes[0].reshape(-1)
    one_hot = (flat_ids[:, None] == jnp.arange(experts_total, dtype=jnp.int32)[None, :]).astype(
        jnp.int32
    )
    slot_rank = jnp.sum(jnp.cumsum(one_hot, axis=0) * one_hot, axis=1) - 1
    position = flat_ids * capacity + slot_rank
    source_row = (
        jnp.full((experts_total * capacity,), total_rows, jnp.int32)
        .at[position]
        .set(jnp.arange(total_rows, dtype=jnp.int32))
    )
    padded = jnp.concatenate([normed, jnp.zeros((1, width), jnp.bfloat16)], axis=0)
    send_buffer = padded[source_row // topk_count].reshape(
        devices_exp, local_experts, capacity, width
    )
    received = lax.all_to_all(send_buffer, "expert", split_axis=0, concat_axis=0, tiled=True)
    projected = jnp.einsum(
        "secd,edf->secf", received, w_gate_up[0], preferred_element_type=jnp.float32
    )
    hidden = (jax.nn.silu(projected[..., :hidden_units]) * projected[..., hidden_units:]).astype(
        jnp.bfloat16
    )
    returned = lax.all_to_all(
        jnp.einsum("secf,efd->secd", hidden, w_down[0], preferred_element_type=jnp.float32).astype(
            jnp.bfloat16
        ),
        "expert",
        split_axis=0,
        concat_axis=0,
        tiled=True,
    )
    flat_back = returned.reshape(experts_total * capacity, width)
    picked = flat_back[position].reshape(tok_dev, topk_count, width).astype(jnp.float32)
    mixed = jnp.sum(picked * gate_weights[0][:, :, None], axis=1)
    return (wide_input + mixed).astype(jnp.bfloat16)[None]


def normed_rows(rows, gain):
    wide = rows.astype(jnp.float32)
    scale = lax.rsqrt(jnp.mean(wide * wide, axis=-1, keepdims=True) + epsilon)
    return (wide * scale * gain).astype(jnp.bfloat16)


def base_kernel(fresh_ref, gain_ref, routes_ref, gates_ref, rows_ref, coefs_ref, fresh_out_ref, gain_out_ref):
    rows_ref[...] = normed_rows(fresh_ref[...], gain_ref[...])
    shape = coefs_ref.shape[1:]
    expert = lax.broadcasted_iota(jnp.int32, shape, 0)
    weight = jnp.zeros(shape, jnp.float32)
    for k in range(routes_ref.shape[0]):
        weight += jnp.where(routes_ref[k : k + 1, :] == expert, gates_ref[k : k + 1, :], 0.0)
    high = weight.astype(jnp.bfloat16).astype(jnp.float32)
    low = weight - high
    left = lax.broadcasted_iota(jnp.int32, shape, 1) < HALF
    coefs_ref[0] = jnp.where(left, high, pltpu.roll(low, HALF, 1)).astype(jnp.bfloat16)
    coefs_ref[1] = jnp.where(left, pltpu.roll(high, HALF, 1), low).astype(jnp.bfloat16)
    fresh_out_ref[...] = fresh_ref[...]
    gain_out_ref[...] = gain_ref[...]


def base_rows(fresh, gain, routes, gates, experts):
    rows, width = fresh.shape
    vmem = pl.BlockSpec(memory_space=pltpu.VMEM)
    return pl.pallas_call(
        base_kernel,
        out_shape=(
            jax.ShapeDtypeStruct((rows, width), jnp.bfloat16),
            jax.ShapeDtypeStruct((2, experts, rows), jnp.bfloat16),
            jax.ShapeDtypeStruct(fresh.shape, fresh.dtype),
            jax.ShapeDtypeStruct(gain.shape, jnp.float32),
        ),
        in_specs=[vmem] * 4,
        out_specs=(vmem,) * 4,
        compiler_params=pltpu.CompilerParams(vmem_limit_bytes=12 * MIB),
        cost_estimate=pl.CostEstimate(flops=rows * width * 6, bytes_accessed=rows * width * 8, transcendentals=rows),
        name="base_rows",
    )(fresh, gain, routes, gates)


def norm_kernel(section_ref, base_ref, coefs_ref, fresh_ref, arrived_ref, gain_ref, rows_ref, arrival_ref, *, chunk):
    rows, width = arrived_ref.shape
    here = slice(chunk * rows, (chunk + 1) * rows)

    def pack(normed):
        for i in range(width // LANES):
            rows_ref[i * rows : (i + 1) * rows, :] = normed[:, i * LANES : (i + 1) * LANES]

    @pl.when(section_ref[0] == 0)
    def _():
        pack(base_ref[here, :])
        arrival_ref[...] = fresh_ref[here, :]

    @pl.when(section_ref[0] != 0)
    def _():
        pack(normed_rows(arrived_ref[...], gain_ref[...]))
        arrival_ref[...] = arrived_ref[...]

    rows_ref[rows * (width // LANES) :, :] = coefs_ref[chunk]


def norm_rows(section_id, base, coefs, fresh, arrived, gain, chunk):
    rows, width = arrived.shape
    vmem = pl.BlockSpec(memory_space=pltpu.VMEM)
    return pl.pallas_call(
        functools.partial(norm_kernel, chunk=chunk),
        out_shape=(
            jax.ShapeDtypeStruct((rows * (width // LANES) + coefs.shape[1], LANES), jnp.bfloat16),
            jax.ShapeDtypeStruct((rows, width), jnp.bfloat16),
        ),
        in_specs=[pl.BlockSpec(memory_space=pltpu.SMEM)] + [vmem] * 5,
        out_specs=(vmem, vmem),
        compiler_params=pltpu.CompilerParams(vmem_limit_bytes=12 * MIB),
        cost_estimate=pl.CostEstimate(flops=rows * width * 6, bytes_accessed=rows * width * 8, transcendentals=rows),
        name="norm_rows",
    )(section_id, base, coefs, fresh, arrived, gain)


def mlp_kernel(expert_ref, *refs, parts, chained):
    payloads = refs[:parts]
    weights = (refs[parts : parts + 2], refs[parts + 2 : parts + 4])
    refs = refs[parts + 4 + chained :]
    outs = refs[:parts]
    x_ref, coef_ref, hidden_ref = refs[parts:]
    width = x_ref.shape[1]
    hidden = weights[0][1].shape[0]
    line = lax.broadcasted_iota(jnp.int32, (HALF, LANES), 0)
    token = line == lax.broadcasted_iota(jnp.int32, (HALF, LANES), 1) % HALF
    bounds = []
    for part, payload in enumerate(payloads):
        here = slice(part * HALF, (part + 1) * HALF)
        bounds.append(here)
        for i in range(width // LANES):
            x_ref[here, i * LANES : (i + 1) * LANES] = payload[i * HALF : (i + 1) * HALF, :]
        block = payload[HALF * (width // LANES) :, :].astype(jnp.float32)
        expert = lax.broadcasted_iota(jnp.int32, block.shape, 0)
        for which in range(2):
            terms = jnp.sum(jnp.where(expert == expert_ref[0] ^ which, block, 0.0), axis=0, keepdims=True)
            value = jnp.sum(jnp.where(token, terms, 0.0), axis=1, keepdims=True)
            coef_ref[which, here, :] = jnp.broadcast_to(value, (HALF, LANES))
    tile = 256
    for which, (gate_up, _) in enumerate(weights):
        for t in range(0, hidden, tile):
            gate = jnp.dot(x_ref[...], gate_up[:, t : t + tile], preferred_element_type=jnp.float32)
            up = jnp.dot(x_ref[...], gate_up[:, hidden + t : hidden + t + tile], preferred_element_type=jnp.float32)
            value = jax.nn.silu(gate) * up * coef_ref[which][:, :1]
            hidden_ref[:, which * hidden + t : which * hidden + t + tile] = value.astype(jnp.bfloat16)
    tile = 512
    for t in range(0, width, tile):
        total = jnp.zeros((x_ref.shape[0], tile), jnp.float32)
        for which, (_, down) in enumerate(weights):
            rows = hidden_ref[:, which * hidden : (which + 1) * hidden]
            total += jnp.dot(rows, down[:, t : t + tile], preferred_element_type=jnp.float32)
        for here, out in zip(bounds, outs):
            out[:, t : t + tile] = total[here, :]


def expert_rows(expert_id, payloads, own, other, after):
    width = own[0].shape[0]
    hidden = own[1].shape[0]
    rows = HALF * len(payloads)
    vmem = pl.BlockSpec(memory_space=pltpu.VMEM)
    chain = [] if after is None else [after]
    return pl.pallas_call(
        functools.partial(mlp_kernel, parts=len(payloads), chained=len(chain)),
        out_shape=[jax.ShapeDtypeStruct((HALF, width), jnp.float32)] * len(payloads),
        in_specs=[pl.BlockSpec(memory_space=pltpu.SMEM)]
        + [vmem] * (len(payloads) + 4)
        + [pl.BlockSpec(memory_space=pl.ANY)] * len(chain),
        out_specs=[vmem] * len(payloads),
        scratch_shapes=[
            pltpu.VMEM((rows, width), jnp.bfloat16),
            pltpu.VMEM((2, rows, LANES), jnp.float32),
            pltpu.VMEM((rows, 2 * hidden), jnp.bfloat16),
        ],
        compiler_params=pltpu.CompilerParams(vmem_limit_bytes=16 * MIB),
        cost_estimate=pl.CostEstimate(
            flops=2 * rows * width * hidden * 6,
            bytes_accessed=rows * width * 6,
            transcendentals=rows * hidden * 2,
        ),
        name="expert_rows",
    )(expert_id, *payloads, *own, *other, *chain)


def last_kernel(near0_ref, near1_ref, total0_ref, total1_ref, out_ref):
    half = near0_ref.shape[0]
    for start, near_ref, total_ref in ((0, near0_ref, total0_ref), (half, near1_ref, total1_ref)):
        total = near_ref[...] + total_ref[...].astype(jnp.float32)
        out_ref[start : start + half, :] = total.astype(jnp.bfloat16)


def last_rows(nears, totals):
    rows, width = nears[0].shape
    vmem = pl.BlockSpec(memory_space=pltpu.VMEM)
    return pl.pallas_call(
        last_kernel,
        out_shape=jax.ShapeDtypeStruct((2 * rows, width), jnp.bfloat16),
        in_specs=[vmem] * 4,
        out_specs=vmem,
        compiler_params=pltpu.CompilerParams(vmem_limit_bytes=8 * MIB),
        cost_estimate=pl.CostEstimate(flops=2 * rows * width, bytes_accessed=rows * width * 16, transcendentals=0),
        name="last_rows",
    )(*nears, *totals)


def chip_ring(depth, across):
    walk = []
    for z in range(depth):
        xs = list(range(1, across))
        walk += [(z, x) for x in (xs if z % 2 == 0 else xs[::-1])]
    return [z * across + x for z, x in walk + [(z, 0) for z in reversed(range(depth))]]


def relay_body(fresh, previous, norm_gain, routes, gate_weights, w_gate_up, w_down, *, across):
    devices_exp = lax.axis_size("expert")
    section_id = lax.axis_index("section").astype(jnp.int32).reshape(1)
    expert_id = lax.axis_index("expert").astype(jnp.int32).reshape(1)
    rows = fresh.shape[0]
    half = HALF
    chips = devices_exp // CORES
    ring = chip_ring(chips // across, across)
    links = list(zip(ring, ring[1:] + ring[:1]))
    up = [(a * CORES + c, b * CORES + c) for a, b in links for c in range(CORES)]
    down = [(b, a) for a, b in up]
    swap = [(i, i ^ 1) for i in range(devices_exp)]

    def move(value, pairs):
        return lax.ppermute(value, "expert", pairs)

    cuts = [slice(0, half), slice(half, rows)]
    own = (w_gate_up[0, 0], w_down[0, 0])
    swapped = lax.optimization_barrier((*own, section_id, expert_id))[:2]
    other = tuple(move(w, swap) for w in swapped)
    base, coefs, fresh, gain = base_rows(fresh, norm_gain, routes[0].T, gate_weights[0].T, devices_exp)
    arrived = [from_behind(previous[0, cut], "section", 1) for cut in cuts]
    packed, arrival = zip(*(norm_rows(section_id, base, coefs, fresh, arrived[c], gain, c) for c in range(2)))
    packed = list(packed)

    hops = chips // 2
    ups = [packed] + [[None, None] for _ in range(hops)]
    downs = [packed] + [[None, None] for _ in range(hops)]

    def pass_on(s, c, after):
        rising, falling = lax.optimization_barrier((ups[s][c], downs[s][c], after))[:2]
        if s < hops - 1 or c == 0:
            ups[s + 1][c] = move(rising, up)
        if s < hops - 1 or c == 1:
            downs[s + 1][c] = move(falling, down)

    last = None

    def mlp(payloads):
        nonlocal last
        sums = expert_rows(expert_id, payloads, own, other, last)
        last = sums[0]
        return sums

    to_down, to_up = {}, {}
    pass_on(0, 0, None)
    pass_on(0, 1, other)
    for s in range(1, hops):
        for c in range(2):
            pass_on(s, c, last)
            to_down[s, c], to_up[s, c] = mlp([ups[s][c], downs[s][c]])
    to_up[hops, 0], to_down[hops, 1] = mlp([ups[hops][0], downs[hops][1]])
    own_sums = mlp(packed)

    def send_on(flow, place, total, after):
        terms, c, pairs = flow
        if total is None:
            total = terms[place, c]
        else:
            carried = lax.optimization_barrier((total, after))[0]
            total = terms[place, c] + carried.astype(jnp.float32)
        total = total.astype(jnp.bfloat16)
        return total, move(total, pairs)

    short = [(to_down, 0, down), (to_up, 1, up)]
    long = [(to_up, 0, up), (to_down, 1, down)]
    short_totals = [send_on(flow, hops - 1, None, None)[1] for flow in short]
    long_totals = [send_on(flow, hops, None, None)[1] for flow in long]
    sent = to_up[hops, 0]
    for s in reversed(range(1, hops)):
        order = [(short, s - 1), (long, s)] if s == hops - 1 else [(long, s), (short, s - 1)]
        for flows, place in order:
            if place == 0:
                continue
            totals = short_totals if flows is short else long_totals
            sent, totals = zip(*(send_on(flow, place, total, sent) for flow, total in zip(flows, totals)))
            if flows is short:
                short_totals = totals
            else:
                long_totals = totals

    nears = [
        arrival[c].astype(jnp.float32) + (own_sums[c] + short_totals[c].astype(jnp.float32)) for c in range(2)
    ]
    nears = lax.optimization_barrier(nears)
    return last_rows(nears, long_totals)[None]


def solution(mesh):
    across = mesh.shape["section"]
    devices_exp = mesh.shape["expert"]

    def body(*args):
        topk_count, local_experts = args[3].shape[2], args[5].shape[1]
        regular = devices_exp % (2 * CORES * across) == 0 and devices_exp % 16 == 0 and args[0].shape[0] == LANES
        if local_experts == 1 and devices_exp <= 2 * topk_count and regular:
            return relay_body(*args, across=across)
        return routed_body(*args)

    return jax.shard_map(
        body,
        mesh=mesh,
        in_specs=(
            P("expert", None),
            P("section", "expert", None),
            P("section", None),
            P("section", "expert", None),
            P("section", "expert", None),
            P("section", "expert", None, None),
            P("section", "expert", None, None),
        ),
        out_specs=P("section", "expert", None),
        check_vma=False,
    )
```

```python
import functools

import jax
import jax.numpy as jnp
from jax import lax
from jax.experimental import pallas as pl
from jax.experimental.pallas import tpu as pltpu
from jax.sharding import PartitionSpec as P

epsilon = 1e-06
LANES = 128
HALF = LANES // 2
CORES = 2
MIB = 1 << 20


def from_behind(value, axis, by):
    peers = lax.axis_size(axis)
    pairs = [(i, i + by) for i in range(peers) if 0 <= i + by < peers]
    return lax.ppermute(value, axis, pairs)


def routed_body(fresh, previous, norm_gain, routes, gate_weights, w_gate_up, w_down):
    devices_exp = lax.axis_size("expert")
    section_id = lax.axis_index("section")
    tok_dev = fresh.shape[0]
    width = fresh.shape[1]
    topk_count = routes.shape[2]
    local_experts = w_gate_up.shape[1]
    hidden_units = w_down.shape[2]
    experts_total = devices_exp * local_experts
    capacity = min(tok_dev, 17 * tok_dev * topk_count // (16 * experts_total))
    total_rows = tok_dev * topk_count
    arrived = from_behind(previous[0], "section", 1)
    arrival = jnp.where(section_id == 0, fresh, arrived)
    wide_input = arrival.astype(jnp.float32)
    scale = lax.rsqrt(jnp.mean(wide_input * wide_input, axis=-1, keepdims=True) + epsilon)
    normed = (wide_input * scale * norm_gain[0][None, :]).astype(jnp.bfloat16)
    flat_ids = routes[0].reshape(-1)
    one_hot = (flat_ids[:, None] == jnp.arange(experts_total, dtype=jnp.int32)[None, :]).astype(
        jnp.int32
    )
    slot_rank = jnp.sum(jnp.cumsum(one_hot, axis=0) * one_hot, axis=1) - 1
    position = flat_ids * capacity + slot_rank
    source_row = (
        jnp.full((experts_total * capacity,), total_rows, jnp.int32)
        .at[position]
        .set(jnp.arange(total_rows, dtype=jnp.int32))
    )
    padded = jnp.concatenate([normed, jnp.zeros((1, width), jnp.bfloat16)], axis=0)
    send_buffer = padded[source_row // topk_count].reshape(
        devices_exp, local_experts, capacity, width
    )
    received = lax.all_to_all(send_buffer, "expert", split_axis=0, concat_axis=0, tiled=True)
    projected = jnp.einsum(
        "secd,edf->secf", received, w_gate_up[0], preferred_element_type=jnp.float32
    )
    hidden = (jax.nn.silu(projected[..., :hidden_units]) * projected[..., hidden_units:]).astype(
        jnp.bfloat16
    )
    returned = lax.all_to_all(
        jnp.einsum("secf,efd->secd", hidden, w_down[0], preferred_element_type=jnp.float32).astype(
            jnp.bfloat16
        ),
        "expert",
        split_axis=0,
        concat_axis=0,
        tiled=True,
    )
    flat_back = returned.reshape(experts_total * capacity, width)
    picked = flat_back[position].reshape(tok_dev, topk_count, width).astype(jnp.float32)
    mixed = jnp.sum(picked * gate_weights[0][:, :, None], axis=1)
    return (wide_input + mixed).astype(jnp.bfloat16)[None]


def normed_rows(rows, gain):
    wide = rows.astype(jnp.float32)
    scale = lax.rsqrt(jnp.mean(wide * wide, axis=-1, keepdims=True) + epsilon)
    return (wide * scale * gain).astype(jnp.bfloat16)


def base_kernel(fresh_ref, gain_ref, routes_ref, gates_ref, rows_ref, coefs_ref, fresh_out_ref, gain_out_ref):
    rows_ref[...] = normed_rows(fresh_ref[...], gain_ref[...])
    shape = coefs_ref.shape[1:]
    expert = lax.broadcasted_iota(jnp.int32, shape, 0)
    weight = jnp.zeros(shape, jnp.float32)
    for k in range(routes_ref.shape[0]):
        weight += jnp.where(routes_ref[k : k + 1, :] == expert, gates_ref[k : k + 1, :], 0.0)
    high = weight.astype(jnp.bfloat16).astype(jnp.float32)
    low = weight - high
    left = lax.broadcasted_iota(jnp.int32, shape, 1) < HALF
    coefs_ref[0] = jnp.where(left, high, pltpu.roll(low, HALF, 1)).astype(jnp.bfloat16)
    coefs_ref[1] = jnp.where(left, pltpu.roll(high, HALF, 1), low).astype(jnp.bfloat16)
    fresh_out_ref[...] = fresh_ref[...]
    gain_out_ref[...] = gain_ref[...]


def base_rows(fresh, gain, routes, gates, experts):
    rows, width = fresh.shape
    vmem = pl.BlockSpec(memory_space=pltpu.VMEM)
    return pl.pallas_call(
        base_kernel,
        out_shape=(
            jax.ShapeDtypeStruct((rows, width), jnp.bfloat16),
            jax.ShapeDtypeStruct((2, experts, rows), jnp.bfloat16),
            jax.ShapeDtypeStruct(fresh.shape, fresh.dtype),
            jax.ShapeDtypeStruct(gain.shape, jnp.float32),
        ),
        in_specs=[vmem] * 4,
        out_specs=(vmem,) * 4,
        compiler_params=pltpu.CompilerParams(vmem_limit_bytes=12 * MIB),
        cost_estimate=pl.CostEstimate(flops=rows * width * 6, bytes_accessed=rows * width * 8, transcendentals=rows),
        name="base_rows",
    )(fresh, gain, routes, gates)


def norm_kernel(section_ref, base_ref, coefs_ref, fresh_ref, arrived_ref, gain_ref, rows_ref, arrival_ref, *, chunk):
    rows, width = arrived_ref.shape
    here = slice(chunk * rows, (chunk + 1) * rows)

    def pack(normed):
        for i in range(width // LANES):
            rows_ref[i * rows : (i + 1) * rows, :] = normed[:, i * LANES : (i + 1) * LANES]

    @pl.when(section_ref[0] == 0)
    def _():
        pack(base_ref[here, :])
        arrival_ref[...] = fresh_ref[here, :]

    @pl.when(section_ref[0] != 0)
    def _():
        pack(normed_rows(arrived_ref[...], gain_ref[...]))
        arrival_ref[...] = arrived_ref[...]

    rows_ref[rows * (width // LANES) :, :] = coefs_ref[chunk]


def norm_rows(section_id, base, coefs, fresh, arrived, gain, chunk):
    rows, width = arrived.shape
    vmem = pl.BlockSpec(memory_space=pltpu.VMEM)
    return pl.pallas_call(
        functools.partial(norm_kernel, chunk=chunk),
        out_shape=(
            jax.ShapeDtypeStruct((rows * (width // LANES) + coefs.shape[1], LANES), jnp.bfloat16),
            jax.ShapeDtypeStruct((rows, width), jnp.bfloat16),
        ),
        in_specs=[pl.BlockSpec(memory_space=pltpu.SMEM)] + [vmem] * 5,
        out_specs=(vmem, vmem),
        compiler_params=pltpu.CompilerParams(vmem_limit_bytes=12 * MIB),
        cost_estimate=pl.CostEstimate(flops=rows * width * 6, bytes_accessed=rows * width * 8, transcendentals=rows),
        name="norm_rows",
    )(section_id, base, coefs, fresh, arrived, gain)


def mlp_kernel(expert_ref, *refs, parts, adds, chained):
    payloads = refs[:parts]
    weights = (refs[parts : parts + 2], refs[parts + 2 : parts + 4])
    refs = refs[parts + 4 :]
    terms, totals = refs[:adds], refs[adds : 2 * adds]
    refs = refs[2 * adds + chained :]
    outs, added = refs[:parts], refs[parts : parts + adds]
    x_ref, coef_ref, hidden_ref = refs[parts + adds :]
    for term, total, result in zip(terms, totals, added):
        result[...] = (term[...] + total[...].astype(jnp.float32)).astype(jnp.bfloat16)
    width = x_ref.shape[1]
    hidden = weights[0][1].shape[0]
    line = lax.broadcasted_iota(jnp.int32, (HALF, LANES), 0)
    token = line == lax.broadcasted_iota(jnp.int32, (HALF, LANES), 1) % HALF
    bounds = []
    for part, payload in enumerate(payloads):
        here = slice(part * HALF, (part + 1) * HALF)
        bounds.append(here)
        for i in range(width // LANES):
            x_ref[here, i * LANES : (i + 1) * LANES] = payload[i * HALF : (i + 1) * HALF, :]
        block = payload[HALF * (width // LANES) :, :].astype(jnp.float32)
        expert = lax.broadcasted_iota(jnp.int32, block.shape, 0)
        for which in range(2):
            terms = jnp.sum(jnp.where(expert == expert_ref[0] ^ which, block, 0.0), axis=0, keepdims=True)
            value = jnp.sum(jnp.where(token, terms, 0.0), axis=1, keepdims=True)
            coef_ref[which, here, :] = jnp.broadcast_to(value, (HALF, LANES))
    tile = 256
    for which, (gate_up, _) in enumerate(weights):
        for t in range(0, hidden, tile):
            gate = jnp.dot(x_ref[...], gate_up[:, t : t + tile], preferred_element_type=jnp.float32)
            up = jnp.dot(x_ref[...], gate_up[:, hidden + t : hidden + t + tile], preferred_element_type=jnp.float32)
            value = jax.nn.silu(gate) * up * coef_ref[which][:, :1]
            hidden_ref[:, which * hidden + t : which * hidden + t + tile] = value.astype(jnp.bfloat16)
    tile = 512
    for t in range(0, width, tile):
        total = jnp.zeros((x_ref.shape[0], tile), jnp.float32)
        for which, (_, down) in enumerate(weights):
            rows = hidden_ref[:, which * hidden : (which + 1) * hidden]
            total += jnp.dot(rows, down[:, t : t + tile], preferred_element_type=jnp.float32)
        for here, out in zip(bounds, outs):
            out[:, t : t + tile] = total[here, :]


def expert_rows(expert_id, payloads, own, other, after, terms=(), totals=()):
    width = own[0].shape[0]
    hidden = own[1].shape[0]
    rows = HALF * len(payloads)
    vmem = pl.BlockSpec(memory_space=pltpu.VMEM)
    chain = [] if after is None else [after]
    return pl.pallas_call(
        functools.partial(mlp_kernel, parts=len(payloads), adds=len(terms), chained=len(chain)),
        out_shape=[jax.ShapeDtypeStruct((HALF, width), jnp.float32)] * len(payloads)
        + [jax.ShapeDtypeStruct((HALF, width), jnp.bfloat16)] * len(terms),
        in_specs=[pl.BlockSpec(memory_space=pltpu.SMEM)]
        + [vmem] * (len(payloads) + 4 + 2 * len(terms))
        + [pl.BlockSpec(memory_space=pl.ANY)] * len(chain),
        out_specs=[vmem] * (len(payloads) + len(terms)),
        scratch_shapes=[
            pltpu.VMEM((rows, width), jnp.bfloat16),
            pltpu.VMEM((2, rows, LANES), jnp.float32),
            pltpu.VMEM((rows, 2 * hidden), jnp.bfloat16),
        ],
        compiler_params=pltpu.CompilerParams(vmem_limit_bytes=16 * MIB),
        cost_estimate=pl.CostEstimate(
            flops=2 * rows * width * hidden * 6,
            bytes_accessed=rows * width * 6,
            transcendentals=rows * hidden * 2,
        ),
        name="expert_rows",
    )(expert_id, *payloads, *own, *other, *terms, *totals, *chain)


def last_kernel(near0_ref, near1_ref, total0_ref, total1_ref, out_ref):
    half = near0_ref.shape[0]
    for start, near_ref, total_ref in ((0, near0_ref, total0_ref), (half, near1_ref, total1_ref)):
        total = near_ref[...] + total_ref[...].astype(jnp.float32)
        out_ref[start : start + half, :] = total.astype(jnp.bfloat16)


def last_rows(nears, totals):
    rows, width = nears[0].shape
    vmem = pl.BlockSpec(memory_space=pltpu.VMEM)
    return pl.pallas_call(
        last_kernel,
        out_shape=jax.ShapeDtypeStruct((2 * rows, width), jnp.bfloat16),
        in_specs=[vmem] * 4,
        out_specs=vmem,
        compiler_params=pltpu.CompilerParams(vmem_limit_bytes=8 * MIB),
        cost_estimate=pl.CostEstimate(flops=2 * rows * width, bytes_accessed=rows * width * 16, transcendentals=0),
        name="last_rows",
    )(*nears, *totals)


def chip_ring(depth, across):
    walk = []
    for z in range(depth):
        xs = list(range(1, across))
        walk += [(z, x) for x in (xs if z % 2 == 0 else xs[::-1])]
    return [z * across + x for z, x in walk + [(z, 0) for z in reversed(range(depth))]]


def relay_body(fresh, previous, norm_gain, routes, gate_weights, w_gate_up, w_down, *, across):
    devices_exp = lax.axis_size("expert")
    section_id = lax.axis_index("section").astype(jnp.int32).reshape(1)
    expert_id = lax.axis_index("expert").astype(jnp.int32).reshape(1)
    rows = fresh.shape[0]
    half = HALF
    chips = devices_exp // CORES
    ring = chip_ring(chips // across, across)
    links = list(zip(ring, ring[1:] + ring[:1]))
    up = [(a * CORES + c, b * CORES + c) for a, b in links for c in range(CORES)]
    down = [(b, a) for a, b in up]
    swap = [(i, i ^ 1) for i in range(devices_exp)]

    def move(value, pairs):
        return lax.ppermute(value, "expert", pairs)

    cuts = [slice(0, half), slice(half, rows)]
    own = (w_gate_up[0, 0], w_down[0, 0])
    swapped = lax.optimization_barrier((*own, section_id, expert_id))[:2]
    other = tuple(move(w, swap) for w in swapped)
    base, coefs, fresh, gain = base_rows(fresh, norm_gain, routes[0].T, gate_weights[0].T, devices_exp)
    arrived = [from_behind(previous[0, cut], "section", 1) for cut in cuts]
    packed, arrival = zip(*(norm_rows(section_id, base, coefs, fresh, arrived[c], gain, c) for c in range(2)))
    packed = list(packed)

    hops = chips // 2
    ups = [packed] + [[None, None] for _ in range(hops)]
    downs = [packed] + [[None, None] for _ in range(hops)]

    def pass_on(s, c, after):
        rising, falling = lax.optimization_barrier((ups[s][c], downs[s][c], after))[:2]
        if s < hops - 1 or c == 0:
            ups[s + 1][c] = move(rising, up)
        if s < hops - 1 or c == 1:
            downs[s + 1][c] = move(falling, down)

    last = None

    def mlp(payloads, terms=(), totals=()):
        nonlocal last
        sums = expert_rows(expert_id, payloads, own, other, last, terms, totals)
        last = sums[0]
        return sums

    to_down, to_up = {}, {}
    pass_on(0, 0, None)
    pass_on(0, 1, other)
    for s in range(1, hops):
        for c in range(2):
            pass_on(s, c, last)
            to_down[s, c], to_up[s, c] = mlp([ups[s][c], downs[s][c]])
    to_up[hops, 0], to_down[hops, 1] = mlp([ups[hops][0], downs[hops][1]])

    def send_on(flow, place, total, after):
        terms, c, pairs = flow
        if total is None:
            total = terms[place, c]
        else:
            carried = lax.optimization_barrier((total, after))[0]
            total = terms[place, c] + carried.astype(jnp.float32)
        total = total.astype(jnp.bfloat16)
        return total, move(total, pairs)

    short = [(to_down, 0, down), (to_up, 1, up)]
    long = [(to_up, 0, up), (to_down, 1, down)]
    short_totals = [send_on(flow, hops - 1, None, None)[1] for flow in short]
    long_totals = [send_on(flow, hops, None, None)[1] for flow in long]
    *own_sums, down_sum, up_sum = mlp(packed, [f[0][hops - 2, f[1]] for f in short], short_totals)
    short_totals = [move(total, flow[2]) for total, flow in zip((down_sum, up_sum), short)]
    after = None
    for s in reversed(range(1, hops)):
        if 1 < s < hops - 1:
            after, short_totals = zip(*(send_on(f, s - 1, t, after) for f, t in zip(short, short_totals)))
        after, long_totals = zip(*(send_on(f, s, t, after) for f, t in zip(long, long_totals)))

    nears = [
        arrival[c].astype(jnp.float32) + (own_sums[c] + short_totals[c].astype(jnp.float32)) for c in range(2)
    ]
    nears = lax.optimization_barrier(nears)
    return last_rows(nears, long_totals)[None]


def solution(mesh):
    across = mesh.shape["section"]
    devices_exp = mesh.shape["expert"]

    def body(*args):
        topk_count, local_experts = args[3].shape[2], args[5].shape[1]
        regular = devices_exp % (2 * CORES * across) == 0 and devices_exp >= 6 * CORES and devices_exp % 16 == 0 and args[0].shape[0] == LANES
        if local_experts == 1 and devices_exp <= 2 * topk_count and regular:
            return relay_body(*args, across=across)
        return routed_body(*args)

    return jax.shard_map(
        body,
        mesh=mesh,
        in_specs=(
            P("expert", None),
            P("section", "expert", None),
            P("section", None),
            P("section", "expert", None),
            P("section", "expert", None),
            P("section", "expert", None, None),
            P("section", "expert", None, None),
        ),
        out_specs=P("section", "expert", None),
        check_vma=False,
    )
```

```python
import functools

import jax
import jax.numpy as jnp
from jax import lax
from jax.experimental import pallas as pl
from jax.experimental.pallas import tpu as pltpu
from jax.sharding import PartitionSpec as P

epsilon = 1e-06
LANES = 128
HALF = LANES // 2
CORES = 2
MIB = 1 << 20


def from_behind(value, axis, by):
    peers = lax.axis_size(axis)
    pairs = [(i, i + by) for i in range(peers) if 0 <= i + by < peers]
    return lax.ppermute(value, axis, pairs)


def routed_body(fresh, previous, norm_gain, routes, gate_weights, w_gate_up, w_down):
    devices_exp = lax.axis_size("expert")
    section_id = lax.axis_index("section")
    tok_dev = fresh.shape[0]
    width = fresh.shape[1]
    topk_count = routes.shape[2]
    local_experts = w_gate_up.shape[1]
    hidden_units = w_down.shape[2]
    experts_total = devices_exp * local_experts
    capacity = min(tok_dev, 17 * tok_dev * topk_count // (16 * experts_total))
    total_rows = tok_dev * topk_count
    arrived = from_behind(previous[0], "section", 1)
    arrival = jnp.where(section_id == 0, fresh, arrived)
    wide_input = arrival.astype(jnp.float32)
    scale = lax.rsqrt(jnp.mean(wide_input * wide_input, axis=-1, keepdims=True) + epsilon)
    normed = (wide_input * scale * norm_gain[0][None, :]).astype(jnp.bfloat16)
    flat_ids = routes[0].reshape(-1)
    one_hot = (flat_ids[:, None] == jnp.arange(experts_total, dtype=jnp.int32)[None, :]).astype(
        jnp.int32
    )
    slot_rank = jnp.sum(jnp.cumsum(one_hot, axis=0) * one_hot, axis=1) - 1
    position = flat_ids * capacity + slot_rank
    source_row = (
        jnp.full((experts_total * capacity,), total_rows, jnp.int32)
        .at[position]
        .set(jnp.arange(total_rows, dtype=jnp.int32))
    )
    padded = jnp.concatenate([normed, jnp.zeros((1, width), jnp.bfloat16)], axis=0)
    send_buffer = padded[source_row // topk_count].reshape(
        devices_exp, local_experts, capacity, width
    )
    received = lax.all_to_all(send_buffer, "expert", split_axis=0, concat_axis=0, tiled=True)
    projected = jnp.einsum(
        "secd,edf->secf", received, w_gate_up[0], preferred_element_type=jnp.float32
    )
    hidden = (jax.nn.silu(projected[..., :hidden_units]) * projected[..., hidden_units:]).astype(
        jnp.bfloat16
    )
    returned = lax.all_to_all(
        jnp.einsum("secf,efd->secd", hidden, w_down[0], preferred_element_type=jnp.float32).astype(
            jnp.bfloat16
        ),
        "expert",
        split_axis=0,
        concat_axis=0,
        tiled=True,
    )
    flat_back = returned.reshape(experts_total * capacity, width)
    picked = flat_back[position].reshape(tok_dev, topk_count, width).astype(jnp.float32)
    mixed = jnp.sum(picked * gate_weights[0][:, :, None], axis=1)
    return (wide_input + mixed).astype(jnp.bfloat16)[None]


def normed_rows(rows, gain):
    wide = rows.astype(jnp.float32)
    scale = lax.rsqrt(jnp.mean(wide * wide, axis=-1, keepdims=True) + epsilon)
    return (wide * scale * gain).astype(jnp.bfloat16)


def base_kernel(fresh_ref, gain_ref, routes_ref, gates_ref, rows_ref, coefs_ref, fresh_out_ref, gain_out_ref):
    rows_ref[...] = normed_rows(fresh_ref[...], gain_ref[...])
    shape = coefs_ref.shape[1:]
    expert = lax.broadcasted_iota(jnp.int32, shape, 0)
    weight = jnp.zeros(shape, jnp.float32)
    for k in range(routes_ref.shape[0]):
        weight += jnp.where(routes_ref[k : k + 1, :] == expert, gates_ref[k : k + 1, :], 0.0)
    high = weight.astype(jnp.bfloat16).astype(jnp.float32)
    low = weight - high
    left = lax.broadcasted_iota(jnp.int32, shape, 1) < HALF
    coefs_ref[0] = jnp.where(left, high, pltpu.roll(low, HALF, 1)).astype(jnp.bfloat16)
    coefs_ref[1] = jnp.where(left, pltpu.roll(high, HALF, 1), low).astype(jnp.bfloat16)
    fresh_out_ref[...] = fresh_ref[...]
    gain_out_ref[...] = gain_ref[...]


def base_rows(fresh, gain, routes, gates, experts):
    rows, width = fresh.shape
    vmem = pl.BlockSpec(memory_space=pltpu.VMEM)
    return pl.pallas_call(
        base_kernel,
        out_shape=(
            jax.ShapeDtypeStruct((rows, width), jnp.bfloat16),
            jax.ShapeDtypeStruct((2, experts, rows), jnp.bfloat16),
            jax.ShapeDtypeStruct(fresh.shape, fresh.dtype),
            jax.ShapeDtypeStruct(gain.shape, jnp.float32),
        ),
        in_specs=[vmem] * 4,
        out_specs=(vmem,) * 4,
        compiler_params=pltpu.CompilerParams(vmem_limit_bytes=12 * MIB),
        cost_estimate=pl.CostEstimate(flops=rows * width * 6, bytes_accessed=rows * width * 8, transcendentals=rows),
        name="base_rows",
    )(fresh, gain, routes, gates)


def norm_kernel(section_ref, base_ref, coefs_ref, fresh_ref, arrived_ref, gain_ref, rows_ref, arrival_ref, *, chunk):
    rows, width = arrived_ref.shape
    here = slice(chunk * rows, (chunk + 1) * rows)

    def pack(normed):
        for i in range(width // LANES):
            rows_ref[i * rows : (i + 1) * rows, :] = normed[:, i * LANES : (i + 1) * LANES]

    @pl.when(section_ref[0] == 0)
    def _():
        pack(base_ref[here, :])
        arrival_ref[...] = fresh_ref[here, :]

    @pl.when(section_ref[0] != 0)
    def _():
        pack(normed_rows(arrived_ref[...], gain_ref[...]))
        arrival_ref[...] = arrived_ref[...]

    rows_ref[rows * (width // LANES) :, :] = coefs_ref[chunk]


def norm_rows(section_id, base, coefs, fresh, arrived, gain, chunk):
    rows, width = arrived.shape
    vmem = pl.BlockSpec(memory_space=pltpu.VMEM)
    return pl.pallas_call(
        functools.partial(norm_kernel, chunk=chunk),
        out_shape=(
            jax.ShapeDtypeStruct((rows * (width // LANES) + coefs.shape[1], LANES), jnp.bfloat16),
            jax.ShapeDtypeStruct((rows, width), jnp.bfloat16),
        ),
        in_specs=[pl.BlockSpec(memory_space=pltpu.SMEM)] + [vmem] * 5,
        out_specs=(vmem, vmem),
        compiler_params=pltpu.CompilerParams(vmem_limit_bytes=12 * MIB),
        cost_estimate=pl.CostEstimate(flops=rows * width * 6, bytes_accessed=rows * width * 8, transcendentals=rows),
        name="norm_rows",
    )(section_id, base, coefs, fresh, arrived, gain)


def mlp_kernel(expert_ref, *refs, parts, adds, chained):
    payloads = refs[:parts]
    weights = (refs[parts : parts + 2], refs[parts + 2 : parts + 4])
    refs = refs[parts + 4 :]
    terms, totals = refs[:adds], refs[adds : 2 * adds]
    refs = refs[2 * adds + chained :]
    outs, added = refs[:parts], refs[parts : parts + adds]
    x_ref, coef_ref, hidden_ref = refs[parts + adds :]
    for term, total, result in zip(terms, totals, added):
        result[...] = (term[...] + total[...].astype(jnp.float32)).astype(jnp.bfloat16)
    width = x_ref.shape[1]
    hidden = weights[0][1].shape[0]
    line = lax.broadcasted_iota(jnp.int32, (HALF, LANES), 0)
    token = line == lax.broadcasted_iota(jnp.int32, (HALF, LANES), 1) % HALF
    bounds = []
    for part, payload in enumerate(payloads):
        here = slice(part * HALF, (part + 1) * HALF)
        bounds.append(here)
        for i in range(width // LANES):
            x_ref[here, i * LANES : (i + 1) * LANES] = payload[i * HALF : (i + 1) * HALF, :]
        block = payload[HALF * (width // LANES) :, :].astype(jnp.float32)
        expert = lax.broadcasted_iota(jnp.int32, block.shape, 0)
        for which in range(2):
            terms = jnp.sum(jnp.where(expert == expert_ref[0] ^ which, block, 0.0), axis=0, keepdims=True)
            value = jnp.sum(jnp.where(token, terms, 0.0), axis=1, keepdims=True)
            coef_ref[which, here, :] = jnp.broadcast_to(value, (HALF, LANES))
    tile = 256
    for which, (gate_up, _) in enumerate(weights):
        for t in range(0, hidden, tile):
            gate = jnp.dot(x_ref[...], gate_up[:, t : t + tile], preferred_element_type=jnp.float32)
            up = jnp.dot(x_ref[...], gate_up[:, hidden + t : hidden + t + tile], preferred_element_type=jnp.float32)
            value = jax.nn.silu(gate) * up * coef_ref[which][:, :1]
            hidden_ref[:, which * hidden + t : which * hidden + t + tile] = value.astype(jnp.bfloat16)
    tile = 512
    for t in range(0, width, tile):
        total = jnp.zeros((x_ref.shape[0], tile), jnp.float32)
        for which, (_, down) in enumerate(weights):
            rows = hidden_ref[:, which * hidden : (which + 1) * hidden]
            total += jnp.dot(rows, down[:, t : t + tile], preferred_element_type=jnp.float32)
        for here, out in zip(bounds, outs):
            out[:, t : t + tile] = total[here, :]


def expert_rows(expert_id, payloads, own, other, after, terms=(), totals=()):
    width = own[0].shape[0]
    hidden = own[1].shape[0]
    rows = HALF * len(payloads)
    vmem = pl.BlockSpec(memory_space=pltpu.VMEM)
    chain = [] if after is None else [after]
    return pl.pallas_call(
        functools.partial(mlp_kernel, parts=len(payloads), adds=len(terms), chained=len(chain)),
        out_shape=[jax.ShapeDtypeStruct((HALF, width), jnp.float32)] * len(payloads)
        + [jax.ShapeDtypeStruct((HALF, width), jnp.bfloat16)] * len(terms),
        in_specs=[pl.BlockSpec(memory_space=pltpu.SMEM)]
        + [vmem] * (len(payloads) + 4 + 2 * len(terms))
        + [pl.BlockSpec(memory_space=pl.ANY)] * len(chain),
        out_specs=[vmem] * (len(payloads) + len(terms)),
        scratch_shapes=[
            pltpu.VMEM((rows, width), jnp.bfloat16),
            pltpu.VMEM((2, rows, LANES), jnp.float32),
            pltpu.VMEM((rows, 2 * hidden), jnp.bfloat16),
        ],
        compiler_params=pltpu.CompilerParams(vmem_limit_bytes=16 * MIB),
        cost_estimate=pl.CostEstimate(
            flops=2 * rows * width * hidden * 6,
            bytes_accessed=rows * width * 6,
            transcendentals=rows * hidden * 2,
        ),
        name="expert_rows",
    )(expert_id, *payloads, *own, *other, *terms, *totals, *chain)


def last_kernel(near0_ref, near1_ref, total0_ref, total1_ref, out_ref):
    half = near0_ref.shape[0]
    for start, near_ref, total_ref in ((0, near0_ref, total0_ref), (half, near1_ref, total1_ref)):
        total = near_ref[...] + total_ref[...].astype(jnp.float32)
        out_ref[start : start + half, :] = total.astype(jnp.bfloat16)


def last_rows(nears, totals):
    rows, width = nears[0].shape
    vmem = pl.BlockSpec(memory_space=pltpu.VMEM)
    return pl.pallas_call(
        last_kernel,
        out_shape=jax.ShapeDtypeStruct((2 * rows, width), jnp.bfloat16),
        in_specs=[vmem] * 4,
        out_specs=vmem,
        compiler_params=pltpu.CompilerParams(vmem_limit_bytes=8 * MIB),
        cost_estimate=pl.CostEstimate(flops=2 * rows * width, bytes_accessed=rows * width * 16, transcendentals=0),
        name="last_rows",
    )(*nears, *totals)


def chip_ring(depth, across):
    walk = []
    for z in range(depth):
        xs = list(range(1, across))
        walk += [(z, x) for x in (xs if z % 2 == 0 else xs[::-1])]
    return [z * across + x for z, x in walk + [(z, 0) for z in reversed(range(depth))]]


def relay_body(fresh, previous, norm_gain, routes, gate_weights, w_gate_up, w_down, *, across):
    devices_exp = lax.axis_size("expert")
    section_id = lax.axis_index("section").astype(jnp.int32).reshape(1)
    expert_id = lax.axis_index("expert").astype(jnp.int32).reshape(1)
    rows = fresh.shape[0]
    half = HALF
    chips = devices_exp // CORES
    ring = chip_ring(chips // across, across)
    links = list(zip(ring, ring[1:] + ring[:1]))
    up = [(a * CORES + c, b * CORES + c) for a, b in links for c in range(CORES)]
    down = [(b, a) for a, b in up]
    swap = [(i, i ^ 1) for i in range(devices_exp)]

    def move(value, pairs):
        return lax.ppermute(value, "expert", pairs)

    cuts = [slice(0, half), slice(half, rows)]
    own = (w_gate_up[0, 0], w_down[0, 0])
    swapped = lax.optimization_barrier((*own, section_id, expert_id))[:2]
    other = tuple(move(w, swap) for w in swapped)
    base, coefs, fresh, gain = base_rows(fresh, norm_gain, routes[0].T, gate_weights[0].T, devices_exp)
    arrived = [from_behind(previous[0, cut], "section", 1) for cut in cuts]
    packed, arrival = zip(*(norm_rows(section_id, base, coefs, fresh, arrived[c], gain, c) for c in range(2)))
    packed = list(packed)

    hops = chips // 2
    ups = [packed] + [[None, None] for _ in range(hops)]
    downs = [packed] + [[None, None] for _ in range(hops)]

    def pass_on(s, c, after):
        rising, falling = lax.optimization_barrier((ups[s][c], downs[s][c], after))[:2]
        if s < hops - 1 or c == 0:
            ups[s + 1][c] = move(rising, up)
        if s < hops - 1 or c == 1:
            downs[s + 1][c] = move(falling, down)

    last = None

    def mlp(payloads, terms=(), totals=()):
        nonlocal last
        sums = expert_rows(expert_id, payloads, own, other, last, terms, totals)
        last = sums[0]
        return sums

    to_down, to_up = {}, {}
    pass_on(0, 0, None)
    pass_on(0, 1, other)
    for s in range(1, hops):
        for c in range(2):
            pass_on(s, c, last)
            to_down[s, c], to_up[s, c] = mlp([ups[s][c], downs[s][c]])
    to_up[hops, 0], to_down[hops, 1] = mlp([ups[hops][0], downs[hops][1]])

    def send_on(flow, place, total, after):
        terms, c, pairs = flow
        if total is None:
            total = terms[place, c]
        else:
            carried = lax.optimization_barrier((total, after))[0]
            total = terms[place, c] + carried.astype(jnp.float32)
        total = total.astype(jnp.bfloat16)
        return total, move(total, pairs)

    short = [(to_down, 0, down), (to_up, 1, up)]
    long = [(to_up, 0, up), (to_down, 1, down)]
    short_totals = [send_on(flow, hops - 1, None, None)[1] for flow in short]
    long_totals = [send_on(flow, hops, None, None)[1] for flow in long]
    *own_sums, down_sum, up_sum = mlp(packed, [f[0][hops - 2, f[1]] for f in short], short_totals)
    short_totals = [move(total, flow[2]) for total, flow in zip((down_sum, up_sum), short)]
    after = None
    for s in reversed(range(1, hops)):
        sent, long_totals = zip(*(send_on(f, s, t, None) for f, t in zip(long, long_totals)))
        if 1 < s < hops - 1:
            short_totals = [send_on(f, s - 1, t, sent)[1] for f, t in zip(short, short_totals)]

    nears = [
        arrival[c].astype(jnp.float32) + (own_sums[c] + short_totals[c].astype(jnp.float32)) for c in range(2)
    ]
    nears = lax.optimization_barrier(nears)
    return last_rows(nears, long_totals)[None]


def solution(mesh):
    across = mesh.shape["section"]
    devices_exp = mesh.shape["expert"]

    def body(*args):
        topk_count, local_experts = args[3].shape[2], args[5].shape[1]
        regular = devices_exp % (2 * CORES * across) == 0 and devices_exp >= 6 * CORES and devices_exp % 16 == 0 and args[0].shape[0] == LANES
        if local_experts == 1 and devices_exp <= 2 * topk_count and regular:
            return relay_body(*args, across=across)
        return routed_body(*args)

    return jax.shard_map(
        body,
        mesh=mesh,
        in_specs=(
            P("expert", None),
            P("section", "expert", None),
            P("section", None),
            P("section", "expert", None),
            P("section", "expert", None),
            P("section", "expert", None, None),
            P("section", "expert", None, None),
        ),
        out_specs=P("section", "expert", None),
        check_vma=False,
    )
```

```python
import functools

import jax
import jax.numpy as jnp
from jax import lax
from jax.experimental import pallas as pl
from jax.experimental.pallas import tpu as pltpu
from jax.sharding import PartitionSpec as P

epsilon = 1e-06
LANES = 128
HALF = LANES // 2
CORES = 2
MIB = 1 << 20


def from_behind(value, axis, by):
    peers = lax.axis_size(axis)
    pairs = [(i, i + by) for i in range(peers) if 0 <= i + by < peers]
    return lax.ppermute(value, axis, pairs)


def routed_body(fresh, previous, norm_gain, routes, gate_weights, w_gate_up, w_down):
    devices_exp = lax.axis_size("expert")
    section_id = lax.axis_index("section")
    tok_dev = fresh.shape[0]
    width = fresh.shape[1]
    topk_count = routes.shape[2]
    local_experts = w_gate_up.shape[1]
    hidden_units = w_down.shape[2]
    experts_total = devices_exp * local_experts
    capacity = min(tok_dev, 17 * tok_dev * topk_count // (16 * experts_total))
    total_rows = tok_dev * topk_count
    arrived = from_behind(previous[0], "section", 1)
    arrival = jnp.where(section_id == 0, fresh, arrived)
    wide_input = arrival.astype(jnp.float32)
    scale = lax.rsqrt(jnp.mean(wide_input * wide_input, axis=-1, keepdims=True) + epsilon)
    normed = (wide_input * scale * norm_gain[0][None, :]).astype(jnp.bfloat16)
    flat_ids = routes[0].reshape(-1)
    one_hot = (flat_ids[:, None] == jnp.arange(experts_total, dtype=jnp.int32)[None, :]).astype(
        jnp.int32
    )
    slot_rank = jnp.sum(jnp.cumsum(one_hot, axis=0) * one_hot, axis=1) - 1
    position = flat_ids * capacity + slot_rank
    source_row = (
        jnp.full((experts_total * capacity,), total_rows, jnp.int32)
        .at[position]
        .set(jnp.arange(total_rows, dtype=jnp.int32))
    )
    padded = jnp.concatenate([normed, jnp.zeros((1, width), jnp.bfloat16)], axis=0)
    send_buffer = padded[source_row // topk_count].reshape(
        devices_exp, local_experts, capacity, width
    )
    received = lax.all_to_all(send_buffer, "expert", split_axis=0, concat_axis=0, tiled=True)
    projected = jnp.einsum(
        "secd,edf->secf", received, w_gate_up[0], preferred_element_type=jnp.float32
    )
    hidden = (jax.nn.silu(projected[..., :hidden_units]) * projected[..., hidden_units:]).astype(
        jnp.bfloat16
    )
    returned = lax.all_to_all(
        jnp.einsum("secf,efd->secd", hidden, w_down[0], preferred_element_type=jnp.float32).astype(
            jnp.bfloat16
        ),
        "expert",
        split_axis=0,
        concat_axis=0,
        tiled=True,
    )
    flat_back = returned.reshape(experts_total * capacity, width)
    picked = flat_back[position].reshape(tok_dev, topk_count, width).astype(jnp.float32)
    mixed = jnp.sum(picked * gate_weights[0][:, :, None], axis=1)
    return (wide_input + mixed).astype(jnp.bfloat16)[None]


def normed_rows(rows, gain):
    wide = rows.astype(jnp.float32)
    scale = lax.rsqrt(jnp.mean(wide * wide, axis=-1, keepdims=True) + epsilon)
    return (wide * scale * gain).astype(jnp.bfloat16)


def base_kernel(fresh_ref, gain_ref, routes_ref, gates_ref, rows_ref, coefs_ref, fresh_out_ref, gain_out_ref):
    rows_ref[...] = normed_rows(fresh_ref[...], gain_ref[...])
    shape = coefs_ref.shape[1:]
    expert = lax.broadcasted_iota(jnp.int32, shape, 0)
    weight = jnp.zeros(shape, jnp.float32)
    for k in range(routes_ref.shape[0]):
        weight += jnp.where(routes_ref[k : k + 1, :] == expert, gates_ref[k : k + 1, :], 0.0)
    high = weight.astype(jnp.bfloat16).astype(jnp.float32)
    low = weight - high
    left = lax.broadcasted_iota(jnp.int32, shape, 1) < HALF
    coefs_ref[0] = jnp.where(left, high, pltpu.roll(low, HALF, 1)).astype(jnp.bfloat16)
    coefs_ref[1] = jnp.where(left, pltpu.roll(high, HALF, 1), low).astype(jnp.bfloat16)
    fresh_out_ref[...] = fresh_ref[...]
    gain_out_ref[...] = gain_ref[...]


def base_rows(fresh, gain, routes, gates, experts):
    rows, width = fresh.shape
    vmem = pl.BlockSpec(memory_space=pltpu.VMEM)
    return pl.pallas_call(
        base_kernel,
        out_shape=(
            jax.ShapeDtypeStruct((rows, width), jnp.bfloat16),
            jax.ShapeDtypeStruct((2, experts, rows), jnp.bfloat16),
            jax.ShapeDtypeStruct(fresh.shape, fresh.dtype),
            jax.ShapeDtypeStruct(gain.shape, jnp.float32),
        ),
        in_specs=[vmem] * 4,
        out_specs=(vmem,) * 4,
        compiler_params=pltpu.CompilerParams(vmem_limit_bytes=12 * MIB),
        cost_estimate=pl.CostEstimate(flops=rows * width * 6, bytes_accessed=rows * width * 8, transcendentals=rows),
        name="base_rows",
    )(fresh, gain, routes, gates)


def norm_kernel(section_ref, base_ref, coefs_ref, fresh_ref, arrived_ref, gain_ref, rows_ref, arrival_ref, *, chunk):
    rows, width = arrived_ref.shape
    here = slice(chunk * rows, (chunk + 1) * rows)

    def pack(normed):
        for i in range(width // LANES):
            rows_ref[i * rows : (i + 1) * rows, :] = normed[:, i * LANES : (i + 1) * LANES]

    @pl.when(section_ref[0] == 0)
    def _():
        pack(base_ref[here, :])
        arrival_ref[...] = fresh_ref[here, :]

    @pl.when(section_ref[0] != 0)
    def _():
        pack(normed_rows(arrived_ref[...], gain_ref[...]))
        arrival_ref[...] = arrived_ref[...]

    rows_ref[rows * (width // LANES) :, :] = coefs_ref[chunk]


def norm_rows(section_id, base, coefs, fresh, arrived, gain, chunk):
    rows, width = arrived.shape
    vmem = pl.BlockSpec(memory_space=pltpu.VMEM)
    return pl.pallas_call(
        functools.partial(norm_kernel, chunk=chunk),
        out_shape=(
            jax.ShapeDtypeStruct((rows * (width // LANES) + coefs.shape[1], LANES), jnp.bfloat16),
            jax.ShapeDtypeStruct((rows, width), jnp.bfloat16),
        ),
        in_specs=[pl.BlockSpec(memory_space=pltpu.SMEM)] + [vmem] * 5,
        out_specs=(vmem, vmem),
        compiler_params=pltpu.CompilerParams(vmem_limit_bytes=12 * MIB),
        cost_estimate=pl.CostEstimate(flops=rows * width * 6, bytes_accessed=rows * width * 8, transcendentals=rows),
        name="norm_rows",
    )(section_id, base, coefs, fresh, arrived, gain)


def mlp_kernel(expert_ref, *refs, parts, adds, chained):
    payloads = refs[:parts]
    weights = (refs[parts : parts + 2], refs[parts + 2 : parts + 4])
    refs = refs[parts + 4 :]
    terms, totals = refs[:adds], refs[adds : 2 * adds]
    refs = refs[2 * adds + chained :]
    outs, added = refs[:parts], refs[parts : parts + adds]
    x_ref, coef_ref, hidden_ref = refs[parts + adds :]
    for term, total, result in zip(terms, totals, added):
        result[...] = (term[...] + total[...].astype(jnp.float32)).astype(jnp.bfloat16)
    width = x_ref.shape[1]
    hidden = weights[0][1].shape[0]
    line = lax.broadcasted_iota(jnp.int32, (HALF, LANES), 0)
    token = line == lax.broadcasted_iota(jnp.int32, (HALF, LANES), 1) % HALF
    bounds = []
    for part, payload in enumerate(payloads):
        here = slice(part * HALF, (part + 1) * HALF)
        bounds.append(here)
        for i in range(width // LANES):
            x_ref[here, i * LANES : (i + 1) * LANES] = payload[i * HALF : (i + 1) * HALF, :]
        block = payload[HALF * (width // LANES) :, :].astype(jnp.float32)
        expert = lax.broadcasted_iota(jnp.int32, block.shape, 0)
        for which in range(2):
            terms = jnp.sum(jnp.where(expert == expert_ref[0] ^ which, block, 0.0), axis=0, keepdims=True)
            value = jnp.sum(jnp.where(token, terms, 0.0), axis=1, keepdims=True)
            coef_ref[which, here, :] = jnp.broadcast_to(value, (HALF, LANES))
    tile = 256
    for which, (gate_up, _) in enumerate(weights):
        for t in range(0, hidden, tile):
            gate = jnp.dot(x_ref[...], gate_up[:, t : t + tile], preferred_element_type=jnp.float32)
            up = jnp.dot(x_ref[...], gate_up[:, hidden + t : hidden + t + tile], preferred_element_type=jnp.float32)
            value = jax.nn.silu(gate) * up * coef_ref[which][:, :1]
            hidden_ref[:, which * hidden + t : which * hidden + t + tile] = value.astype(jnp.bfloat16)
    tile = 512
    for t in range(0, width, tile):
        total = jnp.zeros((x_ref.shape[0], tile), jnp.float32)
        for which, (_, down) in enumerate(weights):
            rows = hidden_ref[:, which * hidden : (which + 1) * hidden]
            total += jnp.dot(rows, down[:, t : t + tile], preferred_element_type=jnp.float32)
        for here, out in zip(bounds, outs):
            out[:, t : t + tile] = total[here, :]


def expert_rows(expert_id, payloads, own, other, after, terms=(), totals=()):
    width = own[0].shape[0]
    hidden = own[1].shape[0]
    rows = HALF * len(payloads)
    vmem = pl.BlockSpec(memory_space=pltpu.VMEM)
    chain = [] if after is None else [after]
    return pl.pallas_call(
        functools.partial(mlp_kernel, parts=len(payloads), adds=len(terms), chained=len(chain)),
        out_shape=[jax.ShapeDtypeStruct((HALF, width), jnp.float32)] * len(payloads)
        + [jax.ShapeDtypeStruct((HALF, width), jnp.bfloat16)] * len(terms),
        in_specs=[pl.BlockSpec(memory_space=pltpu.SMEM)]
        + [vmem] * (len(payloads) + 4 + 2 * len(terms))
        + [pl.BlockSpec(memory_space=pl.ANY)] * len(chain),
        out_specs=[vmem] * (len(payloads) + len(terms)),
        scratch_shapes=[
            pltpu.VMEM((rows, width), jnp.bfloat16),
            pltpu.VMEM((2, rows, LANES), jnp.float32),
            pltpu.VMEM((rows, 2 * hidden), jnp.bfloat16),
        ],
        compiler_params=pltpu.CompilerParams(vmem_limit_bytes=16 * MIB),
        cost_estimate=pl.CostEstimate(
            flops=2 * rows * width * hidden * 6,
            bytes_accessed=rows * width * 6,
            transcendentals=rows * hidden * 2,
        ),
        name="expert_rows",
    )(expert_id, *payloads, *own, *other, *terms, *totals, *chain)


def last_kernel(near0_ref, near1_ref, total0_ref, total1_ref, out_ref):
    half = near0_ref.shape[0]
    for start, near_ref, total_ref in ((0, near0_ref, total0_ref), (half, near1_ref, total1_ref)):
        total = near_ref[...] + total_ref[...].astype(jnp.float32)
        out_ref[start : start + half, :] = total.astype(jnp.bfloat16)


def last_rows(nears, totals):
    rows, width = nears[0].shape
    vmem = pl.BlockSpec(memory_space=pltpu.VMEM)
    return pl.pallas_call(
        last_kernel,
        out_shape=jax.ShapeDtypeStruct((2 * rows, width), jnp.bfloat16),
        in_specs=[vmem] * 4,
        out_specs=vmem,
        compiler_params=pltpu.CompilerParams(vmem_limit_bytes=8 * MIB),
        cost_estimate=pl.CostEstimate(flops=2 * rows * width, bytes_accessed=rows * width * 16, transcendentals=0),
        name="last_rows",
    )(*nears, *totals)


def chip_ring(depth, across):
    walk = []
    for z in range(depth):
        xs = list(range(1, across))
        walk += [(z, x) for x in (xs if z % 2 == 0 else xs[::-1])]
    return [z * across + x for z, x in walk + [(z, 0) for z in reversed(range(depth))]]


def relay_body(fresh, previous, norm_gain, routes, gate_weights, w_gate_up, w_down, *, across):
    devices_exp = lax.axis_size("expert")
    section_id = lax.axis_index("section").astype(jnp.int32).reshape(1)
    expert_id = lax.axis_index("expert").astype(jnp.int32).reshape(1)
    rows = fresh.shape[0]
    half = HALF
    chips = devices_exp // CORES
    ring = chip_ring(chips // across, across)
    links = list(zip(ring, ring[1:] + ring[:1]))
    up = [(a * CORES + c, b * CORES + c) for a, b in links for c in range(CORES)]
    down = [(b, a) for a, b in up]
    swap = [(i, i ^ 1) for i in range(devices_exp)]

    def move(value, pairs):
        return lax.ppermute(value, "expert", pairs)

    cuts = [slice(0, half), slice(half, rows)]
    own = (w_gate_up[0, 0], w_down[0, 0])
    swapped = lax.optimization_barrier((*own, section_id, expert_id))[:2]
    other = tuple(move(w, swap) for w in swapped)
    base, coefs, fresh, gain = base_rows(fresh, norm_gain, routes[0].T, gate_weights[0].T, devices_exp)
    arrived = [from_behind(previous[0, cut], "section", 1) for cut in cuts]
    packed, arrival = zip(*(norm_rows(section_id, base, coefs, fresh, arrived[c], gain, c) for c in range(2)))
    packed = list(packed)

    hops = chips // 2
    ups = [packed] + [[None, None] for _ in range(hops)]
    downs = [packed] + [[None, None] for _ in range(hops)]

    def pass_on(s, c, after):
        rising, falling = lax.optimization_barrier((ups[s][c], downs[s][c], after))[:2]
        if s < hops - 1 or c == 0:
            ups[s + 1][c] = move(rising, up)
        if s < hops - 1 or c == 1:
            downs[s + 1][c] = move(falling, down)

    last = None

    def mlp(payloads, terms=(), totals=()):
        nonlocal last
        sums = expert_rows(expert_id, payloads, own, other, last, terms, totals)
        last = sums[0]
        return sums

    to_down, to_up = {}, {}
    pass_on(0, 0, None)
    pass_on(0, 1, other)
    for s in range(1, hops):
        for c in range(2):
            pass_on(s, c, last)
            to_down[s, c], to_up[s, c] = mlp([ups[s][c], downs[s][c]])
    to_up[hops, 0], to_down[hops, 1] = mlp([ups[hops][0], downs[hops][1]])

    def send_on(flow, place, total, after):
        terms, c, pairs = flow
        if total is None:
            total = terms[place, c]
        else:
            carried = lax.optimization_barrier((total, after))[0]
            total = terms[place, c] + carried.astype(jnp.float32)
        total = total.astype(jnp.bfloat16)
        return total, move(total, pairs)

    short = [(to_down, 0, down), (to_up, 1, up)]
    long = [(to_up, 0, up), (to_down, 1, down)]
    short_totals = [send_on(flow, hops - 1, None, None)[1] for flow in short]
    long_totals = [send_on(flow, hops, None, None)[1] for flow in long]
    for s in reversed(range(1, hops)):
        sent, long_totals = zip(*(send_on(f, s, t, short_totals if s == hops - 1 else None) for f, t in zip(long, long_totals)))
        if s == hops - 1:
            totals = lax.optimization_barrier((short_totals, sent))[0]
            *own_sums, down_sum, up_sum = mlp(packed, [f[0][s - 1, f[1]] for f in short], totals)
            short_totals = [move(total, flow[2]) for total, flow in zip((down_sum, up_sum), short)]
        elif s > 1:
            short_totals = [send_on(f, s - 1, t, sent)[1] for f, t in zip(short, short_totals)]

    nears = [
        arrival[c].astype(jnp.float32) + (own_sums[c] + short_totals[c].astype(jnp.float32)) for c in range(2)
    ]
    nears = lax.optimization_barrier(nears)
    return last_rows(nears, long_totals)[None]


def solution(mesh):
    across = mesh.shape["section"]
    devices_exp = mesh.shape["expert"]

    def body(*args):
        topk_count, local_experts = args[3].shape[2], args[5].shape[1]
        regular = devices_exp % (2 * CORES * across) == 0 and devices_exp >= 6 * CORES and devices_exp % 16 == 0 and args[0].shape[0] == LANES
        if local_experts == 1 and devices_exp <= 2 * topk_count and regular:
            return relay_body(*args, across=across)
        return routed_body(*args)

    return jax.shard_map(
        body,
        mesh=mesh,
        in_specs=(
            P("expert", None),
            P("section", "expert", None),
            P("section", None),
            P("section", "expert", None),
            P("section", "expert", None),
            P("section", "expert", None, None),
            P("section", "expert", None, None),
        ),
        out_specs=P("section", "expert", None),
        check_vma=False,
    )
```

```python
import functools

import jax
import jax.numpy as jnp
from jax import lax
from jax.experimental import pallas as pl
from jax.experimental.pallas import tpu as pltpu
from jax.sharding import PartitionSpec as P

epsilon = 1e-06
LANES = 128
HALF = LANES // 2
CORES = 2
MIB = 1 << 20


def from_behind(value, axis, by):
    peers = lax.axis_size(axis)
    pairs = [(i, i + by) for i in range(peers) if 0 <= i + by < peers]
    return lax.ppermute(value, axis, pairs)


def routed_body(fresh, previous, norm_gain, routes, gate_weights, w_gate_up, w_down):
    devices_exp = lax.axis_size("expert")
    section_id = lax.axis_index("section")
    tok_dev = fresh.shape[0]
    width = fresh.shape[1]
    topk_count = routes.shape[2]
    local_experts = w_gate_up.shape[1]
    hidden_units = w_down.shape[2]
    experts_total = devices_exp * local_experts
    capacity = min(tok_dev, 17 * tok_dev * topk_count // (16 * experts_total))
    total_rows = tok_dev * topk_count
    arrived = from_behind(previous[0], "section", 1)
    arrival = jnp.where(section_id == 0, fresh, arrived)
    wide_input = arrival.astype(jnp.float32)
    scale = lax.rsqrt(jnp.mean(wide_input * wide_input, axis=-1, keepdims=True) + epsilon)
    normed = (wide_input * scale * norm_gain[0][None, :]).astype(jnp.bfloat16)
    flat_ids = routes[0].reshape(-1)
    one_hot = (flat_ids[:, None] == jnp.arange(experts_total, dtype=jnp.int32)[None, :]).astype(
        jnp.int32
    )
    slot_rank = jnp.sum(jnp.cumsum(one_hot, axis=0) * one_hot, axis=1) - 1
    position = flat_ids * capacity + slot_rank
    source_row = (
        jnp.full((experts_total * capacity,), total_rows, jnp.int32)
        .at[position]
        .set(jnp.arange(total_rows, dtype=jnp.int32))
    )
    padded = jnp.concatenate([normed, jnp.zeros((1, width), jnp.bfloat16)], axis=0)
    send_buffer = padded[source_row // topk_count].reshape(
        devices_exp, local_experts, capacity, width
    )
    received = lax.all_to_all(send_buffer, "expert", split_axis=0, concat_axis=0, tiled=True)
    projected = jnp.einsum(
        "secd,edf->secf", received, w_gate_up[0], preferred_element_type=jnp.float32
    )
    hidden = (jax.nn.silu(projected[..., :hidden_units]) * projected[..., hidden_units:]).astype(
        jnp.bfloat16
    )
    returned = lax.all_to_all(
        jnp.einsum("secf,efd->secd", hidden, w_down[0], preferred_element_type=jnp.float32).astype(
            jnp.bfloat16
        ),
        "expert",
        split_axis=0,
        concat_axis=0,
        tiled=True,
    )
    flat_back = returned.reshape(experts_total * capacity, width)
    picked = flat_back[position].reshape(tok_dev, topk_count, width).astype(jnp.float32)
    mixed = jnp.sum(picked * gate_weights[0][:, :, None], axis=1)
    return (wide_input + mixed).astype(jnp.bfloat16)[None]


def normed_rows(rows, gain):
    wide = rows.astype(jnp.float32)
    scale = lax.rsqrt(jnp.mean(wide * wide, axis=-1, keepdims=True) + epsilon)
    return (wide * scale * gain).astype(jnp.bfloat16)


def base_kernel(fresh_ref, gain_ref, routes_ref, gates_ref, rows_ref, coefs_ref, fresh_out_ref, gain_out_ref):
    rows_ref[...] = normed_rows(fresh_ref[...], gain_ref[...])
    shape = coefs_ref.shape[1:]
    expert = lax.broadcasted_iota(jnp.int32, shape, 0)
    weight = jnp.zeros(shape, jnp.float32)
    for k in range(routes_ref.shape[0]):
        weight += jnp.where(routes_ref[k : k + 1, :] == expert, gates_ref[k : k + 1, :], 0.0)
    high = weight.astype(jnp.bfloat16).astype(jnp.float32)
    low = weight - high
    left = lax.broadcasted_iota(jnp.int32, shape, 1) < HALF
    coefs_ref[0] = jnp.where(left, high, pltpu.roll(low, HALF, 1)).astype(jnp.bfloat16)
    coefs_ref[1] = jnp.where(left, pltpu.roll(high, HALF, 1), low).astype(jnp.bfloat16)
    fresh_out_ref[...] = fresh_ref[...]
    gain_out_ref[...] = gain_ref[...]


def base_rows(fresh, gain, routes, gates, experts):
    rows, width = fresh.shape
    vmem = pl.BlockSpec(memory_space=pltpu.VMEM)
    return pl.pallas_call(
        base_kernel,
        out_shape=(
            jax.ShapeDtypeStruct((rows, width), jnp.bfloat16),
            jax.ShapeDtypeStruct((2, experts, rows), jnp.bfloat16),
            jax.ShapeDtypeStruct(fresh.shape, fresh.dtype),
            jax.ShapeDtypeStruct(gain.shape, jnp.float32),
        ),
        in_specs=[vmem] * 4,
        out_specs=(vmem,) * 4,
        compiler_params=pltpu.CompilerParams(vmem_limit_bytes=12 * MIB),
        cost_estimate=pl.CostEstimate(flops=rows * width * 6, bytes_accessed=rows * width * 8, transcendentals=rows),
        name="base_rows",
    )(fresh, gain, routes, gates)


def norm_kernel(section_ref, base_ref, coefs_ref, fresh_ref, arrived_ref, gain_ref, rows_ref, arrival_ref, *, chunk):
    rows, width = arrived_ref.shape
    here = slice(chunk * rows, (chunk + 1) * rows)

    def pack(normed):
        for i in range(width // LANES):
            rows_ref[i * rows : (i + 1) * rows, :] = normed[:, i * LANES : (i + 1) * LANES]

    @pl.when(section_ref[0] == 0)
    def _():
        pack(base_ref[here, :])
        arrival_ref[...] = fresh_ref[here, :]

    @pl.when(section_ref[0] != 0)
    def _():
        pack(normed_rows(arrived_ref[...], gain_ref[...]))
        arrival_ref[...] = arrived_ref[...]

    rows_ref[rows * (width // LANES) :, :] = coefs_ref[chunk]


def norm_rows(section_id, base, coefs, fresh, arrived, gain, chunk):
    rows, width = arrived.shape
    vmem = pl.BlockSpec(memory_space=pltpu.VMEM)
    return pl.pallas_call(
        functools.partial(norm_kernel, chunk=chunk),
        out_shape=(
            jax.ShapeDtypeStruct((rows * (width // LANES) + coefs.shape[1], LANES), jnp.bfloat16),
            jax.ShapeDtypeStruct((rows, width), jnp.bfloat16),
        ),
        in_specs=[pl.BlockSpec(memory_space=pltpu.SMEM)] + [vmem] * 5,
        out_specs=(vmem, vmem),
        compiler_params=pltpu.CompilerParams(vmem_limit_bytes=12 * MIB),
        cost_estimate=pl.CostEstimate(flops=rows * width * 6, bytes_accessed=rows * width * 8, transcendentals=rows),
        name="norm_rows",
    )(section_id, base, coefs, fresh, arrived, gain)


def mlp_kernel(expert_ref, *refs, parts, adds, chained):
    payloads = refs[:parts]
    weights = (refs[parts : parts + 2], refs[parts + 2 : parts + 4])
    refs = refs[parts + 4 :]
    terms, totals = refs[:adds], refs[adds : 2 * adds]
    refs = refs[2 * adds + chained :]
    outs, added = refs[:parts], refs[parts : parts + adds]
    x_ref, coef_ref, hidden_ref = refs[parts + adds :]
    for term, total, result in zip(terms, totals, added):
        result[...] = (term[...] + total[...].astype(jnp.float32)).astype(jnp.bfloat16)
    width = x_ref.shape[1]
    hidden = weights[0][1].shape[0]
    line = lax.broadcasted_iota(jnp.int32, (HALF, LANES), 0)
    token = line == lax.broadcasted_iota(jnp.int32, (HALF, LANES), 1) % HALF
    bounds = []
    for part, payload in enumerate(payloads):
        here = slice(part * HALF, (part + 1) * HALF)
        bounds.append(here)
        for i in range(width // LANES):
            x_ref[here, i * LANES : (i + 1) * LANES] = payload[i * HALF : (i + 1) * HALF, :]
        block = payload[HALF * (width // LANES) :, :].astype(jnp.float32)
        expert = lax.broadcasted_iota(jnp.int32, block.shape, 0)
        for which in range(2):
            terms = jnp.sum(jnp.where(expert == expert_ref[0] ^ which, block, 0.0), axis=0, keepdims=True)
            value = jnp.sum(jnp.where(token, terms, 0.0), axis=1, keepdims=True)
            coef_ref[which, here, :] = jnp.broadcast_to(value, (HALF, LANES))
    tile = 256
    for which, (gate_up, _) in enumerate(weights):
        for t in range(0, hidden, tile):
            gate = jnp.dot(x_ref[...], gate_up[:, t : t + tile], preferred_element_type=jnp.float32)
            up = jnp.dot(x_ref[...], gate_up[:, hidden + t : hidden + t + tile], preferred_element_type=jnp.float32)
            value = jax.nn.silu(gate) * up * coef_ref[which][:, :1]
            hidden_ref[:, which * hidden + t : which * hidden + t + tile] = value.astype(jnp.bfloat16)
    tile = 512
    for t in range(0, width, tile):
        total = jnp.zeros((x_ref.shape[0], tile), jnp.float32)
        for which, (_, down) in enumerate(weights):
            rows = hidden_ref[:, which * hidden : (which + 1) * hidden]
            total += jnp.dot(rows, down[:, t : t + tile], preferred_element_type=jnp.float32)
        for here, out in zip(bounds, outs):
            out[:, t : t + tile] = total[here, :]


def expert_rows(expert_id, payloads, own, other, after, terms=(), totals=()):
    width = own[0].shape[0]
    hidden = own[1].shape[0]
    rows = HALF * len(payloads)
    vmem = pl.BlockSpec(memory_space=pltpu.VMEM)
    chain = [] if after is None else [after]
    return pl.pallas_call(
        functools.partial(mlp_kernel, parts=len(payloads), adds=len(terms), chained=len(chain)),
        out_shape=[jax.ShapeDtypeStruct((HALF, width), jnp.float32)] * len(payloads)
        + [jax.ShapeDtypeStruct((HALF, width), jnp.bfloat16)] * len(terms),
        in_specs=[pl.BlockSpec(memory_space=pltpu.SMEM)]
        + [vmem] * (len(payloads) + 4 + 2 * len(terms))
        + [pl.BlockSpec(memory_space=pl.ANY)] * len(chain),
        out_specs=[vmem] * (len(payloads) + len(terms)),
        scratch_shapes=[
            pltpu.VMEM((rows, width), jnp.bfloat16),
            pltpu.VMEM((2, rows, LANES), jnp.float32),
            pltpu.VMEM((rows, 2 * hidden), jnp.bfloat16),
        ],
        compiler_params=pltpu.CompilerParams(vmem_limit_bytes=16 * MIB),
        cost_estimate=pl.CostEstimate(
            flops=2 * rows * width * hidden * 6,
            bytes_accessed=rows * width * 6,
            transcendentals=rows * hidden * 2,
        ),
        name="expert_rows",
    )(expert_id, *payloads, *own, *other, *terms, *totals, *chain)


def last_kernel(near0_ref, near1_ref, total0_ref, total1_ref, out_ref):
    half = near0_ref.shape[0]
    for start, near_ref, total_ref in ((0, near0_ref, total0_ref), (half, near1_ref, total1_ref)):
        total = near_ref[...] + total_ref[...].astype(jnp.float32)
        out_ref[start : start + half, :] = total.astype(jnp.bfloat16)


def last_rows(nears, totals):
    rows, width = nears[0].shape
    vmem = pl.BlockSpec(memory_space=pltpu.VMEM)
    return pl.pallas_call(
        last_kernel,
        out_shape=jax.ShapeDtypeStruct((2 * rows, width), jnp.bfloat16),
        in_specs=[vmem] * 4,
        out_specs=vmem,
        compiler_params=pltpu.CompilerParams(vmem_limit_bytes=8 * MIB),
        cost_estimate=pl.CostEstimate(flops=2 * rows * width, bytes_accessed=rows * width * 16, transcendentals=0),
        name="last_rows",
    )(*nears, *totals)


def chip_ring(depth, across):
    walk = []
    for z in range(depth):
        xs = list(range(1, across))
        walk += [(z, x) for x in (xs if z % 2 == 0 else xs[::-1])]
    return [z * across + x for z, x in walk + [(z, 0) for z in reversed(range(depth))]]


def relay_body(fresh, previous, norm_gain, routes, gate_weights, w_gate_up, w_down, *, across):
    devices_exp = lax.axis_size("expert")
    section_id = lax.axis_index("section").astype(jnp.int32).reshape(1)
    expert_id = lax.axis_index("expert").astype(jnp.int32).reshape(1)
    rows = fresh.shape[0]
    half = HALF
    chips = devices_exp // CORES
    ring = chip_ring(chips // across, across)
    links = list(zip(ring, ring[1:] + ring[:1]))
    up = [(a * CORES + c, b * CORES + c) for a, b in links for c in range(CORES)]
    down = [(b, a) for a, b in up]
    swap = [(i, i ^ 1) for i in range(devices_exp)]

    def move(value, pairs):
        return lax.ppermute(value, "expert", pairs)

    cuts = [slice(0, half), slice(half, rows)]
    own = (w_gate_up[0, 0], w_down[0, 0])
    swapped = lax.optimization_barrier((*own, section_id, expert_id))[:2]
    other = tuple(move(w, swap) for w in swapped)
    base, coefs, fresh, gain = base_rows(fresh, norm_gain, routes[0].T, gate_weights[0].T, devices_exp)
    arrived = [from_behind(previous[0, cut], "section", 1) for cut in cuts]
    packed, arrival = zip(*(norm_rows(section_id, base, coefs, fresh, arrived[c], gain, c) for c in range(2)))
    packed = list(packed)

    hops = chips // 2
    ups = [packed] + [[None, None] for _ in range(hops)]
    downs = [packed] + [[None, None] for _ in range(hops)]

    def pass_on(s, c, after):
        if s < 2:
            rising = lax.optimization_barrier((ups[s][c], after))[0]
            falling = lax.optimization_barrier((downs[s][c], after))[0]
        else:
            rising, falling = lax.optimization_barrier((ups[s][c], downs[s][c], after))[:2]
        if s < hops - 1 or c == 0:
            ups[s + 1][c] = move(rising, up)
        if s < hops - 1 or c == 1:
            downs[s + 1][c] = move(falling, down)

    last = None

    def mlp(payloads, terms=(), totals=()):
        nonlocal last
        sums = expert_rows(expert_id, payloads, own, other, last, terms, totals)
        last = sums[0]
        return sums

    to_down, to_up = {}, {}
    pass_on(0, 0, None)
    pass_on(0, 1, other)
    for s in range(1, hops):
        for c in range(2):
            pass_on(s, c, last)
            to_down[s, c], to_up[s, c] = mlp([ups[s][c], downs[s][c]])
    to_up[hops, 0], to_down[hops, 1] = mlp([ups[hops][0], downs[hops][1]])

    def send_on(flow, place, total, after):
        terms, c, pairs = flow
        if total is None:
            total = terms[place, c]
        else:
            carried = lax.optimization_barrier((total, after))[0]
            total = terms[place, c] + carried.astype(jnp.float32)
        total = total.astype(jnp.bfloat16)
        return total, move(total, pairs)

    short = [(to_down, 0, down), (to_up, 1, up)]
    long = [(to_up, 0, up), (to_down, 1, down)]
    short_totals = [send_on(flow, hops - 1, None, None)[1] for flow in short]
    long_totals = [send_on(flow, hops, None, None)[1] for flow in long]
    *own_sums, down_sum, up_sum = mlp(packed, [f[0][hops - 2, f[1]] for f in short], short_totals)
    short_totals = [move(total, flow[2]) for total, flow in zip((down_sum, up_sum), short)]
    after = None
    for s in reversed(range(1, hops)):
        sent, long_totals = zip(*(send_on(f, s, t, None) for f, t in zip(long, long_totals)))
        if 1 < s < hops - 1:
            short_totals = [send_on(f, s - 1, t, sent)[1] for f, t in zip(short, short_totals)]

    nears = [
        arrival[c].astype(jnp.float32) + (own_sums[c] + short_totals[c].astype(jnp.float32)) for c in range(2)
    ]
    nears = lax.optimization_barrier(nears)
    return last_rows(nears, long_totals)[None]


def solution(mesh):
    across = mesh.shape["section"]
    devices_exp = mesh.shape["expert"]

    def body(*args):
        topk_count, local_experts = args[3].shape[2], args[5].shape[1]
        regular = devices_exp % (2 * CORES * across) == 0 and devices_exp >= 6 * CORES and devices_exp % 16 == 0 and args[0].shape[0] == LANES
        if local_experts == 1 and devices_exp <= 2 * topk_count and regular:
            return relay_body(*args, across=across)
        return routed_body(*args)

    return jax.shard_map(
        body,
        mesh=mesh,
        in_specs=(
            P("expert", None),
            P("section", "expert", None),
            P("section", None),
            P("section", "expert", None),
            P("section", "expert", None),
            P("section", "expert", None, None),
            P("section", "expert", None, None),
        ),
        out_specs=P("section", "expert", None),
        check_vma=False,
    )
```

```python
import functools

import jax
import jax.numpy as jnp
from jax import lax
from jax.experimental import pallas as pl
from jax.experimental.pallas import tpu as pltpu
from jax.sharding import PartitionSpec as P

epsilon = 1e-06
LANES = 128
HALF = LANES // 2
CORES = 2
MIB = 1 << 20


def from_behind(value, axis, by):
    peers = lax.axis_size(axis)
    pairs = [(i, i + by) for i in range(peers) if 0 <= i + by < peers]
    return lax.ppermute(value, axis, pairs)


def routed_body(fresh, previous, norm_gain, routes, gate_weights, w_gate_up, w_down):
    devices_exp = lax.axis_size("expert")
    section_id = lax.axis_index("section")
    tok_dev = fresh.shape[0]
    width = fresh.shape[1]
    topk_count = routes.shape[2]
    local_experts = w_gate_up.shape[1]
    hidden_units = w_down.shape[2]
    experts_total = devices_exp * local_experts
    capacity = min(tok_dev, 17 * tok_dev * topk_count // (16 * experts_total))
    total_rows = tok_dev * topk_count
    arrived = from_behind(previous[0], "section", 1)
    arrival = jnp.where(section_id == 0, fresh, arrived)
    wide_input = arrival.astype(jnp.float32)
    scale = lax.rsqrt(jnp.mean(wide_input * wide_input, axis=-1, keepdims=True) + epsilon)
    normed = (wide_input * scale * norm_gain[0][None, :]).astype(jnp.bfloat16)
    flat_ids = routes[0].reshape(-1)
    one_hot = (flat_ids[:, None] == jnp.arange(experts_total, dtype=jnp.int32)[None, :]).astype(
        jnp.int32
    )
    slot_rank = jnp.sum(jnp.cumsum(one_hot, axis=0) * one_hot, axis=1) - 1
    position = flat_ids * capacity + slot_rank
    source_row = (
        jnp.full((experts_total * capacity,), total_rows, jnp.int32)
        .at[position]
        .set(jnp.arange(total_rows, dtype=jnp.int32))
    )
    padded = jnp.concatenate([normed, jnp.zeros((1, width), jnp.bfloat16)], axis=0)
    send_buffer = padded[source_row // topk_count].reshape(
        devices_exp, local_experts, capacity, width
    )
    received = lax.all_to_all(send_buffer, "expert", split_axis=0, concat_axis=0, tiled=True)
    projected = jnp.einsum(
        "secd,edf->secf", received, w_gate_up[0], preferred_element_type=jnp.float32
    )
    hidden = (jax.nn.silu(projected[..., :hidden_units]) * projected[..., hidden_units:]).astype(
        jnp.bfloat16
    )
    returned = lax.all_to_all(
        jnp.einsum("secf,efd->secd", hidden, w_down[0], preferred_element_type=jnp.float32).astype(
            jnp.bfloat16
        ),
        "expert",
        split_axis=0,
        concat_axis=0,
        tiled=True,
    )
    flat_back = returned.reshape(experts_total * capacity, width)
    picked = flat_back[position].reshape(tok_dev, topk_count, width).astype(jnp.float32)
    mixed = jnp.sum(picked * gate_weights[0][:, :, None], axis=1)
    return (wide_input + mixed).astype(jnp.bfloat16)[None]


def normed_rows(rows, gain):
    wide = rows.astype(jnp.float32)
    scale = lax.rsqrt(jnp.mean(wide * wide, axis=-1, keepdims=True) + epsilon)
    return (wide * scale * gain).astype(jnp.bfloat16)


def base_kernel(fresh_ref, gain_ref, routes_ref, gates_ref, rows_ref, coefs_ref, fresh_out_ref, gain_out_ref):
    rows_ref[...] = normed_rows(fresh_ref[...], gain_ref[...])
    shape = coefs_ref.shape[1:]
    expert = lax.broadcasted_iota(jnp.int32, shape, 0)
    weight = jnp.zeros(shape, jnp.float32)
    for k in range(routes_ref.shape[0]):
        weight += jnp.where(routes_ref[k : k + 1, :] == expert, gates_ref[k : k + 1, :], 0.0)
    high = weight.astype(jnp.bfloat16).astype(jnp.float32)
    low = weight - high
    left = lax.broadcasted_iota(jnp.int32, shape, 1) < HALF
    coefs_ref[0] = jnp.where(left, high, pltpu.roll(low, HALF, 1)).astype(jnp.bfloat16)
    coefs_ref[1] = jnp.where(left, pltpu.roll(high, HALF, 1), low).astype(jnp.bfloat16)
    fresh_out_ref[...] = fresh_ref[...]
    gain_out_ref[...] = gain_ref[...]


def base_rows(fresh, gain, routes, gates, experts):
    rows, width = fresh.shape
    vmem = pl.BlockSpec(memory_space=pltpu.VMEM)
    return pl.pallas_call(
        base_kernel,
        out_shape=(
            jax.ShapeDtypeStruct((rows, width), jnp.bfloat16),
            jax.ShapeDtypeStruct((2, experts, rows), jnp.bfloat16),
            jax.ShapeDtypeStruct(fresh.shape, fresh.dtype),
            jax.ShapeDtypeStruct(gain.shape, jnp.float32),
        ),
        in_specs=[vmem] * 4,
        out_specs=(vmem,) * 4,
        compiler_params=pltpu.CompilerParams(vmem_limit_bytes=12 * MIB),
        cost_estimate=pl.CostEstimate(flops=rows * width * 6, bytes_accessed=rows * width * 8, transcendentals=rows),
        name="base_rows",
    )(fresh, gain, routes, gates)


def norm_kernel(section_ref, base_ref, coefs_ref, fresh_ref, arrived_ref, gain_ref, rows_ref, arrival_ref, *, chunk):
    rows, width = arrived_ref.shape
    here = slice(chunk * rows, (chunk + 1) * rows)

    def pack(normed):
        for i in range(width // LANES):
            rows_ref[i * rows : (i + 1) * rows, :] = normed[:, i * LANES : (i + 1) * LANES]

    @pl.when(section_ref[0] == 0)
    def _():
        pack(base_ref[here, :])
        arrival_ref[...] = fresh_ref[here, :]

    @pl.when(section_ref[0] != 0)
    def _():
        pack(normed_rows(arrived_ref[...], gain_ref[...]))
        arrival_ref[...] = arrived_ref[...]

    rows_ref[rows * (width // LANES) :, :] = coefs_ref[chunk]


def norm_rows(section_id, base, coefs, fresh, arrived, gain, chunk):
    rows, width = arrived.shape
    vmem = pl.BlockSpec(memory_space=pltpu.VMEM)
    return pl.pallas_call(
        functools.partial(norm_kernel, chunk=chunk),
        out_shape=(
            jax.ShapeDtypeStruct((rows * (width // LANES) + coefs.shape[1], LANES), jnp.bfloat16),
            jax.ShapeDtypeStruct((rows, width), jnp.bfloat16),
        ),
        in_specs=[pl.BlockSpec(memory_space=pltpu.SMEM)] + [vmem] * 5,
        out_specs=(vmem, vmem),
        compiler_params=pltpu.CompilerParams(vmem_limit_bytes=12 * MIB),
        cost_estimate=pl.CostEstimate(flops=rows * width * 6, bytes_accessed=rows * width * 8, transcendentals=rows),
        name="norm_rows",
    )(section_id, base, coefs, fresh, arrived, gain)


def mlp_kernel(expert_ref, *refs, parts, adds, chained, core, given):
    payloads = refs[:parts]
    weights = (refs[parts : parts + 2], refs[parts + 2 : parts + 4])
    refs = refs[parts + 4 :]
    terms, totals = refs[:adds], refs[adds : 2 * adds]
    earlier, refs = refs[2 * adds : 2 * adds + given], refs[2 * adds + given + chained :]
    outs, added = refs[:parts], refs[parts : parts + adds]
    x_ref, coef_ref, hidden_ref = refs[parts + adds :]
    for term, total, result in zip(terms, totals, added):
        result[...] = (term[...] + total[...].astype(jnp.float32)).astype(jnp.bfloat16)

    def experts():
        width = x_ref.shape[1]
        hidden = weights[0][1].shape[0]
        line = lax.broadcasted_iota(jnp.int32, (HALF, LANES), 0)
        token = line == lax.broadcasted_iota(jnp.int32, (HALF, LANES), 1) % HALF
        bounds = []
        for part, payload in enumerate(payloads):
            here = slice(part * HALF, (part + 1) * HALF)
            bounds.append(here)
            for i in range(width // LANES):
                x_ref[here, i * LANES : (i + 1) * LANES] = payload[i * HALF : (i + 1) * HALF, :]
            block = payload[HALF * (width // LANES) :, :].astype(jnp.float32)
            expert = lax.broadcasted_iota(jnp.int32, block.shape, 0)
            for which in range(2):
                terms = jnp.sum(jnp.where(expert == expert_ref[0] ^ which, block, 0.0), axis=0, keepdims=True)
                value = jnp.sum(jnp.where(token, terms, 0.0), axis=1, keepdims=True)
                coef_ref[which, here, :] = jnp.broadcast_to(value, (HALF, LANES))
        tile = 256
        for which, (gate_up, _) in enumerate(weights):
            for t in range(0, hidden, tile):
                gate = jnp.dot(x_ref[...], gate_up[:, t : t + tile], preferred_element_type=jnp.float32)
                up = jnp.dot(x_ref[...], gate_up[:, hidden + t : hidden + t + tile], preferred_element_type=jnp.float32)
                value = jax.nn.silu(gate) * up * coef_ref[which][:, :1]
                hidden_ref[:, which * hidden + t : which * hidden + t + tile] = value.astype(jnp.bfloat16)
        tile = 512
        for t in range(0, width, tile):
            total = jnp.zeros((x_ref.shape[0], tile), jnp.float32)
            for which, (_, down) in enumerate(weights):
                rows = hidden_ref[:, which * hidden : (which + 1) * hidden]
                total += jnp.dot(rows, down[:, t : t + tile], preferred_element_type=jnp.float32)
            for here, out in zip(bounds, outs):
                out[:, t : t + tile] = total[here, :]

    if core is None:
        experts()
    else:
        here = expert_ref[0] % CORES == core
        pl.when(here)(experts)

        @pl.when(jnp.logical_not(here))
        def _():
            for source, out in zip(earlier, outs):
                out[...] = source[...]


def expert_rows(expert_id, payloads, own, other, after, terms=(), totals=(), core=None, earlier=()):
    width = own[0].shape[0]
    hidden = own[1].shape[0]
    rows = HALF * len(payloads)
    vmem = pl.BlockSpec(memory_space=pltpu.VMEM)
    chain = [] if after is None else [after]
    return pl.pallas_call(
        functools.partial(
            mlp_kernel, parts=len(payloads), adds=len(terms), chained=len(chain), core=core, given=len(earlier)
        ),
        out_shape=[jax.ShapeDtypeStruct((HALF, width), jnp.float32)] * len(payloads)
        + [jax.ShapeDtypeStruct((HALF, width), jnp.bfloat16)] * len(terms),
        in_specs=[pl.BlockSpec(memory_space=pltpu.SMEM)]
        + [vmem] * (len(payloads) + 4 + 2 * len(terms) + len(earlier))
        + [pl.BlockSpec(memory_space=pl.ANY)] * len(chain),
        out_specs=[vmem] * (len(payloads) + len(terms)),
        scratch_shapes=[
            pltpu.VMEM((rows, width), jnp.bfloat16),
            pltpu.VMEM((2, rows, LANES), jnp.float32),
            pltpu.VMEM((rows, 2 * hidden), jnp.bfloat16),
        ],
        compiler_params=pltpu.CompilerParams(vmem_limit_bytes=16 * MIB),
        cost_estimate=pl.CostEstimate(
            flops=2 * rows * width * hidden * 6,
            bytes_accessed=rows * width * 6,
            transcendentals=rows * hidden * 2,
        ),
        name="expert_rows",
    )(expert_id, *payloads, *own, *other, *terms, *totals, *earlier, *chain)


def last_kernel(near0_ref, near1_ref, total0_ref, total1_ref, out_ref):
    half = near0_ref.shape[0]
    for start, near_ref, total_ref in ((0, near0_ref, total0_ref), (half, near1_ref, total1_ref)):
        total = near_ref[...] + total_ref[...].astype(jnp.float32)
        out_ref[start : start + half, :] = total.astype(jnp.bfloat16)


def last_rows(nears, totals):
    rows, width = nears[0].shape
    vmem = pl.BlockSpec(memory_space=pltpu.VMEM)
    return pl.pallas_call(
        last_kernel,
        out_shape=jax.ShapeDtypeStruct((2 * rows, width), jnp.bfloat16),
        in_specs=[vmem] * 4,
        out_specs=vmem,
        compiler_params=pltpu.CompilerParams(vmem_limit_bytes=8 * MIB),
        cost_estimate=pl.CostEstimate(flops=2 * rows * width, bytes_accessed=rows * width * 16, transcendentals=0),
        name="last_rows",
    )(*nears, *totals)


def chip_ring(depth, across):
    walk = []
    for z in range(depth):
        xs = list(range(1, across))
        walk += [(z, x) for x in (xs if z % 2 == 0 else xs[::-1])]
    return [z * across + x for z, x in walk + [(z, 0) for z in reversed(range(depth))]]


def relay_body(fresh, previous, norm_gain, routes, gate_weights, w_gate_up, w_down, *, across):
    devices_exp = lax.axis_size("expert")
    section_id = lax.axis_index("section").astype(jnp.int32).reshape(1)
    expert_id = lax.axis_index("expert").astype(jnp.int32).reshape(1)
    rows = fresh.shape[0]
    half = HALF
    chips = devices_exp // CORES
    ring = chip_ring(chips // across, across)
    links = list(zip(ring, ring[1:] + ring[:1]))
    up = [(a * CORES + c, b * CORES + c) for a, b in links for c in range(CORES)]
    down = [(b, a) for a, b in up]
    swap = [(i, i ^ 1) for i in range(devices_exp)]

    def move(value, pairs):
        return lax.ppermute(value, "expert", pairs)

    cuts = [slice(0, half), slice(half, rows)]
    own = (w_gate_up[0, 0], w_down[0, 0])
    swapped = lax.optimization_barrier((*own, section_id, expert_id))[:2]
    other = tuple(move(w, swap) for w in swapped)
    base, coefs, fresh, gain = base_rows(fresh, norm_gain, routes[0].T, gate_weights[0].T, devices_exp)
    arrived = [from_behind(previous[0, cut], "section", 1) for cut in cuts]
    packed, arrival = zip(*(norm_rows(section_id, base, coefs, fresh, arrived[c], gain, c) for c in range(2)))
    packed = list(packed)

    hops = chips // 2
    ups = [packed] + [[None, None] for _ in range(hops)]
    downs = [packed] + [[None, None] for _ in range(hops)]

    def pass_on(s, c, after):
        rising, falling = lax.optimization_barrier((ups[s][c], downs[s][c], after))[:2]
        if s < hops - 1 or c == 0:
            ups[s + 1][c] = move(rising, up)
        if s < hops - 1 or c == 1:
            downs[s + 1][c] = move(falling, down)

    last = None

    def mlp(payloads, *args):
        nonlocal last
        sums = expert_rows(expert_id, payloads, own, other, last, *args)
        last = sums[0]
        return sums

    to_down, to_up = {}, {}
    pass_on(0, 0, None)
    pass_on(0, 1, other)
    for s in range(1, hops):
        for c in range(2):
            pass_on(s, c, last)
            to_down[s, c], to_up[s, c] = mlp([ups[s][c], downs[s][c]])
    early_sums = mlp(packed, (), (), 1)
    to_up[hops, 0], to_down[hops, 1] = mlp([ups[hops][0], downs[hops][1]])

    def send_on(flow, place, total, after):
        terms, c, pairs = flow
        if total is None:
            total = lax.optimization_barrier((terms[place, c], after))[0]
        else:
            carried = lax.optimization_barrier((total, after))[0]
            total = terms[place, c] + carried.astype(jnp.float32)
        total = total.astype(jnp.bfloat16)
        return total, move(total, pairs)

    short = [(to_down, 0, down), (to_up, 1, up)]
    long = [(to_up, 0, up), (to_down, 1, down)]
    short_totals = [send_on(flow, hops - 1, None, to_up[hops - 1, 1])[1] for flow in short]
    long_totals = [send_on(flow, hops, None, None)[1] for flow in long]
    *own_sums, down_sum, up_sum = mlp(packed, [f[0][hops - 2, f[1]] for f in short], short_totals, 0, early_sums)
    short_totals = [move(total, flow[2]) for total, flow in zip((down_sum, up_sum), short)]
    after = None
    for s in reversed(range(1, hops)):
        sent, long_totals = zip(*(send_on(f, s, t, None) for f, t in zip(long, long_totals)))
        if 1 < s < hops - 1:
            short_totals = [send_on(f, s - 1, t, sent)[1] for f, t in zip(short, short_totals)]

    nears = [
        arrival[c].astype(jnp.float32) + (own_sums[c] + short_totals[c].astype(jnp.float32)) for c in range(2)
    ]
    nears = lax.optimization_barrier(nears)
    return last_rows(nears, long_totals)[None]


def solution(mesh):
    across = mesh.shape["section"]
    devices_exp = mesh.shape["expert"]

    def body(*args):
        topk_count, local_experts = args[3].shape[2], args[5].shape[1]
        regular = devices_exp % (2 * CORES * across) == 0 and devices_exp >= 6 * CORES and devices_exp % 16 == 0 and args[0].shape[0] == LANES
        if local_experts == 1 and devices_exp <= 2 * topk_count and regular:
            return relay_body(*args, across=across)
        return routed_body(*args)

    return jax.shard_map(
        body,
        mesh=mesh,
        in_specs=(
            P("expert", None),
            P("section", "expert", None),
            P("section", None),
            P("section", "expert", None),
            P("section", "expert", None),
            P("section", "expert", None, None),
            P("section", "expert", None, None),
        ),
        out_specs=P("section", "expert", None),
        check_vma=False,
    )
```

```python
import functools

import jax
import jax.numpy as jnp
from jax import lax
from jax.experimental import pallas as pl
from jax.experimental.pallas import tpu as pltpu
from jax.sharding import PartitionSpec as P

epsilon = 1e-06
LANES = 128
HALF = LANES // 2
CORES = 2
MIB = 1 << 20


def from_behind(value, axis, by):
    peers = lax.axis_size(axis)
    pairs = [(i, i + by) for i in range(peers) if 0 <= i + by < peers]
    return lax.ppermute(value, axis, pairs)


def routed_body(fresh, previous, norm_gain, routes, gate_weights, w_gate_up, w_down):
    devices_exp = lax.axis_size("expert")
    section_id = lax.axis_index("section")
    tok_dev = fresh.shape[0]
    width = fresh.shape[1]
    topk_count = routes.shape[2]
    local_experts = w_gate_up.shape[1]
    hidden_units = w_down.shape[2]
    experts_total = devices_exp * local_experts
    capacity = min(tok_dev, 17 * tok_dev * topk_count // (16 * experts_total))
    total_rows = tok_dev * topk_count
    arrived = from_behind(previous[0], "section", 1)
    arrival = jnp.where(section_id == 0, fresh, arrived)
    wide_input = arrival.astype(jnp.float32)
    scale = lax.rsqrt(jnp.mean(wide_input * wide_input, axis=-1, keepdims=True) + epsilon)
    normed = (wide_input * scale * norm_gain[0][None, :]).astype(jnp.bfloat16)
    flat_ids = routes[0].reshape(-1)
    one_hot = (flat_ids[:, None] == jnp.arange(experts_total, dtype=jnp.int32)[None, :]).astype(
        jnp.int32
    )
    slot_rank = jnp.sum(jnp.cumsum(one_hot, axis=0) * one_hot, axis=1) - 1
    position = flat_ids * capacity + slot_rank
    source_row = (
        jnp.full((experts_total * capacity,), total_rows, jnp.int32)
        .at[position]
        .set(jnp.arange(total_rows, dtype=jnp.int32))
    )
    padded = jnp.concatenate([normed, jnp.zeros((1, width), jnp.bfloat16)], axis=0)
    send_buffer = padded[source_row // topk_count].reshape(
        devices_exp, local_experts, capacity, width
    )
    received = lax.all_to_all(send_buffer, "expert", split_axis=0, concat_axis=0, tiled=True)
    projected = jnp.einsum(
        "secd,edf->secf", received, w_gate_up[0], preferred_element_type=jnp.float32
    )
    hidden = (jax.nn.silu(projected[..., :hidden_units]) * projected[..., hidden_units:]).astype(
        jnp.bfloat16
    )
    returned = lax.all_to_all(
        jnp.einsum("secf,efd->secd", hidden, w_down[0], preferred_element_type=jnp.float32).astype(
            jnp.bfloat16
        ),
        "expert",
        split_axis=0,
        concat_axis=0,
        tiled=True,
    )
    flat_back = returned.reshape(experts_total * capacity, width)
    picked = flat_back[position].reshape(tok_dev, topk_count, width).astype(jnp.float32)
    mixed = jnp.sum(picked * gate_weights[0][:, :, None], axis=1)
    return (wide_input + mixed).astype(jnp.bfloat16)[None]


def chunks_kernel(rows_ref, first_ref, second_ref, sems):
    half = first_ref.shape[0]
    copies = [
        pltpu.make_async_copy(rows_ref.at[i * half : (i + 1) * half, :], out_ref, sems.at[i])
        for i, out_ref in enumerate((first_ref, second_ref))
    ]
    for copy in copies:
        copy.start()
    for copy in copies:
        copy.wait()


def two_chunks(rows):
    half = jax.ShapeDtypeStruct((rows.shape[0] // 2, rows.shape[1]), rows.dtype)
    return pl.pallas_call(
        chunks_kernel,
        out_shape=(half, half),
        in_specs=[pl.BlockSpec(memory_space=pltpu.HBM)],
        out_specs=(pl.BlockSpec(memory_space=pltpu.HBM),) * 2,
        scratch_shapes=[pltpu.SemaphoreType.DMA((2,))],
        compiler_params=pltpu.CompilerParams(vmem_limit_bytes=60 * MIB),
        cost_estimate=pl.CostEstimate(flops=0, bytes_accessed=4 * half.size * 2, transcendentals=0),
        name="two_chunks",
    )(rows)


def normed_rows(rows, gain):
    wide = rows.astype(jnp.float32)
    scale = lax.rsqrt(jnp.mean(wide * wide, axis=-1, keepdims=True) + epsilon)
    return (wide * scale * gain).astype(jnp.bfloat16)


def base_kernel(fresh_ref, gain_ref, routes_ref, gates_ref, rows_ref, coefs_ref, fresh_out_ref, gain_out_ref):
    rows_ref[...] = normed_rows(fresh_ref[...], gain_ref[...])
    shape = coefs_ref.shape[1:]
    expert = lax.broadcasted_iota(jnp.int32, shape, 0)
    weight = jnp.zeros(shape, jnp.float32)
    for k in range(routes_ref.shape[0]):
        weight += jnp.where(routes_ref[k : k + 1, :] == expert, gates_ref[k : k + 1, :], 0.0)
    high = weight.astype(jnp.bfloat16).astype(jnp.float32)
    low = weight - high
    left = lax.broadcasted_iota(jnp.int32, shape, 1) < HALF
    coefs_ref[0] = jnp.where(left, high, pltpu.roll(low, HALF, 1)).astype(jnp.bfloat16)
    coefs_ref[1] = jnp.where(left, pltpu.roll(high, HALF, 1), low).astype(jnp.bfloat16)
    fresh_out_ref[...] = fresh_ref[...]
    gain_out_ref[...] = gain_ref[...]


def base_rows(fresh, gain, routes, gates, experts):
    rows, width = fresh.shape
    vmem = pl.BlockSpec(memory_space=pltpu.VMEM)
    return pl.pallas_call(
        base_kernel,
        out_shape=(
            jax.ShapeDtypeStruct((rows, width), jnp.bfloat16),
            jax.ShapeDtypeStruct((2, experts, rows), jnp.bfloat16),
            jax.ShapeDtypeStruct(fresh.shape, fresh.dtype),
            jax.ShapeDtypeStruct(gain.shape, jnp.float32),
        ),
        in_specs=[vmem] * 4,
        out_specs=(vmem,) * 4,
        compiler_params=pltpu.CompilerParams(vmem_limit_bytes=12 * MIB),
        cost_estimate=pl.CostEstimate(flops=rows * width * 6, bytes_accessed=rows * width * 8, transcendentals=rows),
        name="base_rows",
    )(fresh, gain, routes, gates)


def norm_kernel(section_ref, base_ref, coefs_ref, fresh_ref, arrived_ref, gain_ref, rows_ref, arrival_ref, *, chunk):
    rows, width = arrived_ref.shape
    here = slice(chunk * rows, (chunk + 1) * rows)

    def pack(normed):
        for i in range(width // LANES):
            rows_ref[i * rows : (i + 1) * rows, :] = normed[:, i * LANES : (i + 1) * LANES]

    @pl.when(section_ref[0] == 0)
    def _():
        pack(base_ref[here, :])
        arrival_ref[...] = fresh_ref[here, :]

    @pl.when(section_ref[0] != 0)
    def _():
        pack(normed_rows(arrived_ref[...], gain_ref[...]))
        arrival_ref[...] = arrived_ref[...]

    rows_ref[rows * (width // LANES) :, :] = coefs_ref[chunk]


def norm_rows(section_id, base, coefs, fresh, arrived, gain, chunk):
    rows, width = arrived.shape
    vmem = pl.BlockSpec(memory_space=pltpu.VMEM)
    return pl.pallas_call(
        functools.partial(norm_kernel, chunk=chunk),
        out_shape=(
            jax.ShapeDtypeStruct((rows * (width // LANES) + coefs.shape[1], LANES), jnp.bfloat16),
            jax.ShapeDtypeStruct((rows, width), jnp.bfloat16),
        ),
        in_specs=[pl.BlockSpec(memory_space=pltpu.SMEM)] + [vmem] * 5,
        out_specs=(vmem, vmem),
        compiler_params=pltpu.CompilerParams(vmem_limit_bytes=12 * MIB),
        cost_estimate=pl.CostEstimate(flops=rows * width * 6, bytes_accessed=rows * width * 8, transcendentals=rows),
        name="norm_rows",
    )(section_id, base, coefs, fresh, arrived, gain)


def mlp_kernel(expert_ref, *refs, parts, adds, chained, core, given):
    payloads = refs[:parts]
    weights = (refs[parts : parts + 2], refs[parts + 2 : parts + 4])
    refs = refs[parts + 4 :]
    terms, totals = refs[:adds], refs[adds : 2 * adds]
    earlier, refs = refs[2 * adds : 2 * adds + given], refs[2 * adds + given + chained :]
    outs, added = refs[:parts], refs[parts : parts + adds]
    x_ref, coef_ref, hidden_ref = refs[parts + adds :]
    for term, total, result in zip(terms, totals, added):
        result[...] = (term[...] + total[...].astype(jnp.float32)).astype(jnp.bfloat16)

    def experts():
        width = x_ref.shape[1]
        hidden = weights[0][1].shape[0]
        line = lax.broadcasted_iota(jnp.int32, (HALF, LANES), 0)
        token = line == lax.broadcasted_iota(jnp.int32, (HALF, LANES), 1) % HALF
        bounds = []
        for part, payload in enumerate(payloads):
            here = slice(part * HALF, (part + 1) * HALF)
            bounds.append(here)
            for i in range(width // LANES):
                x_ref[here, i * LANES : (i + 1) * LANES] = payload[i * HALF : (i + 1) * HALF, :]
            block = payload[HALF * (width // LANES) :, :].astype(jnp.float32)
            expert = lax.broadcasted_iota(jnp.int32, block.shape, 0)
            for which in range(2):
                terms = jnp.sum(jnp.where(expert == expert_ref[0] ^ which, block, 0.0), axis=0, keepdims=True)
                value = jnp.sum(jnp.where(token, terms, 0.0), axis=1, keepdims=True)
                coef_ref[which, here, :] = jnp.broadcast_to(value, (HALF, LANES))
        tile = 256
        for which, (gate_up, _) in enumerate(weights):
            for t in range(0, hidden, tile):
                gate = jnp.dot(x_ref[...], gate_up[:, t : t + tile], preferred_element_type=jnp.float32)
                up = jnp.dot(x_ref[...], gate_up[:, hidden + t : hidden + t + tile], preferred_element_type=jnp.float32)
                value = jax.nn.silu(gate) * up * coef_ref[which][:, :1]
                hidden_ref[:, which * hidden + t : which * hidden + t + tile] = value.astype(jnp.bfloat16)
        tile = 512
        for t in range(0, width, tile):
            total = jnp.zeros((x_ref.shape[0], tile), jnp.float32)
            for which, (_, down) in enumerate(weights):
                rows = hidden_ref[:, which * hidden : (which + 1) * hidden]
                total += jnp.dot(rows, down[:, t : t + tile], preferred_element_type=jnp.float32)
            for here, out in zip(bounds, outs):
                out[:, t : t + tile] = total[here, :]

    if core is None:
        experts()
    else:
        here = expert_ref[0] % CORES == core
        pl.when(here)(experts)

        @pl.when(jnp.logical_not(here))
        def _():
            for source, out in zip(earlier, outs):
                out[...] = source[...]


def expert_rows(expert_id, payloads, own, other, after, terms=(), totals=(), core=None, earlier=()):
    width = own[0].shape[0]
    hidden = own[1].shape[0]
    rows = HALF * len(payloads)
    vmem = pl.BlockSpec(memory_space=pltpu.VMEM)
    chain = [] if after is None else [after]
    return pl.pallas_call(
        functools.partial(
            mlp_kernel, parts=len(payloads), adds=len(terms), chained=len(chain), core=core, given=len(earlier)
        ),
        out_shape=[jax.ShapeDtypeStruct((HALF, width), jnp.float32)] * len(payloads)
        + [jax.ShapeDtypeStruct((HALF, width), jnp.bfloat16)] * len(terms),
        in_specs=[pl.BlockSpec(memory_space=pltpu.SMEM)]
        + [vmem] * (len(payloads) + 4 + 2 * len(terms) + len(earlier))
        + [pl.BlockSpec(memory_space=pl.ANY)] * len(chain),
        out_specs=[vmem] * (len(payloads) + len(terms)),
        scratch_shapes=[
            pltpu.VMEM((rows, width), jnp.bfloat16),
            pltpu.VMEM((2, rows, LANES), jnp.float32),
            pltpu.VMEM((rows, 2 * hidden), jnp.bfloat16),
        ],
        compiler_params=pltpu.CompilerParams(vmem_limit_bytes=16 * MIB),
        cost_estimate=pl.CostEstimate(
            flops=2 * rows * width * hidden * 6,
            bytes_accessed=rows * width * 6,
            transcendentals=rows * hidden * 2,
        ),
        name="expert_rows",
    )(expert_id, *payloads, *own, *other, *terms, *totals, *earlier, *chain)


def last_kernel(near0_ref, near1_ref, total0_ref, total1_ref, out_ref):
    half = near0_ref.shape[0]
    for start, near_ref, total_ref in ((0, near0_ref, total0_ref), (half, near1_ref, total1_ref)):
        total = near_ref[...] + total_ref[...].astype(jnp.float32)
        out_ref[start : start + half, :] = total.astype(jnp.bfloat16)


def last_rows(nears, totals):
    rows, width = nears[0].shape
    vmem = pl.BlockSpec(memory_space=pltpu.VMEM)
    return pl.pallas_call(
        last_kernel,
        out_shape=jax.ShapeDtypeStruct((2 * rows, width), jnp.bfloat16),
        in_specs=[vmem] * 4,
        out_specs=vmem,
        compiler_params=pltpu.CompilerParams(vmem_limit_bytes=8 * MIB),
        cost_estimate=pl.CostEstimate(flops=2 * rows * width, bytes_accessed=rows * width * 16, transcendentals=0),
        name="last_rows",
    )(*nears, *totals)


def chip_ring(depth, across):
    walk = []
    for z in range(depth):
        xs = list(range(1, across))
        walk += [(z, x) for x in (xs if z % 2 == 0 else xs[::-1])]
    return [z * across + x for z, x in walk + [(z, 0) for z in reversed(range(depth))]]


def relay_body(fresh, previous, norm_gain, routes, gate_weights, w_gate_up, w_down, *, across):
    devices_exp = lax.axis_size("expert")
    section_id = lax.axis_index("section").astype(jnp.int32).reshape(1)
    expert_id = lax.axis_index("expert").astype(jnp.int32).reshape(1)
    rows = fresh.shape[0]
    half = HALF
    chips = devices_exp // CORES
    ring = chip_ring(chips // across, across)
    links = list(zip(ring, ring[1:] + ring[:1]))
    up = [(a * CORES + c, b * CORES + c) for a, b in links for c in range(CORES)]
    down = [(b, a) for a, b in up]
    swap = [(i, i ^ 1) for i in range(devices_exp)]

    def move(value, pairs):
        return lax.ppermute(value, "expert", pairs)

    cuts = [slice(0, half), slice(half, rows)]
    own = (w_gate_up[0, 0], w_down[0, 0])
    leaving = two_chunks(previous[0])
    swapped = lax.optimization_barrier((*own, section_id, expert_id, leaving))[:2]
    other = tuple(move(w, swap) for w in swapped)
    base, coefs, fresh, gain = base_rows(fresh, norm_gain, routes[0].T, gate_weights[0].T, devices_exp)
    arrived = [from_behind(chunk, "section", 1) for chunk in leaving]
    packed, arrival = zip(*(norm_rows(section_id, base, coefs, fresh, arrived[c], gain, c) for c in range(2)))
    packed = list(packed)

    hops = chips // 2
    ups = [packed] + [[None, None] for _ in range(hops)]
    downs = [packed] + [[None, None] for _ in range(hops)]

    def pass_on(s, c, after):
        rising, falling = lax.optimization_barrier((ups[s][c], downs[s][c], after))[:2]
        if s < hops - 1 or c == 0:
            ups[s + 1][c] = move(rising, up)
        if s < hops - 1 or c == 1:
            downs[s + 1][c] = move(falling, down)

    last = None

    def mlp(payloads, *args):
        nonlocal last
        sums = expert_rows(expert_id, payloads, own, other, last, *args)
        last = sums[0]
        return sums

    to_down, to_up = {}, {}
    pass_on(0, 0, None)
    pass_on(0, 1, other)
    for s in range(1, hops):
        for c in range(2):
            pass_on(s, c, last)
            to_down[s, c], to_up[s, c] = mlp([ups[s][c], downs[s][c]])
    early_sums = mlp(packed, (), (), 1)
    to_up[hops, 0], to_down[hops, 1] = mlp([ups[hops][0], downs[hops][1]])

    def send_on(flow, place, total, after):
        terms, c, pairs = flow
        if total is None:
            total = lax.optimization_barrier((terms[place, c], after))[0]
        else:
            carried = lax.optimization_barrier((total, after))[0]
            total = terms[place, c] + carried.astype(jnp.float32)
        total = total.astype(jnp.bfloat16)
        return total, move(total, pairs)

    short = [(to_down, 0, down), (to_up, 1, up)]
    long = [(to_up, 0, up), (to_down, 1, down)]
    short_totals = [send_on(flow, hops - 1, None, to_up[hops - 1, 1])[1] for flow in short]
    long_totals = [send_on(flow, hops, None, None)[1] for flow in long]
    *own_sums, down_sum, up_sum = mlp(packed, [f[0][hops - 2, f[1]] for f in short], short_totals, 0, early_sums)
    short_totals = [move(total, flow[2]) for total, flow in zip((down_sum, up_sum), short)]
    after = None
    for s in reversed(range(1, hops)):
        sent, long_totals = zip(*(send_on(f, s, t, None) for f, t in zip(long, long_totals)))
        if 1 < s < hops - 1:
            short_totals = [send_on(f, s - 1, t, sent)[1] for f, t in zip(short, short_totals)]

    nears = [
        arrival[c].astype(jnp.float32) + (own_sums[c] + short_totals[c].astype(jnp.float32)) for c in range(2)
    ]
    nears = lax.optimization_barrier(nears)
    return last_rows(nears, long_totals)[None]


def solution(mesh):
    across = mesh.shape["section"]
    devices_exp = mesh.shape["expert"]

    def body(*args):
        topk_count, local_experts = args[3].shape[2], args[5].shape[1]
        regular = devices_exp % (2 * CORES * across) == 0 and devices_exp >= 6 * CORES and devices_exp % 16 == 0 and args[0].shape[0] == LANES
        if local_experts == 1 and devices_exp <= 2 * topk_count and regular:
            return relay_body(*args, across=across)
        return routed_body(*args)

    return jax.shard_map(
        body,
        mesh=mesh,
        in_specs=(
            P("expert", None),
            P("section", "expert", None),
            P("section", None),
            P("section", "expert", None),
            P("section", "expert", None),
            P("section", "expert", None, None),
            P("section", "expert", None, None),
        ),
        out_specs=P("section", "expert", None),
        check_vma=False,
    )
```

```python
import functools

import jax
import jax.numpy as jnp
from jax import lax
from jax.experimental import pallas as pl
from jax.experimental.pallas import tpu as pltpu
from jax.sharding import PartitionSpec as P

epsilon = 1e-06
LANES = 128
HALF = LANES // 2
CORES = 2
MIB = 1 << 20


def from_behind(value, axis, by):
    peers = lax.axis_size(axis)
    pairs = [(i, i + by) for i in range(peers) if 0 <= i + by < peers]
    return lax.ppermute(value, axis, pairs)


def routed_body(fresh, previous, norm_gain, routes, gate_weights, w_gate_up, w_down):
    devices_exp = lax.axis_size("expert")
    section_id = lax.axis_index("section")
    tok_dev = fresh.shape[0]
    width = fresh.shape[1]
    topk_count = routes.shape[2]
    local_experts = w_gate_up.shape[1]
    hidden_units = w_down.shape[2]
    experts_total = devices_exp * local_experts
    capacity = min(tok_dev, 17 * tok_dev * topk_count // (16 * experts_total))
    total_rows = tok_dev * topk_count
    arrived = from_behind(previous[0], "section", 1)
    arrival = jnp.where(section_id == 0, fresh, arrived)
    wide_input = arrival.astype(jnp.float32)
    scale = lax.rsqrt(jnp.mean(wide_input * wide_input, axis=-1, keepdims=True) + epsilon)
    normed = (wide_input * scale * norm_gain[0][None, :]).astype(jnp.bfloat16)
    flat_ids = routes[0].reshape(-1)
    one_hot = (flat_ids[:, None] == jnp.arange(experts_total, dtype=jnp.int32)[None, :]).astype(
        jnp.int32
    )
    slot_rank = jnp.sum(jnp.cumsum(one_hot, axis=0) * one_hot, axis=1) - 1
    position = flat_ids * capacity + slot_rank
    source_row = (
        jnp.full((experts_total * capacity,), total_rows, jnp.int32)
        .at[position]
        .set(jnp.arange(total_rows, dtype=jnp.int32))
    )
    padded = jnp.concatenate([normed, jnp.zeros((1, width), jnp.bfloat16)], axis=0)
    send_buffer = padded[source_row // topk_count].reshape(
        devices_exp, local_experts, capacity, width
    )
    received = lax.all_to_all(send_buffer, "expert", split_axis=0, concat_axis=0, tiled=True)
    projected = jnp.einsum(
        "secd,edf->secf", received, w_gate_up[0], preferred_element_type=jnp.float32
    )
    hidden = (jax.nn.silu(projected[..., :hidden_units]) * projected[..., hidden_units:]).astype(
        jnp.bfloat16
    )
    returned = lax.all_to_all(
        jnp.einsum("secf,efd->secd", hidden, w_down[0], preferred_element_type=jnp.float32).astype(
            jnp.bfloat16
        ),
        "expert",
        split_axis=0,
        concat_axis=0,
        tiled=True,
    )
    flat_back = returned.reshape(experts_total * capacity, width)
    picked = flat_back[position].reshape(tok_dev, topk_count, width).astype(jnp.float32)
    mixed = jnp.sum(picked * gate_weights[0][:, :, None], axis=1)
    return (wide_input + mixed).astype(jnp.bfloat16)[None]


def normed_rows(rows, gain):
    wide = rows.astype(jnp.float32)
    scale = lax.rsqrt(jnp.mean(wide * wide, axis=-1, keepdims=True) + epsilon)
    return (wide * scale * gain).astype(jnp.bfloat16)


def base_kernel(fresh_ref, gain_ref, routes_ref, gates_ref, rows_ref, coefs_ref, fresh_out_ref, gain_out_ref):
    rows_ref[...] = normed_rows(fresh_ref[...], gain_ref[...])
    shape = coefs_ref.shape[1:]
    expert = lax.broadcasted_iota(jnp.int32, shape, 0)
    weight = jnp.zeros(shape, jnp.float32)
    for k in range(routes_ref.shape[0]):
        weight += jnp.where(routes_ref[k : k + 1, :] == expert, gates_ref[k : k + 1, :], 0.0)
    high = weight.astype(jnp.bfloat16).astype(jnp.float32)
    low = weight - high
    left = lax.broadcasted_iota(jnp.int32, shape, 1) < HALF
    coefs_ref[0] = jnp.where(left, high, pltpu.roll(low, HALF, 1)).astype(jnp.bfloat16)
    coefs_ref[1] = jnp.where(left, pltpu.roll(high, HALF, 1), low).astype(jnp.bfloat16)
    fresh_out_ref[...] = fresh_ref[...]
    gain_out_ref[...] = gain_ref[...]


def base_rows(fresh, gain, routes, gates, experts):
    rows, width = fresh.shape
    vmem = pl.BlockSpec(memory_space=pltpu.VMEM)
    return pl.pallas_call(
        base_kernel,
        out_shape=(
            jax.ShapeDtypeStruct((rows, width), jnp.bfloat16),
            jax.ShapeDtypeStruct((2, experts, rows), jnp.bfloat16),
            jax.ShapeDtypeStruct(fresh.shape, fresh.dtype),
            jax.ShapeDtypeStruct(gain.shape, jnp.float32),
        ),
        in_specs=[vmem] * 4,
        out_specs=(vmem,) * 4,
        compiler_params=pltpu.CompilerParams(vmem_limit_bytes=12 * MIB),
        cost_estimate=pl.CostEstimate(flops=rows * width * 6, bytes_accessed=rows * width * 8, transcendentals=rows),
        name="base_rows",
    )(fresh, gain, routes, gates)


def norm_kernel(section_ref, base_ref, coefs_ref, fresh_ref, arrived_ref, gain_ref, rows_ref, arrival_ref, *, chunk):
    rows, width = arrived_ref.shape
    here = slice(chunk * rows, (chunk + 1) * rows)

    def pack(normed):
        for i in range(width // LANES):
            rows_ref[i * rows : (i + 1) * rows, :] = normed[:, i * LANES : (i + 1) * LANES]

    @pl.when(section_ref[0] == 0)
    def _():
        pack(base_ref[here, :])
        arrival_ref[...] = fresh_ref[here, :]

    @pl.when(section_ref[0] != 0)
    def _():
        pack(normed_rows(arrived_ref[...], gain_ref[...]))
        arrival_ref[...] = arrived_ref[...]

    rows_ref[rows * (width // LANES) :, :] = coefs_ref[chunk]


def norm_rows(section_id, base, coefs, fresh, arrived, gain, chunk):
    rows, width = arrived.shape
    vmem = pl.BlockSpec(memory_space=pltpu.VMEM)
    return pl.pallas_call(
        functools.partial(norm_kernel, chunk=chunk),
        out_shape=(
            jax.ShapeDtypeStruct((rows * (width // LANES) + coefs.shape[1], LANES), jnp.bfloat16),
            jax.ShapeDtypeStruct((rows, width), jnp.bfloat16),
        ),
        in_specs=[pl.BlockSpec(memory_space=pltpu.SMEM)] + [vmem] * 5,
        out_specs=(vmem, vmem),
        compiler_params=pltpu.CompilerParams(vmem_limit_bytes=12 * MIB),
        cost_estimate=pl.CostEstimate(flops=rows * width * 6, bytes_accessed=rows * width * 8, transcendentals=rows),
        name="norm_rows",
    )(section_id, base, coefs, fresh, arrived, gain)


def mlp_kernel(expert_ref, *refs, parts, adds, chained, core, given):
    payloads = refs[:parts]
    weights = (refs[parts : parts + 2], refs[parts + 2 : parts + 4])
    refs = refs[parts + 4 :]
    terms, totals = refs[:adds], refs[adds : 2 * adds]
    earlier, refs = refs[2 * adds : 2 * adds + given], refs[2 * adds + given + chained :]
    outs, added = refs[:parts], refs[parts : parts + adds]
    x_ref, coef_ref, hidden_ref = refs[parts + adds :]
    for term, total, result in zip(terms, totals, added):
        result[...] = (term[...] + total[...].astype(jnp.float32)).astype(jnp.bfloat16)

    def experts():
        width = x_ref.shape[1]
        hidden = weights[0][1].shape[0]
        line = lax.broadcasted_iota(jnp.int32, (HALF, LANES), 0)
        token = line == lax.broadcasted_iota(jnp.int32, (HALF, LANES), 1) % HALF
        bounds = []
        for part, payload in enumerate(payloads):
            here = slice(part * HALF, (part + 1) * HALF)
            bounds.append(here)
            for i in range(width // LANES):
                x_ref[here, i * LANES : (i + 1) * LANES] = payload[i * HALF : (i + 1) * HALF, :]
            block = payload[HALF * (width // LANES) :, :].astype(jnp.float32)
            expert = lax.broadcasted_iota(jnp.int32, block.shape, 0)
            for which in range(2):
                terms = jnp.sum(jnp.where(expert == expert_ref[0] ^ which, block, 0.0), axis=0, keepdims=True)
                value = jnp.sum(jnp.where(token, terms, 0.0), axis=1, keepdims=True)
                coef_ref[which, here, :] = jnp.broadcast_to(value, (HALF, LANES))
        tile = 256
        for which, (gate_up, _) in enumerate(weights):
            for t in range(0, hidden, tile):
                gate = jnp.dot(x_ref[...], gate_up[:, t : t + tile], preferred_element_type=jnp.float32)
                up = jnp.dot(x_ref[...], gate_up[:, hidden + t : hidden + t + tile], preferred_element_type=jnp.float32)
                value = jax.nn.silu(gate) * up * coef_ref[which][:, :1]
                hidden_ref[:, which * hidden + t : which * hidden + t + tile] = value.astype(jnp.bfloat16)
        tile = 512
        for t in range(0, width, tile):
            total = jnp.zeros((x_ref.shape[0], tile), jnp.float32)
            for which, (_, down) in enumerate(weights):
                rows = hidden_ref[:, which * hidden : (which + 1) * hidden]
                total += jnp.dot(rows, down[:, t : t + tile], preferred_element_type=jnp.float32)
            for here, out in zip(bounds, outs):
                out[:, t : t + tile] = total[here, :]

    if core is None:
        experts()
    else:
        here = expert_ref[0] % CORES == core
        pl.when(here)(experts)

        @pl.when(jnp.logical_not(here))
        def _():
            for source, out in zip(earlier, outs):
                out[...] = source[...]


def expert_rows(expert_id, payloads, own, other, after, terms=(), totals=(), core=None, earlier=()):
    width = own[0].shape[0]
    hidden = own[1].shape[0]
    rows = HALF * len(payloads)
    vmem = pl.BlockSpec(memory_space=pltpu.VMEM)
    chain = [] if after is None else [after]
    return pl.pallas_call(
        functools.partial(
            mlp_kernel, parts=len(payloads), adds=len(terms), chained=len(chain), core=core, given=len(earlier)
        ),
        out_shape=[jax.ShapeDtypeStruct((HALF, width), jnp.float32)] * len(payloads)
        + [jax.ShapeDtypeStruct((HALF, width), jnp.bfloat16)] * len(terms),
        in_specs=[pl.BlockSpec(memory_space=pltpu.SMEM)]
        + [vmem] * (len(payloads) + 4 + 2 * len(terms) + len(earlier))
        + [pl.BlockSpec(memory_space=pl.ANY)] * len(chain),
        out_specs=[vmem] * (len(payloads) + len(terms)),
        scratch_shapes=[
            pltpu.VMEM((rows, width), jnp.bfloat16),
            pltpu.VMEM((2, rows, LANES), jnp.float32),
            pltpu.VMEM((rows, 2 * hidden), jnp.bfloat16),
        ],
        compiler_params=pltpu.CompilerParams(vmem_limit_bytes=16 * MIB),
        cost_estimate=pl.CostEstimate(
            flops=2 * rows * width * hidden * 6,
            bytes_accessed=rows * width * 6,
            transcendentals=rows * hidden * 2,
        ),
        name="expert_rows",
    )(expert_id, *payloads, *own, *other, *terms, *totals, *earlier, *chain)


def last_kernel(near0_ref, near1_ref, total0_ref, total1_ref, out_ref):
    half = near0_ref.shape[0]
    for start, near_ref, total_ref in ((0, near0_ref, total0_ref), (half, near1_ref, total1_ref)):
        total = near_ref[...] + total_ref[...].astype(jnp.float32)
        out_ref[start : start + half, :] = total.astype(jnp.bfloat16)


def last_rows(nears, totals):
    rows, width = nears[0].shape
    vmem = pl.BlockSpec(memory_space=pltpu.VMEM)
    return pl.pallas_call(
        last_kernel,
        out_shape=jax.ShapeDtypeStruct((2 * rows, width), jnp.bfloat16),
        in_specs=[vmem] * 4,
        out_specs=vmem,
        compiler_params=pltpu.CompilerParams(vmem_limit_bytes=8 * MIB),
        cost_estimate=pl.CostEstimate(flops=2 * rows * width, bytes_accessed=rows * width * 16, transcendentals=0),
        name="last_rows",
    )(*nears, *totals)


def chip_ring(depth, across):
    walk = []
    for z in range(depth):
        xs = list(range(1, across))
        walk += [(z, x) for x in (xs if z % 2 == 0 else xs[::-1])]
    return [z * across + x for z, x in walk + [(z, 0) for z in reversed(range(depth))]]


def relay_body(fresh, previous, norm_gain, routes, gate_weights, w_gate_up, w_down, *, across):
    devices_exp = lax.axis_size("expert")
    section_id = lax.axis_index("section").astype(jnp.int32).reshape(1)
    expert_id = lax.axis_index("expert").astype(jnp.int32).reshape(1)
    rows = fresh.shape[0]
    half = HALF
    chips = devices_exp // CORES
    ring = chip_ring(chips // across, across)
    links = list(zip(ring, ring[1:] + ring[:1]))
    up = [(a * CORES + c, b * CORES + c) for a, b in links for c in range(CORES)]
    down = [(b, a) for a, b in up]
    swap = [(i, i ^ 1) for i in range(devices_exp)]

    def move(value, pairs):
        return lax.ppermute(value, "expert", pairs)

    cuts = [slice(0, half), slice(half, rows)]
    own = (w_gate_up[0, 0], w_down[0, 0])
    swapped = lax.optimization_barrier((*own, section_id, expert_id))[:2]
    other = tuple(move(w, swap) for w in swapped)
    base, coefs, fresh, gain = base_rows(fresh, norm_gain, routes[0].T, gate_weights[0].T, devices_exp)
    arrived = [from_behind(previous[0, cut], "section", 1) for cut in cuts]
    packed, arrival = zip(*(norm_rows(section_id, base, coefs, fresh, arrived[c], gain, c) for c in range(2)))
    packed = list(packed)

    hops = chips // 2
    ups = [packed] + [[None, None] for _ in range(hops)]
    downs = [packed] + [[None, None] for _ in range(hops)]

    def pass_on(s, c, after):
        rising, falling = lax.optimization_barrier((ups[s][c], downs[s][c], after))[:2]
        if s < hops - 1 or c == 0:
            ups[s + 1][c] = move(rising, up)
        if s < hops - 1 or c == 1:
            downs[s + 1][c] = move(falling, down)

    last = None

    def mlp(payloads, *args):
        nonlocal last
        sums = expert_rows(expert_id, payloads, own, other, last, *args)
        last = sums[0]
        return sums

    to_down, to_up = {}, {}
    pass_on(0, 0, None)
    pass_on(0, 1, other)
    for s in range(1, hops):
        for c in range(2):
            if (s, c) != (hops - 1, 1):
                pass_on(s, c, last)
            came = [ups[s][c], downs[s][c]]
            if s == hops - 1 and c == 0:
                pass_on(s, 1, last)
                came = lax.optimization_barrier((*came, ups[s][1], downs[s][1]))[:2]
            to_down[s, c], to_up[s, c] = mlp(came)
    early_sums = mlp(packed, (), (), 1)
    to_up[hops, 0], to_down[hops, 1] = mlp([ups[hops][0], downs[hops][1]])

    def send_on(flow, place, total, after):
        terms, c, pairs = flow
        if total is None:
            total = lax.optimization_barrier((terms[place, c], after))[0]
        else:
            carried = lax.optimization_barrier((total, after))[0]
            total = terms[place, c] + carried.astype(jnp.float32)
        total = total.astype(jnp.bfloat16)
        return total, move(total, pairs)

    short = [(to_down, 0, down), (to_up, 1, up)]
    long = [(to_up, 0, up), (to_down, 1, down)]
    short_totals = [send_on(flow, hops - 1, None, to_up[hops - 1, 1])[1] for flow in short]
    long_totals = [send_on(flow, hops, None, None)[1] for flow in long]
    *own_sums, down_sum, up_sum = mlp(packed, [f[0][hops - 2, f[1]] for f in short], short_totals, 0, early_sums)
    short_totals = [move(total, flow[2]) for total, flow in zip((down_sum, up_sum), short)]
    after = None
    for s in reversed(range(1, hops)):
        sent, long_totals = zip(*(send_on(f, s, t, None) for f, t in zip(long, long_totals)))
        if 1 < s < hops - 1:
            short_totals = [send_on(f, s - 1, t, sent)[1] for f, t in zip(short, short_totals)]

    nears = [
        arrival[c].astype(jnp.float32) + (own_sums[c] + short_totals[c].astype(jnp.float32)) for c in range(2)
    ]
    nears = lax.optimization_barrier(nears)
    return last_rows(nears, long_totals)[None]


def solution(mesh):
    across = mesh.shape["section"]
    devices_exp = mesh.shape["expert"]

    def body(*args):
        topk_count, local_experts = args[3].shape[2], args[5].shape[1]
        regular = devices_exp % (2 * CORES * across) == 0 and devices_exp >= 6 * CORES and devices_exp % 16 == 0 and args[0].shape[0] == LANES
        if local_experts == 1 and devices_exp <= 2 * topk_count and regular:
            return relay_body(*args, across=across)
        return routed_body(*args)

    return jax.shard_map(
        body,
        mesh=mesh,
        in_specs=(
            P("expert", None),
            P("section", "expert", None),
            P("section", None),
            P("section", "expert", None),
            P("section", "expert", None),
            P("section", "expert", None, None),
            P("section", "expert", None, None),
        ),
        out_specs=P("section", "expert", None),
        check_vma=False,
    )
```

```python
import functools

import jax
import jax.numpy as jnp
from jax import lax
from jax.experimental import pallas as pl
from jax.experimental.pallas import tpu as pltpu
from jax.sharding import PartitionSpec as P

epsilon = 1e-06
LANES = 128
HALF = LANES // 2
CORES = 2
MIB = 1 << 20


def from_behind(value, axis, by):
    peers = lax.axis_size(axis)
    pairs = [(i, i + by) for i in range(peers) if 0 <= i + by < peers]
    return lax.ppermute(value, axis, pairs)


def routed_body(fresh, previous, norm_gain, routes, gate_weights, w_gate_up, w_down):
    devices_exp = lax.axis_size("expert")
    section_id = lax.axis_index("section")
    tok_dev = fresh.shape[0]
    width = fresh.shape[1]
    topk_count = routes.shape[2]
    local_experts = w_gate_up.shape[1]
    hidden_units = w_down.shape[2]
    experts_total = devices_exp * local_experts
    capacity = min(tok_dev, 17 * tok_dev * topk_count // (16 * experts_total))
    total_rows = tok_dev * topk_count
    arrived = from_behind(previous[0], "section", 1)
    arrival = jnp.where(section_id == 0, fresh, arrived)
    wide_input = arrival.astype(jnp.float32)
    scale = lax.rsqrt(jnp.mean(wide_input * wide_input, axis=-1, keepdims=True) + epsilon)
    normed = (wide_input * scale * norm_gain[0][None, :]).astype(jnp.bfloat16)
    flat_ids = routes[0].reshape(-1)
    one_hot = (flat_ids[:, None] == jnp.arange(experts_total, dtype=jnp.int32)[None, :]).astype(
        jnp.int32
    )
    slot_rank = jnp.sum(jnp.cumsum(one_hot, axis=0) * one_hot, axis=1) - 1
    position = flat_ids * capacity + slot_rank
    source_row = (
        jnp.full((experts_total * capacity,), total_rows, jnp.int32)
        .at[position]
        .set(jnp.arange(total_rows, dtype=jnp.int32))
    )
    padded = jnp.concatenate([normed, jnp.zeros((1, width), jnp.bfloat16)], axis=0)
    send_buffer = padded[source_row // topk_count].reshape(
        devices_exp, local_experts, capacity, width
    )
    received = lax.all_to_all(send_buffer, "expert", split_axis=0, concat_axis=0, tiled=True)
    projected = jnp.einsum(
        "secd,edf->secf", received, w_gate_up[0], preferred_element_type=jnp.float32
    )
    hidden = (jax.nn.silu(projected[..., :hidden_units]) * projected[..., hidden_units:]).astype(
        jnp.bfloat16
    )
    returned = lax.all_to_all(
        jnp.einsum("secf,efd->secd", hidden, w_down[0], preferred_element_type=jnp.float32).astype(
            jnp.bfloat16
        ),
        "expert",
        split_axis=0,
        concat_axis=0,
        tiled=True,
    )
    flat_back = returned.reshape(experts_total * capacity, width)
    picked = flat_back[position].reshape(tok_dev, topk_count, width).astype(jnp.float32)
    mixed = jnp.sum(picked * gate_weights[0][:, :, None], axis=1)
    return (wide_input + mixed).astype(jnp.bfloat16)[None]


def normed_rows(rows, gain):
    wide = rows.astype(jnp.float32)
    scale = lax.rsqrt(jnp.mean(wide * wide, axis=-1, keepdims=True) + epsilon)
    return (wide * scale * gain).astype(jnp.bfloat16)


def base_kernel(fresh_ref, gain_ref, routes_ref, gates_ref, rows_ref, coefs_ref, fresh_out_ref, gain_out_ref):
    rows_ref[...] = normed_rows(fresh_ref[...], gain_ref[...])
    shape = coefs_ref.shape[1:]
    expert = lax.broadcasted_iota(jnp.int32, shape, 0)
    weight = jnp.zeros(shape, jnp.float32)
    for k in range(routes_ref.shape[0]):
        weight += jnp.where(routes_ref[k : k + 1, :] == expert, gates_ref[k : k + 1, :], 0.0)
    high = weight.astype(jnp.bfloat16).astype(jnp.float32)
    low = weight - high
    left = lax.broadcasted_iota(jnp.int32, shape, 1) < HALF
    coefs_ref[0] = jnp.where(left, high, pltpu.roll(low, HALF, 1)).astype(jnp.bfloat16)
    coefs_ref[1] = jnp.where(left, pltpu.roll(high, HALF, 1), low).astype(jnp.bfloat16)
    fresh_out_ref[...] = fresh_ref[...]
    gain_out_ref[...] = gain_ref[...]


def base_rows(fresh, gain, routes, gates, experts):
    rows, width = fresh.shape
    vmem = pl.BlockSpec(memory_space=pltpu.VMEM)
    return pl.pallas_call(
        base_kernel,
        out_shape=(
            jax.ShapeDtypeStruct((rows, width), jnp.bfloat16),
            jax.ShapeDtypeStruct((2, experts, rows), jnp.bfloat16),
            jax.ShapeDtypeStruct(fresh.shape, fresh.dtype),
            jax.ShapeDtypeStruct(gain.shape, jnp.float32),
        ),
        in_specs=[vmem] * 4,
        out_specs=(vmem,) * 4,
        compiler_params=pltpu.CompilerParams(vmem_limit_bytes=12 * MIB),
        cost_estimate=pl.CostEstimate(flops=rows * width * 6, bytes_accessed=rows * width * 8, transcendentals=rows),
        name="base_rows",
    )(fresh, gain, routes, gates)


def norm_kernel(section_ref, base_ref, coefs_ref, fresh_ref, arrived_ref, gain_ref, rows_ref, arrival_ref, *, chunk):
    rows, width = arrived_ref.shape
    here = slice(chunk * rows, (chunk + 1) * rows)

    def pack(normed):
        for i in range(width // LANES):
            rows_ref[i * rows : (i + 1) * rows, :] = normed[:, i * LANES : (i + 1) * LANES]

    @pl.when(section_ref[0] == 0)
    def _():
        pack(base_ref[here, :])
        arrival_ref[...] = fresh_ref[here, :]

    @pl.when(section_ref[0] != 0)
    def _():
        pack(normed_rows(arrived_ref[...], gain_ref[...]))
        arrival_ref[...] = arrived_ref[...]

    rows_ref[rows * (width // LANES) :, :] = coefs_ref[chunk]


def norm_rows(section_id, base, coefs, fresh, arrived, gain, chunk):
    rows, width = arrived.shape
    vmem = pl.BlockSpec(memory_space=pltpu.VMEM)
    return pl.pallas_call(
        functools.partial(norm_kernel, chunk=chunk),
        out_shape=(
            jax.ShapeDtypeStruct((rows * (width // LANES) + coefs.shape[1], LANES), jnp.bfloat16),
            jax.ShapeDtypeStruct((rows, width), jnp.bfloat16),
        ),
        in_specs=[pl.BlockSpec(memory_space=pltpu.SMEM)] + [vmem] * 5,
        out_specs=(vmem, vmem),
        compiler_params=pltpu.CompilerParams(vmem_limit_bytes=12 * MIB),
        cost_estimate=pl.CostEstimate(flops=rows * width * 6, bytes_accessed=rows * width * 8, transcendentals=rows),
        name="norm_rows",
    )(section_id, base, coefs, fresh, arrived, gain)


def mlp_kernel(expert_ref, *refs, parts, adds, chained, core, given):
    payloads = refs[:parts]
    weights = (refs[parts : parts + 2], refs[parts + 2 : parts + 4])
    refs = refs[parts + 4 :]
    terms, totals = refs[:adds], refs[adds : 2 * adds]
    earlier, refs = refs[2 * adds : 2 * adds + given], refs[2 * adds + given + chained :]
    outs, added = refs[:parts], refs[parts : parts + adds]
    x_ref, coef_ref, hidden_ref = refs[parts + adds :]
    for term, total, result in zip(terms, totals, added):
        result[...] = (term[...] + total[...].astype(jnp.float32)).astype(jnp.bfloat16)

    def experts():
        width = x_ref.shape[1]
        hidden = weights[0][1].shape[0]
        line = lax.broadcasted_iota(jnp.int32, (HALF, LANES), 0)
        token = line == lax.broadcasted_iota(jnp.int32, (HALF, LANES), 1) % HALF
        bounds = []
        for part, payload in enumerate(payloads):
            here = slice(part * HALF, (part + 1) * HALF)
            bounds.append(here)
            for i in range(width // LANES):
                x_ref[here, i * LANES : (i + 1) * LANES] = payload[i * HALF : (i + 1) * HALF, :]
            block = payload[HALF * (width // LANES) :, :].astype(jnp.float32)
            expert = lax.broadcasted_iota(jnp.int32, block.shape, 0)
            for which in range(2):
                terms = jnp.sum(jnp.where(expert == expert_ref[0] ^ which, block, 0.0), axis=0, keepdims=True)
                value = jnp.sum(jnp.where(token, terms, 0.0), axis=1, keepdims=True)
                coef_ref[which, here, :] = jnp.broadcast_to(value, (HALF, LANES))
        tile = 256
        for which, (gate_up, _) in enumerate(weights):
            for t in range(0, hidden, tile):
                gate = jnp.dot(x_ref[...], gate_up[:, t : t + tile], preferred_element_type=jnp.float32)
                up = jnp.dot(x_ref[...], gate_up[:, hidden + t : hidden + t + tile], preferred_element_type=jnp.float32)
                value = jax.nn.silu(gate) * up * coef_ref[which][:, :1]
                hidden_ref[:, which * hidden + t : which * hidden + t + tile] = value.astype(jnp.bfloat16)
        tile = 512
        for t in range(0, width, tile):
            total = jnp.zeros((x_ref.shape[0], tile), jnp.float32)
            for which, (_, down) in enumerate(weights):
                rows = hidden_ref[:, which * hidden : (which + 1) * hidden]
                total += jnp.dot(rows, down[:, t : t + tile], preferred_element_type=jnp.float32)
            for here, out in zip(bounds, outs):
                out[:, t : t + tile] = total[here, :]

    if core is None:
        experts()
    else:
        here = expert_ref[0] % CORES == core
        pl.when(here)(experts)

        @pl.when(jnp.logical_not(here))
        def _():
            for source, out in zip(earlier, outs):
                out[...] = source[...]


def expert_rows(expert_id, payloads, own, other, after, terms=(), totals=(), core=None, earlier=()):
    width = own[0].shape[0]
    hidden = own[1].shape[0]
    rows = HALF * len(payloads)
    vmem = pl.BlockSpec(memory_space=pltpu.VMEM)
    chain = [] if after is None else [after]
    return pl.pallas_call(
        functools.partial(
            mlp_kernel, parts=len(payloads), adds=len(terms), chained=len(chain), core=core, given=len(earlier)
        ),
        out_shape=[jax.ShapeDtypeStruct((HALF, width), jnp.float32)] * len(payloads)
        + [jax.ShapeDtypeStruct((HALF, width), jnp.bfloat16)] * len(terms),
        in_specs=[pl.BlockSpec(memory_space=pltpu.SMEM)]
        + [vmem] * (len(payloads) + 4 + 2 * len(terms) + len(earlier))
        + [pl.BlockSpec(memory_space=pl.ANY)] * len(chain),
        out_specs=[vmem] * (len(payloads) + len(terms)),
        scratch_shapes=[
            pltpu.VMEM((rows, width), jnp.bfloat16),
            pltpu.VMEM((2, rows, LANES), jnp.float32),
            pltpu.VMEM((rows, 2 * hidden), jnp.bfloat16),
        ],
        compiler_params=pltpu.CompilerParams(vmem_limit_bytes=16 * MIB),
        cost_estimate=pl.CostEstimate(
            flops=2 * rows * width * hidden * 6,
            bytes_accessed=rows * width * 6,
            transcendentals=rows * hidden * 2,
        ),
        name="expert_rows",
    )(expert_id, *payloads, *own, *other, *terms, *totals, *earlier, *chain)


def last_kernel(near0_ref, near1_ref, total0_ref, total1_ref, out_ref):
    half = near0_ref.shape[0]
    for start, near_ref, total_ref in ((0, near0_ref, total0_ref), (half, near1_ref, total1_ref)):
        total = near_ref[...] + total_ref[...].astype(jnp.float32)
        out_ref[start : start + half, :] = total.astype(jnp.bfloat16)


def last_rows(nears, totals):
    rows, width = nears[0].shape
    vmem = pl.BlockSpec(memory_space=pltpu.VMEM)
    return pl.pallas_call(
        last_kernel,
        out_shape=jax.ShapeDtypeStruct((2 * rows, width), jnp.bfloat16),
        in_specs=[vmem] * 4,
        out_specs=vmem,
        compiler_params=pltpu.CompilerParams(vmem_limit_bytes=8 * MIB),
        cost_estimate=pl.CostEstimate(flops=2 * rows * width, bytes_accessed=rows * width * 16, transcendentals=0),
        name="last_rows",
    )(*nears, *totals)


def chip_ring(depth, across):
    walk = []
    for z in range(depth):
        xs = list(range(1, across))
        walk += [(z, x) for x in (xs if z % 2 == 0 else xs[::-1])]
    return [z * across + x for z, x in walk + [(z, 0) for z in reversed(range(depth))]]


def relay_body(fresh, previous, norm_gain, routes, gate_weights, w_gate_up, w_down, *, across):
    devices_exp = lax.axis_size("expert")
    section_id = lax.axis_index("section").astype(jnp.int32).reshape(1)
    expert_id = lax.axis_index("expert").astype(jnp.int32).reshape(1)
    rows = fresh.shape[0]
    half = HALF
    chips = devices_exp // CORES
    ring = chip_ring(chips // across, across)
    links = list(zip(ring, ring[1:] + ring[:1]))
    up = [(a * CORES + c, b * CORES + c) for a, b in links for c in range(CORES)]
    down = [(b, a) for a, b in up]
    swap = [(i, i ^ 1) for i in range(devices_exp)]

    def move(value, pairs):
        return lax.ppermute(value, "expert", pairs)

    cuts = [slice(0, half), slice(half, rows)]
    own = (w_gate_up[0, 0], w_down[0, 0])
    swapped = lax.optimization_barrier((*own, section_id, expert_id))[:2]
    other = tuple(move(w, swap) for w in swapped)
    base, coefs, fresh, gain = base_rows(fresh, norm_gain, routes[0].T, gate_weights[0].T, devices_exp)
    arrived = [from_behind(previous[0, cut], "section", 1) for cut in cuts]
    packed, arrival = zip(*(norm_rows(section_id, base, coefs, fresh, arrived[c], gain, c) for c in range(2)))
    packed = list(packed)

    hops = chips // 2
    ups = [packed] + [[None, None] for _ in range(hops)]
    downs = [packed] + [[None, None] for _ in range(hops)]

    def pass_on(s, c, after):
        rising, falling = lax.optimization_barrier((ups[s][c], downs[s][c], after))[:2]
        if s < hops - 1 or c == 0:
            ups[s + 1][c] = move(rising, up)
        if s < hops - 1 or c == 1:
            downs[s + 1][c] = move(falling, down)

    last = None

    def mlp(payloads, *args):
        nonlocal last
        sums = expert_rows(expert_id, payloads, own, other, last, *args)
        last = sums[0]
        return sums

    to_down, to_up = {}, {}
    pass_on(0, 0, None)
    pass_on(0, 1, other)
    for s in range(1, hops):
        for c in range(2):
            pass_on(s, c, last)
            if (s, c) == (2, 0):
                early_sums = mlp(packed, (), (), 1)
            to_down[s, c], to_up[s, c] = mlp([ups[s][c], downs[s][c]])
    to_up[hops, 0], to_down[hops, 1] = mlp([ups[hops][0], downs[hops][1]])

    def send_on(flow, place, total, after):
        terms, c, pairs = flow
        if total is None:
            total = lax.optimization_barrier((terms[place, c], after))[0]
        else:
            carried = lax.optimization_barrier((total, after))[0]
            total = terms[place, c] + carried.astype(jnp.float32)
        total = total.astype(jnp.bfloat16)
        return total, move(total, pairs)

    short = [(to_down, 0, down), (to_up, 1, up)]
    long = [(to_up, 0, up), (to_down, 1, down)]
    short_totals = [send_on(flow, hops - 1, None, to_up[hops - 1, 1])[1] for flow in short]
    long_totals = [send_on(flow, hops, None, None)[1] for flow in long]
    *own_sums, down_sum, up_sum = mlp(packed, [f[0][hops - 2, f[1]] for f in short], short_totals, 0, early_sums)
    short_totals = [move(total, flow[2]) for total, flow in zip((down_sum, up_sum), short)]
    after = None
    for s in reversed(range(1, hops)):
        sent, long_totals = zip(*(send_on(f, s, t, None) for f, t in zip(long, long_totals)))
        if 1 < s < hops - 1:
            short_totals = [send_on(f, s - 1, t, sent)[1] for f, t in zip(short, short_totals)]

    nears = [
        arrival[c].astype(jnp.float32) + (own_sums[c] + short_totals[c].astype(jnp.float32)) for c in range(2)
    ]
    nears = lax.optimization_barrier(nears)
    return last_rows(nears, long_totals)[None]


def solution(mesh):
    across = mesh.shape["section"]
    devices_exp = mesh.shape["expert"]

    def body(*args):
        topk_count, local_experts = args[3].shape[2], args[5].shape[1]
        regular = devices_exp % (2 * CORES * across) == 0 and devices_exp >= 6 * CORES and devices_exp % 16 == 0 and args[0].shape[0] == LANES
        if local_experts == 1 and devices_exp <= 2 * topk_count and regular:
            return relay_body(*args, across=across)
        return routed_body(*args)

    return jax.shard_map(
        body,
        mesh=mesh,
        in_specs=(
            P("expert", None),
            P("section", "expert", None),
            P("section", None),
            P("section", "expert", None),
            P("section", "expert", None),
            P("section", "expert", None, None),
            P("section", "expert", None, None),
        ),
        out_specs=P("section", "expert", None),
        check_vma=False,
    )
```

```python
import functools

import jax
import jax.numpy as jnp
from jax import lax
from jax.experimental import pallas as pl
from jax.experimental.pallas import tpu as pltpu
from jax.sharding import PartitionSpec as P

epsilon = 1e-06
LANES = 128
HALF = LANES // 2
CORES = 2
MIB = 1 << 20


def from_behind(value, axis, by):
    peers = lax.axis_size(axis)
    pairs = [(i, i + by) for i in range(peers) if 0 <= i + by < peers]
    return lax.ppermute(value, axis, pairs)


def routed_body(fresh, previous, norm_gain, routes, gate_weights, w_gate_up, w_down):
    devices_exp = lax.axis_size("expert")
    section_id = lax.axis_index("section")
    tok_dev = fresh.shape[0]
    width = fresh.shape[1]
    topk_count = routes.shape[2]
    local_experts = w_gate_up.shape[1]
    hidden_units = w_down.shape[2]
    experts_total = devices_exp * local_experts
    capacity = min(tok_dev, 17 * tok_dev * topk_count // (16 * experts_total))
    total_rows = tok_dev * topk_count
    arrived = from_behind(previous[0], "section", 1)
    arrival = jnp.where(section_id == 0, fresh, arrived)
    wide_input = arrival.astype(jnp.float32)
    scale = lax.rsqrt(jnp.mean(wide_input * wide_input, axis=-1, keepdims=True) + epsilon)
    normed = (wide_input * scale * norm_gain[0][None, :]).astype(jnp.bfloat16)
    flat_ids = routes[0].reshape(-1)
    one_hot = (flat_ids[:, None] == jnp.arange(experts_total, dtype=jnp.int32)[None, :]).astype(
        jnp.int32
    )
    slot_rank = jnp.sum(jnp.cumsum(one_hot, axis=0) * one_hot, axis=1) - 1
    position = flat_ids * capacity + slot_rank
    source_row = (
        jnp.full((experts_total * capacity,), total_rows, jnp.int32)
        .at[position]
        .set(jnp.arange(total_rows, dtype=jnp.int32))
    )
    padded = jnp.concatenate([normed, jnp.zeros((1, width), jnp.bfloat16)], axis=0)
    send_buffer = padded[source_row // topk_count].reshape(
        devices_exp, local_experts, capacity, width
    )
    received = lax.all_to_all(send_buffer, "expert", split_axis=0, concat_axis=0, tiled=True)
    projected = jnp.einsum(
        "secd,edf->secf", received, w_gate_up[0], preferred_element_type=jnp.float32
    )
    hidden = (jax.nn.silu(projected[..., :hidden_units]) * projected[..., hidden_units:]).astype(
        jnp.bfloat16
    )
    returned = lax.all_to_all(
        jnp.einsum("secf,efd->secd", hidden, w_down[0], preferred_element_type=jnp.float32).astype(
            jnp.bfloat16
        ),
        "expert",
        split_axis=0,
        concat_axis=0,
        tiled=True,
    )
    flat_back = returned.reshape(experts_total * capacity, width)
    picked = flat_back[position].reshape(tok_dev, topk_count, width).astype(jnp.float32)
    mixed = jnp.sum(picked * gate_weights[0][:, :, None], axis=1)
    return (wide_input + mixed).astype(jnp.bfloat16)[None]


def normed_rows(rows, gain):
    wide = rows.astype(jnp.float32)
    scale = lax.rsqrt(jnp.mean(wide * wide, axis=-1, keepdims=True) + epsilon)
    return (wide * scale * gain).astype(jnp.bfloat16)


def base_kernel(fresh_ref, gain_ref, routes_ref, gates_ref, rows_ref, coefs_ref, fresh_out_ref, gain_out_ref):
    rows_ref[...] = normed_rows(fresh_ref[...], gain_ref[...])
    shape = coefs_ref.shape[1:]
    expert = lax.broadcasted_iota(jnp.int32, shape, 0)
    weight = jnp.zeros(shape, jnp.float32)
    for k in range(routes_ref.shape[0]):
        weight += jnp.where(routes_ref[k : k + 1, :] == expert, gates_ref[k : k + 1, :], 0.0)
    high = weight.astype(jnp.bfloat16).astype(jnp.float32)
    low = weight - high
    left = lax.broadcasted_iota(jnp.int32, shape, 1) < HALF
    coefs_ref[0] = jnp.where(left, high, pltpu.roll(low, HALF, 1)).astype(jnp.bfloat16)
    coefs_ref[1] = jnp.where(left, pltpu.roll(high, HALF, 1), low).astype(jnp.bfloat16)
    fresh_out_ref[...] = fresh_ref[...]
    gain_out_ref[...] = gain_ref[...]


def base_rows(fresh, gain, routes, gates, experts):
    rows, width = fresh.shape
    vmem = pl.BlockSpec(memory_space=pltpu.VMEM)
    return pl.pallas_call(
        base_kernel,
        out_shape=(
            jax.ShapeDtypeStruct((rows, width), jnp.bfloat16),
            jax.ShapeDtypeStruct((2, experts, rows), jnp.bfloat16),
            jax.ShapeDtypeStruct(fresh.shape, fresh.dtype),
            jax.ShapeDtypeStruct(gain.shape, jnp.float32),
        ),
        in_specs=[vmem] * 4,
        out_specs=(vmem,) * 4,
        compiler_params=pltpu.CompilerParams(vmem_limit_bytes=12 * MIB),
        cost_estimate=pl.CostEstimate(flops=rows * width * 6, bytes_accessed=rows * width * 8, transcendentals=rows),
        name="base_rows",
    )(fresh, gain, routes, gates)


def norm_kernel(section_ref, base_ref, coefs_ref, fresh_ref, arrived_ref, gain_ref, rows_ref, arrival_ref, *, chunk):
    rows, width = arrived_ref.shape
    here = slice(chunk * rows, (chunk + 1) * rows)

    def pack(normed):
        for i in range(width // LANES):
            rows_ref[i * rows : (i + 1) * rows, :] = normed[:, i * LANES : (i + 1) * LANES]

    @pl.when(section_ref[0] == 0)
    def _():
        pack(base_ref[here, :])
        arrival_ref[...] = fresh_ref[here, :]

    @pl.when(section_ref[0] != 0)
    def _():
        pack(normed_rows(arrived_ref[...], gain_ref[...]))
        arrival_ref[...] = arrived_ref[...]

    rows_ref[rows * (width // LANES) :, :] = coefs_ref[chunk]


def norm_rows(section_id, base, coefs, fresh, arrived, gain, chunk):
    rows, width = arrived.shape
    vmem = pl.BlockSpec(memory_space=pltpu.VMEM)
    return pl.pallas_call(
        functools.partial(norm_kernel, chunk=chunk),
        out_shape=(
            jax.ShapeDtypeStruct((rows * (width // LANES) + coefs.shape[1], LANES), jnp.bfloat16),
            jax.ShapeDtypeStruct((rows, width), jnp.bfloat16),
        ),
        in_specs=[pl.BlockSpec(memory_space=pltpu.SMEM)] + [vmem] * 5,
        out_specs=(vmem, vmem),
        compiler_params=pltpu.CompilerParams(vmem_limit_bytes=12 * MIB),
        cost_estimate=pl.CostEstimate(flops=rows * width * 6, bytes_accessed=rows * width * 8, transcendentals=rows),
        name="norm_rows",
    )(section_id, base, coefs, fresh, arrived, gain)


def mlp_kernel(expert_ref, *refs, parts, adds, chained, core, given):
    payloads = refs[:parts]
    weights = (refs[parts : parts + 2], refs[parts + 2 : parts + 4])
    refs = refs[parts + 4 :]
    terms, totals = refs[:adds], refs[adds : 2 * adds]
    earlier, refs = refs[2 * adds : 2 * adds + given], refs[2 * adds + given + chained :]
    outs, added = refs[:parts], refs[parts : parts + adds]
    x_ref, coef_ref, hidden_ref = refs[parts + adds :]
    for term, total, result in zip(terms, totals, added):
        result[...] = (term[...] + total[...].astype(jnp.float32)).astype(jnp.bfloat16)

    def experts():
        width = x_ref.shape[1]
        hidden = weights[0][1].shape[0]
        line = lax.broadcasted_iota(jnp.int32, (HALF, LANES), 0)
        token = line == lax.broadcasted_iota(jnp.int32, (HALF, LANES), 1) % HALF
        bounds = []
        for part, payload in enumerate(payloads):
            here = slice(part * HALF, (part + 1) * HALF)
            bounds.append(here)
            for i in range(width // LANES):
                x_ref[here, i * LANES : (i + 1) * LANES] = payload[i * HALF : (i + 1) * HALF, :]
            block = payload[HALF * (width // LANES) :, :].astype(jnp.float32)
            expert = lax.broadcasted_iota(jnp.int32, block.shape, 0)
            for which in range(2):
                terms = jnp.sum(jnp.where(expert == expert_ref[0] ^ which, block, 0.0), axis=0, keepdims=True)
                value = jnp.sum(jnp.where(token, terms, 0.0), axis=1, keepdims=True)
                coef_ref[which, here, :] = jnp.broadcast_to(value, (HALF, LANES))
        tile = 256
        for which, (gate_up, _) in enumerate(weights):
            for t in range(0, hidden, tile):
                gate = jnp.dot(x_ref[...], gate_up[:, t : t + tile], preferred_element_type=jnp.float32)
                up = jnp.dot(x_ref[...], gate_up[:, hidden + t : hidden + t + tile], preferred_element_type=jnp.float32)
                value = jax.nn.silu(gate) * up * coef_ref[which][:, :1]
                hidden_ref[:, which * hidden + t : which * hidden + t + tile] = value.astype(jnp.bfloat16)
        tile = 512
        for t in range(0, width, tile):
            total = jnp.zeros((x_ref.shape[0], tile), jnp.float32)
            for which, (_, down) in enumerate(weights):
                rows = hidden_ref[:, which * hidden : (which + 1) * hidden]
                total += jnp.dot(rows, down[:, t : t + tile], preferred_element_type=jnp.float32)
            for here, out in zip(bounds, outs):
                out[:, t : t + tile] = total[here, :]

    if core is None:
        experts()
    else:
        here = expert_ref[0] % CORES == core
        pl.when(here)(experts)

        @pl.when(jnp.logical_not(here))
        def _():
            for source, out in zip(earlier, outs):
                out[...] = source[...]


def expert_rows(expert_id, payloads, own, other, after, terms=(), totals=(), core=None, earlier=()):
    width = own[0].shape[0]
    hidden = own[1].shape[0]
    rows = HALF * len(payloads)
    vmem = pl.BlockSpec(memory_space=pltpu.VMEM)
    chain = [] if after is None else [after]
    return pl.pallas_call(
        functools.partial(
            mlp_kernel, parts=len(payloads), adds=len(terms), chained=len(chain), core=core, given=len(earlier)
        ),
        out_shape=[jax.ShapeDtypeStruct((HALF, width), jnp.float32)] * len(payloads)
        + [jax.ShapeDtypeStruct((HALF, width), jnp.bfloat16)] * len(terms),
        in_specs=[pl.BlockSpec(memory_space=pltpu.SMEM)]
        + [vmem] * (len(payloads) + 4 + 2 * len(terms) + len(earlier))
        + [pl.BlockSpec(memory_space=pl.ANY)] * len(chain),
        out_specs=[vmem] * (len(payloads) + len(terms)),
        scratch_shapes=[
            pltpu.VMEM((rows, width), jnp.bfloat16),
            pltpu.VMEM((2, rows, LANES), jnp.float32),
            pltpu.VMEM((rows, 2 * hidden), jnp.bfloat16),
        ],
        compiler_params=pltpu.CompilerParams(vmem_limit_bytes=16 * MIB),
        cost_estimate=pl.CostEstimate(
            flops=2 * rows * width * hidden * 6,
            bytes_accessed=rows * width * 6,
            transcendentals=rows * hidden * 2,
        ),
        name="expert_rows",
    )(expert_id, *payloads, *own, *other, *terms, *totals, *earlier, *chain)


def add_kernel(*refs):
    for term, total, out in ((refs[0], refs[2], refs[5]), (refs[1], refs[3], refs[6])):
        out[...] = (term[...] + total[...].astype(jnp.float32)).astype(jnp.bfloat16)


def add_rows(terms, totals, after):
    vmem = pl.BlockSpec(memory_space=pltpu.VMEM)
    return pl.pallas_call(
        add_kernel,
        out_shape=[jax.ShapeDtypeStruct(total.shape, jnp.bfloat16) for total in totals],
        in_specs=[vmem] * 4 + [pl.BlockSpec(memory_space=pl.ANY)],
        out_specs=[vmem] * 2,
        compiler_params=pltpu.CompilerParams(vmem_limit_bytes=8 * MIB),
        cost_estimate=pl.CostEstimate(flops=2 * terms[0].size, bytes_accessed=terms[0].size * 16, transcendentals=0),
        name="add_rows",
    )(*terms, *totals, after)


def last_kernel(near0_ref, near1_ref, total0_ref, total1_ref, out_ref):
    half = near0_ref.shape[0]
    for start, near_ref, total_ref in ((0, near0_ref, total0_ref), (half, near1_ref, total1_ref)):
        total = near_ref[...] + total_ref[...].astype(jnp.float32)
        out_ref[start : start + half, :] = total.astype(jnp.bfloat16)


def last_rows(nears, totals):
    rows, width = nears[0].shape
    vmem = pl.BlockSpec(memory_space=pltpu.VMEM)
    return pl.pallas_call(
        last_kernel,
        out_shape=jax.ShapeDtypeStruct((2 * rows, width), jnp.bfloat16),
        in_specs=[vmem] * 4,
        out_specs=vmem,
        compiler_params=pltpu.CompilerParams(vmem_limit_bytes=8 * MIB),
        cost_estimate=pl.CostEstimate(flops=2 * rows * width, bytes_accessed=rows * width * 16, transcendentals=0),
        name="last_rows",
    )(*nears, *totals)


def chip_ring(depth, across):
    walk = []
    for z in range(depth):
        xs = list(range(1, across))
        walk += [(z, x) for x in (xs if z % 2 == 0 else xs[::-1])]
    return [z * across + x for z, x in walk + [(z, 0) for z in reversed(range(depth))]]


def relay_body(fresh, previous, norm_gain, routes, gate_weights, w_gate_up, w_down, *, across):
    devices_exp = lax.axis_size("expert")
    section_id = lax.axis_index("section").astype(jnp.int32).reshape(1)
    expert_id = lax.axis_index("expert").astype(jnp.int32).reshape(1)
    rows = fresh.shape[0]
    half = HALF
    chips = devices_exp // CORES
    ring = chip_ring(chips // across, across)
    links = list(zip(ring, ring[1:] + ring[:1]))
    up = [(a * CORES + c, b * CORES + c) for a, b in links for c in range(CORES)]
    down = [(b, a) for a, b in up]
    swap = [(i, i ^ 1) for i in range(devices_exp)]

    def move(value, pairs):
        return lax.ppermute(value, "expert", pairs)

    cuts = [slice(0, half), slice(half, rows)]
    own = (w_gate_up[0, 0], w_down[0, 0])
    swapped = lax.optimization_barrier((*own, section_id, expert_id))[:2]
    other = tuple(move(w, swap) for w in swapped)
    base, coefs, fresh, gain = base_rows(fresh, norm_gain, routes[0].T, gate_weights[0].T, devices_exp)
    arrived = [from_behind(previous[0, cut], "section", 1) for cut in cuts]
    packed, arrival = zip(*(norm_rows(section_id, base, coefs, fresh, arrived[c], gain, c) for c in range(2)))
    packed = list(packed)

    hops = chips // 2
    ups = [packed] + [[None, None] for _ in range(hops)]
    downs = [packed] + [[None, None] for _ in range(hops)]

    def pass_on(s, c, after):
        rising, falling = lax.optimization_barrier((ups[s][c], downs[s][c], after))[:2]
        if s < hops - 1 or c == 0:
            ups[s + 1][c] = move(rising, up)
        if s < hops - 1 or c == 1:
            downs[s + 1][c] = move(falling, down)

    last = None

    def mlp(payloads, *args):
        nonlocal last
        sums = expert_rows(expert_id, payloads, own, other, last, *args)
        last = sums[0]
        return sums

    to_down, to_up = {}, {}
    pass_on(0, 0, None)
    pass_on(0, 1, other)
    for s in range(1, hops):
        for c in range(2):
            pass_on(s, c, last)
            to_down[s, c], to_up[s, c] = mlp([ups[s][c], downs[s][c]])
    early_sums = mlp(packed, (), (), 1)
    to_up[hops, 0], to_down[hops, 1] = mlp([ups[hops][0], downs[hops][1]])

    def send_on(flow, place, total, after):
        terms, c, pairs = flow
        if total is None:
            total = lax.optimization_barrier((terms[place, c], after))[0]
        else:
            carried = lax.optimization_barrier((total, after))[0]
            total = terms[place, c] + carried.astype(jnp.float32)
        total = total.astype(jnp.bfloat16)
        return total, move(total, pairs)

    short = [(to_down, 0, down), (to_up, 1, up)]
    long = [(to_up, 0, up), (to_down, 1, down)]
    short_totals = [send_on(flow, hops - 1, None, to_up[hops - 1, 1])[1] for flow in short]
    long_totals = [send_on(flow, hops, None, None)[1] for flow in long]
    down_sum, up_sum = add_rows([f[0][hops - 2, f[1]] for f in short], short_totals, last)
    last = down_sum
    own_sums = mlp(packed, (), (), 0, early_sums)
    short_totals = [move(total, flow[2]) for total, flow in zip((down_sum, up_sum), short)]
    after = None
    for s in reversed(range(1, hops)):
        sent, long_totals = zip(*(send_on(f, s, t, None) for f, t in zip(long, long_totals)))
        if 1 < s < hops - 1:
            short_totals = [send_on(f, s - 1, t, sent)[1] for f, t in zip(short, short_totals)]

    nears = [
        arrival[c].astype(jnp.float32) + (own_sums[c] + short_totals[c].astype(jnp.float32)) for c in range(2)
    ]
    nears = lax.optimization_barrier(nears)
    return last_rows(nears, long_totals)[None]


def solution(mesh):
    across = mesh.shape["section"]
    devices_exp = mesh.shape["expert"]

    def body(*args):
        topk_count, local_experts = args[3].shape[2], args[5].shape[1]
        regular = devices_exp % (2 * CORES * across) == 0 and devices_exp >= 6 * CORES and devices_exp % 16 == 0 and args[0].shape[0] == LANES
        if local_experts == 1 and devices_exp <= 2 * topk_count and regular:
            return relay_body(*args, across=across)
        return routed_body(*args)

    return jax.shard_map(
        body,
        mesh=mesh,
        in_specs=(
            P("expert", None),
            P("section", "expert", None),
            P("section", None),
            P("section", "expert", None),
            P("section", "expert", None),
            P("section", "expert", None, None),
            P("section", "expert", None, None),
        ),
        out_specs=P("section", "expert", None),
        check_vma=False,
    )
```
